32 devices in a mesh: section: 2 (over x), dp: 16 (over z, y, core).
Axes of the slice: x: 2, y: 2, z: 4, core: 2. Of those that a mesh axis runs over, the one named last changes fastest.
Arguments:
- inputs: bfloat16 [2, 2048, 768], P(None, 'dp'), may hold values from -6 to 6
- segments: int32 [2, 2048], P(None, 'dp'), may hold values from 0 to 47, never falling along the last dimension, each value on 1 to 64 neighbouring positions
- cotangent: bfloat16 [2, 2048, 768], P(None, 'dp'), may hold values from -6 to 6
- norm_gain: bfloat16 [2, 768], P('section', 'dp'), may hold values from 0.099609375 to 1.8984375
- w_main: bfloat16 [2, 768, 3328], P('section', 'dp'), may hold values from -0.21875 to 0.21875
- w_dt: bfloat16 [2, 768, 24], P('section', 'dp'), may hold values from -0.21875 to 0.21875
- conv_weight: bfloat16 [2, 4, 1792], P('section', None, 'dp'), may hold values from -3 to 3
- conv_bias: bfloat16 [2, 1792], P('section', 'dp'), may hold values from -3 to 3
- dt_bias: float32 [2, 24], P('section'), may hold values from -4 to -1
- a_log: float32 [2, 24], P('section'), may hold values from -3 to 0
- skip_d: float32 [2, 24], P('section'), may hold values from 0.5 to 2
- gate_gain: bfloat16 [2, 1536], P('section', 'dp'), may hold values from 0.099609375 to 1.8984375
- w_out: bfloat16 [2, 1536, 768], P('section', 'dp'), may hold values from -0.15625 to 0.15625
Outputs:
- hidden: bfloat16 [2, 2, 2048, 768], P('section', None, 'dp')
- grad_inputs: float32 [2, 2, 2048, 768], P('section', None, 'dp')
- grad_norm_gain: float32 [2, 768], P('section', 'dp')
- grad_w_main: float32 [2, 768, 3328], P('section', 'dp')
- grad_w_dt: float32 [2, 768, 24], P('section', 'dp')
- grad_conv_weight: float32 [2, 4, 1792], P('section', None, 'dp')
- grad_conv_bias: float32 [2, 1792], P('section', 'dp')
- grad_dt_bias: float32 [2, 24], P('section')
- grad_a_log: float32 [2, 24], P('section')
- grad_skip_d: float32 [2, 24], P('section')
- grad_gate_gain: float32 [2, 1536], P('section', 'dp')
- grad_w_out: float32 [2, 1536, 768], P('section', 'dp')
The draws below stay inside these ranges and needn't reach their ends.
Inputs may be any that keep to these rules, and one draw needn't show every extreme that they name: `segments`: segment numbers never fall along a micro-batch's tokens; each segment spans 1 to 64 tokens, and one spans exactly that many.
All inputs are finite; a program needn't handle non-finite values.
Results may differ from the reference program's by a relative error of at most 0.011.
Values may be sent and summed in bfloat16 or wider, within the bound.
No kernel may reach another device: no remote copies, remote signals or barrier semaphores. Data moves between devices by JAX's collectives and lax.ppermute only.
A program may use at most 128 MiB of HBM per device.

```python
import math
import jax
import jax.numpy as jnp
import numpy as np
from jax import lax

D = 768
HEADS = 24
NSTATE = 128
CONV = 4
MICRO = 2
TOK_DEV = 128
E = 1536
TOKENS = 2048
LAYERS = 2
N_DP = 16


def block_levels(rng, shape, shards, smallest, largest):
    loudness, own = 1.0, jax.random.fold_in(rng, 6)
    for axis_at, parts in shards:
        steps = jnp.exp(jax.random.uniform(jax.random.fold_in(own, axis_at), (parts,), jnp.float32, smallest / len(shards), largest / len(shards)))
        loudness = loudness * jnp.repeat(steps, shape[axis_at] // parts).reshape([-1 if axis == axis_at else 1 for axis in range(len(shape))])
    return loudness


def profile(number_of, total, most, skew):
    loads = [(1 << 20) // math.isqrt(standing ** skew) + 1 for standing in range(2, number_of + 1)]
    spare, counts = total - most - (number_of - 1), [1] * (number_of - 1)
    while spare > 0:
        movable = [i for i in range(number_of - 1) if counts[i] < most]
        mass, left = sum([loads[i] for i in movable]), spare
        for i in movable:
            addition = min(most - counts[i], max(1, left * loads[i] // mass), spare)
            counts[i] = counts[i] + addition
            spare = spare - addition
    return np.array([most] + counts)


def ragged(rng, amount, total, reach, skew):
    if amount == 2:
        one = jax.random.randint(rng, (), max(1, total - reach), min(reach, total - 1) + 1)
        return jnp.stack([one, total - one])
    sizes = jnp.asarray(profile(amount, total, reach, skew), jnp.int32)
    twos = (amount - 1) // 2
    giver, sink = sizes[1:1 + 2 * twos:2], sizes[2:2 + 2 * twos:2]
    room = jnp.minimum(giver - 1, reach - sink)
    shifted = jax.random.randint(jax.random.fold_in(rng, 1), (twos,), 0, 1 << 20) % (room + 1)
    sizes = sizes.at[1:1 + 2 * twos:2].set(giver - shifted).at[2:2 + 2 * twos:2].set(sink + shifted)
    return sizes[jax.random.permutation(jax.random.fold_in(rng, 2), amount)]


def normal_values(rng, dims, deviation, most, split=(), kind=jnp.bfloat16):
    level = block_levels(rng, dims, split, -0.22, 0.18) if split else 1.0
    array = jax.random.normal(rng, dims, jnp.float32) * deviation * level
    return jnp.minimum(jnp.maximum(array, -most), most).astype(kind)


def setup_inputs(seed: int = 0) -> dict:
    key_of = jax.random.split(jax.random.key(seed), 14)
    inputs = normal_values(key_of[0], (MICRO, TOKENS, D), 1.0, 6.0, ((1, 16),))
    segments = jax.vmap(lambda own: jnp.searchsorted(jnp.cumsum(ragged(own, 3 * TOKENS // TOK_DEV, TOKENS, TOK_DEV // 2, 1)), jnp.arange(TOKENS), side="right"))(jax.random.split(key_of[1], MICRO)).reshape((MICRO, TOKENS)).astype(jnp.int32)
    cotangent = normal_values(key_of[2], (MICRO, TOKENS, D), 1.0, 6.0, ((1, 16),))
    norm_gain = jnp.clip(1.0 + 0.18 * jax.random.normal(key_of[3], (LAYERS, D), jnp.float32), 0.099609375, 1.8984375).astype(jnp.bfloat16)
    w_main = normal_values(key_of[4], (LAYERS, D, 2 * E + 2 * NSTATE), D ** -0.5, 0.21875, ((0, 2), (1, 16)))
    w_dt = normal_values(key_of[5], (LAYERS, D, HEADS), D ** -0.5, 0.21875, ((0, 2), (1, 16)))
    conv_weight = normal_values(key_of[6], (LAYERS, CONV, E + 2 * NSTATE), CONV ** -0.5, 3.0, ((0, 2), (2, 16)))
    conv_bias = normal_values(key_of[7], (LAYERS, E + 2 * NSTATE), 0.5, 3.0, ((0, 2), (1, 16)))
    dt_bias = jnp.clip(-4.0 + 3.0 * jax.random.uniform(key_of[8], (LAYERS, HEADS), jnp.float32) ** block_levels(key_of[8], (LAYERS, HEADS), ((0, 2),), -0.2, 0.2), -4.0, -1.0)
    a_log = jnp.clip(-3.0 + 3.0 * jax.random.uniform(key_of[9], (LAYERS, HEADS), jnp.float32) ** block_levels(key_of[9], (LAYERS, HEADS), ((0, 2),), -0.2, 0.2), -3.0, 0.0)
    skip_d = jnp.clip(0.5 + 1.5 * jax.random.uniform(key_of[10], (LAYERS, HEADS), jnp.float32) ** block_levels(key_of[10], (LAYERS, HEADS), ((0, 2),), -0.2, 0.2), 0.5, 2.0)
    gate_gain = jnp.clip(1.0 + 0.18 * jax.random.normal(key_of[11], (LAYERS, E), jnp.float32), 0.099609375, 1.8984375).astype(jnp.bfloat16)
    w_out = normal_values(key_of[12], (LAYERS, E, D), E ** -0.5, 0.15625, ((0, 2), (1, 16)))
    return {"inputs": inputs, "segments": segments, "cotangent": cotangent, "norm_gain": norm_gain, "w_main": w_main, "w_dt": w_dt, "conv_weight": conv_weight, "conv_bias": conv_bias, "dt_bias": dt_bias, "a_log": a_log, "skip_d": skip_d, "gate_gain": gate_gain, "w_out": w_out}


@jax.custom_vjp
def low(v):
    return lax.optimization_barrier(v.astype(jnp.bfloat16)).astype(jnp.float32)

@jax.custom_vjp
def low_back(v):
    return v

def low_keep(v):
    return (low(v), None)

def low_pass(kept, grad):
    return (grad,)

def back_keep(v):
    return (v, None)

def back_low(kept, grad):
    return (low(grad),)
low.defvjp(low_keep, low_pass)
low_back.defvjp(back_keep, back_low)
norm_eps = 1e-05
highest_precision = lax.Precision.HIGHEST

def rms_scale(values, weight_gain):
    factor = lax.rsqrt(lax.optimization_barrier(jnp.mean(values * values, axis=-1, keepdims=True)) + norm_eps)
    return values * factor * weight_gain

def mixer(projected_input, timestep_logits, doc_ids, kernel, kernel_bias, dt_bias, a_log, skip_d, gate_gain):
    length = projected_input.shape[0]
    inner_width = gate_gain.shape[0]
    n_heads = dt_bias.shape[0]
    n_state = (projected_input.shape[1] - 2 * inner_width) // 2
    kernel_taps = kernel.shape[0]
    gate_part = projected_input[:, :inner_width]
    conv_in = projected_input[:, inner_width:]
    summed = kernel_bias[None, :] + kernel[kernel_taps - 1][None, :] * conv_in
    for offset in range(1, kernel_taps):
        earlier = jnp.pad(conv_in, ((offset, 0), (0, 0)))[:length]
        early_ids = jnp.pad(doc_ids, (offset, 0), constant_values=-1)[:length]
        summed = summed + kernel[kernel_taps - 1 - offset][None, :] * jnp.where((early_ids == doc_ids)[:, None], earlier, 0.0)
    activated = jax.nn.silu(summed)
    x_heads = activated[:, :inner_width].reshape(length, n_heads, inner_width // n_heads)
    b_state = activated[:, inner_width:inner_width + n_state]
    c_state = activated[:, inner_width + n_state:]
    dt_step = jax.nn.softplus(timestep_logits + dt_bias[None, :])
    log_decay = jnp.cumsum(-dt_step * jnp.exp(a_log)[None, :], axis=0)
    positions = jnp.arange(length)
    linked = (positions[:, None] >= positions[None, :]) & (doc_ids[:, None] == doc_ids[None, :])
    spread = log_decay.T[:, :, None] - log_decay.T[:, None, :]
    decay_mask = jnp.where(linked[None], jnp.exp(jnp.where(linked[None], spread, 0.0)), 0.0)
    intersection = jnp.dot(c_state, b_state.T, precision=highest_precision)
    weighted = x_heads * dt_step[:, :, None]
    y_heads = jnp.einsum('hts,shp->thp', intersection[None] * decay_mask, weighted, precision=highest_precision)
    y_heads = y_heads + skip_d[None, :, None] * x_heads
    gated_out = y_heads.reshape(length, inner_width) * jax.nn.silu(gate_part)
    return rms_scale(gated_out, gate_gain[None, :])

def layer_block(hidden_in, doc_ids, params):
    gain_in, primary_weight, timestep_weight, kernel, kernel_bias, dt_bias, a_log, skip_d, gate_gain, output_weight = params
    normalized_input = low(rms_scale(hidden_in, gain_in))
    projected_input = low_back(jnp.einsum('rca,af->rcf', normalized_input, primary_weight, precision=highest_precision))
    timestep_logits = low_back(jnp.einsum('ekp,pz->ekz', normalized_input, timestep_weight, precision=highest_precision))
    mixer_output = jax.vmap(mixer, in_axes=(0, 0, 0, None, None, None, None, None, None))(projected_input, timestep_logits, doc_ids, kernel, kernel_bias, dt_bias, a_log, skip_d, gate_gain)
    branch_path = low_back(jnp.einsum('qzb,bn->qzn', low(mixer_output), output_weight, precision=highest_precision))
    return hidden_in + branch_path

def run_layer(hidden_in, doc_ids, params):
    seq_count = hidden_in.shape[0]
    length = hidden_in.shape[1]
    group_size = math.gcd(seq_count, max(1, 4096 // length))
    blocks = hidden_in.reshape(seq_count // group_size, group_size, length, hidden_in.shape[2])
    block_ids = doc_ids.reshape(seq_count // group_size, group_size, length)
    checked = jax.checkpoint(layer_block)
    result = lax.map(lambda paired: checked(paired[0], paired[1], params), (blocks, block_ids))
    return result.reshape(hidden_in.shape)

def reference(inputs, segments, cotangent, norm_gain, w_main, w_dt, conv_weight, conv_bias, dt_bias, a_log, skip_d, gate_gain, w_out):
    seq_count = MICRO * N_DP
    doc_ids = segments.reshape(seq_count, TOK_DEV)
    weights = tuple((tensor.astype(jnp.float32) for tensor in (norm_gain, w_main, w_dt, conv_weight, conv_bias, dt_bias, a_log, skip_d, gate_gain, w_out)))
    first_in = inputs.astype(jnp.float32).reshape(seq_count, TOK_DEV, D)
    probes = jnp.zeros((LAYERS - 1, seq_count, TOK_DEV, D), jnp.float32)

    def forward(first_in, probes, weights):
        current = first_in
        layer_outs = []
        for layer_no in range(LAYERS):
            params = tuple((tensor[layer_no] for tensor in weights))
            current_out = run_layer(current, doc_ids, params)
            if layer_no + 1 < LAYERS:
                rounded = low(current_out)
                layer_outs.append(rounded)
                current = low_back(rounded) + probes[layer_no]
            else:
                layer_outs.append(current_out)
        return (current_out, tuple(layer_outs))
    final_out, pullback, layer_outs = jax.vjp(forward, first_in, probes, weights, has_aux=True)
    seed_grad = cotangent.astype(jnp.float32).reshape(seq_count, TOK_DEV, D)
    grad_first, grad_probes, grad_weights = pullback(seed_grad)
    hidden_out = jnp.stack(layer_outs).reshape(LAYERS, MICRO, TOKENS, D).astype(jnp.bfloat16)
    grad_inputs = jnp.concatenate([grad_first[None], grad_probes], axis=0).reshape(LAYERS, MICRO, TOKENS, D)
    return (hidden_out, grad_inputs, grad_weights[0], grad_weights[1], grad_weights[2], grad_weights[3], grad_weights[4], grad_weights[5], grad_weights[6], grad_weights[7], grad_weights[8], grad_weights[9])
```

```python
import functools

import jax
import jax.numpy as jnp
from jax import lax
from jax.experimental import pallas as pl
from jax.experimental.pallas import tpu as pltpu
from jax.sharding import PartitionSpec as P

norm_eps = 1e-05
F32 = jnp.float32
BF16 = jnp.bfloat16
LANES = 128
TAPS = 4
VMEM_BYTES = 56 * 1024 * 1024


def dot_nn(a, b):
    return lax.dot_general(a, b, (((1,), (0,)), ((), ())), preferred_element_type=F32)


def dot_nt(a, b):
    return lax.dot_general(a, b, (((1,), (1,)), ((), ())), preferred_element_type=F32)


def dot_tn(a, b):
    return lax.dot_general(a, b, (((0,), (0,)), ((), ())), preferred_element_type=F32)


def split(a):
    high = a.astype(BF16)
    return high, (a - high.astype(F32)).astype(BF16)


def exact(dot, a, b):
    ah, al = split(a)
    bh, bl = split(b)
    return dot(ah, bh) + (dot(ah, bl) + dot(al, bh))


def near(dot, a, b):
    return exact(dot, a, b)


def triangle(lower):
    rows = lax.broadcasted_iota(jnp.int32, (LANES, LANES), 0)
    cols = lax.broadcasted_iota(jnp.int32, (LANES, LANES), 1)
    return jnp.where(rows >= cols if lower else rows <= cols, 1.0, 0.0).astype(BF16)


def running(tri, a):
    high = a.astype(BF16)
    rest = a - high.astype(F32)
    mid = rest.astype(BF16)
    low = (rest - mid.astype(F32)).astype(BF16)
    return dot_nn(tri, high) + (dot_nn(tri, mid) + dot_nn(tri, low))


def sigmoid(a):
    return 1.0 / (1.0 + jnp.exp(-a))


def softplus(a):
    return jnp.maximum(a, 0.0) + jnp.log1p(jnp.exp(-jnp.abs(a)))


def cols(j, width=LANES):
    return slice(j * width, (j + 1) * width)


def token_masks(segc_ref, segr_ref):
    length = segc_ref.shape[0]
    wide = jnp.broadcast_to(segc_ref[...], (length, LANES))
    rows = lax.broadcasted_iota(jnp.int32, (length, LANES), 0)
    lane = lax.broadcasted_iota(jnp.int32, (length, LANES), 1)
    linked = jnp.where((rows >= lane) & (wide == segr_ref[...]), 1.0, 0.0)
    sees = [None]
    for k in range(1, TAPS):
        sees.append(jnp.where((rows >= k) & (pltpu.roll(wide, k, 0) == wide), 1.0, 0.0))
    return linked, sees


def conv_taps(v, sees):
    return [v] + [sees[k] * pltpu.roll(v, k, 0) for k in range(1, TAPS)]


def conv_sum(taps, cw_ref, cb_ref, at):
    total = cb_ref[:, at] + cw_ref[TAPS - 1 : TAPS, at] * taps[0]
    for k in range(1, TAPS):
        total = total + cw_ref[TAPS - 1 - k : TAPS - k, at] * taps[k]
    return total


def pair_of(values, j):
    lane = lax.broadcasted_iota(jnp.int32, (values.shape[0], LANES), 1)
    first = jnp.broadcast_to(values[:, 2 * j : 2 * j + 1], lane.shape)
    second = jnp.broadcast_to(values[:, 2 * j + 1 : 2 * j + 2], lane.shape)
    return jnp.where(lane < LANES // 2, first, second)


def halves(values):
    lane = lax.broadcasted_iota(jnp.int32, values.shape, 1)
    low = jnp.where(lane < LANES // 2, values, 0.0)
    return jnp.concatenate([low, values - low], axis=0)


def decay(cum, cum_t, linked, h):
    spread = cum[:, h : h + 1] - cum_t[h : h + 1, :]
    return linked * jnp.exp(jnp.minimum(spread, 0.0))


def fwd_kernel(u_ref, segc_ref, segr_ref, wm_ref, wdt_ref, wo_ref, gin_ref, cw_ref, cb_ref, gg_ref, hp_ref, sk_ref,
               v_ref, n_ref, p_ref, dtr_ref, y_ref, mix_ref, g_scr):
    inner = gg_ref.shape[1]
    pairs = inner // LANES
    u = u_ref[...].astype(F32)
    r = lax.rsqrt(jnp.mean(u * u, axis=-1, keepdims=True) + norm_eps)
    n = (u * r * gin_ref[...]).astype(BF16)
    n_ref[...] = n
    width = wm_ref.shape[1]
    for c in range(width // 256):
        p_ref[:, cols(c, 256)] = dot_nn(n, wm_ref[:, cols(c, 256)])
    dtr = dot_nn(n, wdt_ref[...])
    dtr_ref[...] = dtr
    linked, sees = token_masks(segc_ref, segr_ref)

    def conv(j):
        total = conv_sum(conv_taps(p_ref[:, inner + j * LANES : inner + (j + 1) * LANES], sees), cw_ref, cb_ref, cols(j))
        return total * sigmoid(total)

    b_state = conv(pairs)
    c_state = conv(pairs + 1)
    cross = exact(dot_nt, c_state, b_state)
    dt = softplus(dtr + hp_ref[0:1, :])
    cum = running(triangle(True), -dt * jnp.exp(hp_ref[1:2, :]))
    cum_t = cum.T
    squares = jnp.zeros((u.shape[0], LANES), F32)
    for j in range(pairs):
        at = cols(j)
        x = conv(j)
        m = jnp.concatenate([cross * decay(cum, cum_t, linked, 2 * j), cross * decay(cum, cum_t, linked, 2 * j + 1)], axis=1)
        y = near(dot_nn, m, halves(x * pair_of(dt, j))) + sk_ref[:, at] * x
        y_ref[:, at] = y
        z = p_ref[:, at]
        g = y * (z * sigmoid(z))
        g_scr[:, at] = g
        squares = squares + g * g
    r2 = lax.rsqrt(jnp.sum(squares, axis=-1, keepdims=True) / inner + norm_eps)
    for j in range(pairs):
        at = cols(j)
        mix_ref[:, at] = (g_scr[:, at] * r2 * gg_ref[:, at]).astype(BF16)
    mixed = mix_ref[...]
    for c in range(u.shape[1] // 256):
        at = cols(c, 256)
        v_ref[:, at] = (u[:, at] + dot_nn(mixed, wo_ref[:, at])).astype(BF16)


def bwd_kernel(gv_ref, u_ref, segc_ref, segr_ref, wm_ref, wdt_ref, wo_ref, gin_ref, cw_ref, cb_ref, gg_ref, hp_ref, sk_ref,
               p_ref, dtr_ref, y_ref,
               gi_ref, gp_ref, gdt_ref, dgg_ref, dcw_ref, dcb_ref, dgin_ref, dsk_ref, dhp_ref,
               g_scr, gm_scr):
    inner = gg_ref.shape[1]
    pairs = inner // LANES
    length = u_ref.shape[0]
    gb = gv_ref[...]
    for c in range(inner // 256):
        gm_scr[:, cols(c, 256)] = dot_nt(gb, wo_ref[cols(c, 256), :])
    linked, sees = token_masks(segc_ref, segr_ref)

    def conv(j):
        taps = conv_taps(p_ref[:, inner + j * LANES : inner + (j + 1) * LANES], sees)
        total = conv_sum(taps, cw_ref, cb_ref, cols(j))
        sig = sigmoid(total)
        return taps, total, sig

    def conv_back(j, taps, total, sig, grad):
        at = cols(j)
        ds = grad * (sig * (1.0 + total * (1.0 - sig)))
        dcb_ref[:, at] = jnp.sum(ds, axis=0, keepdims=True)
        dcw_ref[TAPS - 1 : TAPS, at] = jnp.sum(ds * taps[0], axis=0, keepdims=True)
        dv = cw_ref[TAPS - 1 : TAPS, at] * ds
        for k in range(1, TAPS):
            row = slice(TAPS - 1 - k, TAPS - k)
            dcw_ref[row, at] = jnp.sum(ds * taps[k], axis=0, keepdims=True)
            dv = dv + cw_ref[row, at] * pltpu.roll(sees[k] * ds, length - k, 0)
        gp_ref[:, inner + j * LANES : inner + (j + 1) * LANES] = dv.astype(BF16)

    squares = jnp.zeros((length, LANES), F32)
    inners = jnp.zeros((length, LANES), F32)
    for j in range(pairs):
        at = cols(j)
        z = p_ref[:, at]
        g = y_ref[:, at] * (z * sigmoid(z))
        g_scr[:, at] = g
        squares = squares + g * g
        inners = inners + gm_scr[:, at] * gg_ref[:, at] * g
    r2 = lax.rsqrt(jnp.sum(squares, axis=-1, keepdims=True) / inner + norm_eps)
    pull = r2 * r2 * r2 * (jnp.sum(inners, axis=-1, keepdims=True) / inner)

    tb, sb, gb_sig = conv(pairs)
    b_state = sb * gb_sig
    tc, sc, gc_sig = conv(pairs + 1)
    c_state = sc * gc_sig
    cross = exact(dot_nt, c_state, b_state)
    dt_arg = dtr_ref[...] + hp_ref[0:1, :]
    dt = softplus(dt_arg)
    rate = jnp.exp(hp_ref[1:2, :])
    cum = running(triangle(True), -dt * rate)
    cum_t = cum.T
    dcross = jnp.zeros((length, length), F32)
    dcum = jnp.zeros((length, LANES), F32)
    ddt = jnp.zeros((length, LANES), F32)
    lane = lax.broadcasted_iota(jnp.int32, (2 * LANES, LANES), 1)
    row = lax.broadcasted_iota(jnp.int32, (2 * LANES, LANES), 0)
    half = jnp.where((row % LANES) < LANES // 2, 0, 1)
    for j in range(pairs):
        at = cols(j)
        pick = jnp.where(lane == 2 * j + half, 1.0, 0.0).astype(BF16)
        gm = gm_scr[:, at]
        g = g_scr[:, at]
        dgg_ref[:, at] = jnp.sum(gm * (g * r2), axis=0, keepdims=True)
        dg = gm * gg_ref[:, at] * r2 - g * pull
        z = p_ref[:, at]
        sig = sigmoid(z)
        y = y_ref[:, at]
        dy = dg * (z * sig)
        gp_ref[:, at] = (dg * y * (sig * (1.0 + z * (1.0 - sig)))).astype(BF16)
        taps, total, tsig = conv(j)
        x = total * tsig
        dtp = pair_of(dt, j)
        xw = x * dtp
        dy_st = halves(dy)
        l1 = decay(cum, cum_t, linked, 2 * j)
        l2 = decay(cum, cum_t, linked, 2 * j + 1)
        dm = near(dot_nt, dy_st, xw)
        dcross = dcross + dm[:length] * l1 + dm[length:] * l2
        m = jnp.concatenate([cross * l1, cross * l2], axis=0)
        dxw = near(dot_tn, m, dy_st)
        skip = sk_ref[:, at]
        dsk_ref[:, at] = jnp.sum(dy * x, axis=0, keepdims=True)
        q = dy * (y - skip * x) - dxw * xw
        dcum = dcum + dot_nn(jnp.concatenate(split(q), axis=1), pick)
        ddt = ddt + dot_nn(jnp.concatenate(split(dxw * x), axis=1), pick)
        conv_back(j, taps, total, tsig, skip * dy + dxw * dtp)
    conv_back(pairs, tb, sb, gb_sig, exact(dot_tn, dcross, c_state))
    conv_back(pairs + 1, tc, sc, gc_sig, exact(dot_nn, dcross, b_state))
    dlog = running(triangle(False), dcum)
    draw = (ddt - rate * dlog) * sigmoid(dt_arg)
    gdt = draw.astype(BF16)
    gdt_ref[...] = gdt
    dhp_ref[0:1, :] = jnp.sum(draw, axis=0, keepdims=True)
    dhp_ref[1:2, :] = jnp.sum(dlog * (-dt * rate), axis=0, keepdims=True)
    dhp_ref[2:8, :] = jnp.zeros((6, LANES), F32)
    u = u_ref[...].astype(F32)
    gin = gin_ref[...]
    r = lax.rsqrt(jnp.mean(u * u, axis=-1, keepdims=True) + norm_eps)
    gp = gp_ref[...]
    gn = jnp.concatenate(
        [dot_nt(gp, wm_ref[cols(c, 256), :]) + dot_nt(gdt, wdt_ref[cols(c, 256), :]) for c in range(u.shape[1] // 256)], axis=1
    )
    dgin_ref[...] = jnp.sum(gn * (u * r), axis=0, keepdims=True)
    gng = gn * gin
    back = r * r * r * jnp.mean(gng * u, axis=-1, keepdims=True)
    gi_ref[...] = gb.astype(F32) + (gng * r - u * back)


def shape_of(shape, dtype=F32):
    return jax.ShapeDtypeStruct(shape, dtype)


def forward_layer(u, segc, segr, weights):
    tok, feat = u.shape
    wm, wdt, wo = weights[:3]
    inner, width = wo.shape[0], wm.shape[1]
    return pl.pallas_call(
        fwd_kernel,
        out_shape=(
            shape_of((tok, feat), BF16),
            shape_of((tok, feat), BF16),
            shape_of((tok, width)),
            shape_of((tok, LANES)),
            shape_of((tok, inner)),
            shape_of((tok, inner), BF16),
        ),
        scratch_shapes=[pltpu.VMEM((tok, inner), F32)],
        compiler_params=pltpu.CompilerParams(vmem_limit_bytes=VMEM_BYTES),
        name="layer_forward",
    )(u, segc, segr, *weights)


def backward_layer(gv, u, segc, segr, weights, stored):
    tok, feat = u.shape
    wm, wdt, wo = weights[:3]
    inner, width = wo.shape[0], wm.shape[1]
    chans = width - inner
    return pl.pallas_call(
        bwd_kernel,
        out_shape=(
            shape_of((tok, feat)),
            shape_of((tok, width), BF16),
            shape_of((tok, LANES), BF16),
            shape_of((1, inner)),
            shape_of((TAPS, chans)),
            shape_of((1, chans)),
            shape_of((1, feat)),
            shape_of((1, inner)),
            shape_of((8, LANES)),
        ),
        scratch_shapes=[pltpu.VMEM((tok, inner), F32), pltpu.VMEM((tok, inner), F32)],
        compiler_params=pltpu.CompilerParams(vmem_limit_bytes=VMEM_BYTES),
        name="layer_backward",
    )(gv, u, segc, segr, *weights, *stored)


def weight_kernel(rows, n_ref, mix_ref, gp_ref, gb_ref, gdt_ref, small_ref, out_ref):
    feat, inner, width = n_ref.shape[1], mix_ref.shape[1], gp_ref.shape[1]
    n = n_ref[...]
    for c in range(width // 256):
        out_ref[:, cols(c, 256)] = dot_tn(n, gp_ref[:, cols(c, 256)]).astype(BF16)
    blocks = inner // feat
    for e in range(inner // 256):
        term = dot_tn(mix_ref[:, cols(e, 256)], gb_ref[...]).astype(BF16)
        at = e * 256
        while at < (e + 1) * 256:
            owner, inside = at // (blocks * rows), at % (blocks * rows)
            block, row = inside // rows, inside % rows
            count = min(rows - row, (e + 1) * 256 - at)
            out_ref[owner * rows + row : owner * rows + row + count, width + block * feat : width + (block + 1) * feat] = term[
                at - e * 256 : at - e * 256 + count
            ]
            at = at + count
    last = width + inner
    out_ref[:, last : last + LANES] = dot_tn(n, gdt_ref[...]).astype(BF16)
    out_ref[:, last + LANES :] = small_ref[...]


def weight_terms(n, mix, gp, gb, gdt, small, rows):
    feat, inner, width = n.shape[1], mix.shape[1], gp.shape[1]
    full = width + inner + LANES + small.shape[1]
    if rows % 16 == 0:
        return pl.pallas_call(
            functools.partial(weight_kernel, rows),
            out_shape=shape_of((feat, full), BF16),
            compiler_params=pltpu.CompilerParams(vmem_limit_bytes=VMEM_BYTES),
            name="weight_gradients",
        )(n, mix, gp, gb, gdt, small)
    blocks = inner // feat
    wide = dot_tn(mix, gb).reshape(feat // rows, blocks, rows, feat).transpose(0, 2, 1, 3).reshape(feat, inner)
    return jnp.concatenate([dot_tn(n, gp).astype(BF16), wide.astype(BF16), dot_tn(n, gdt).astype(BF16), small], axis=1)


def small_rows(vectors, rows):
    flat = jnp.concatenate([vector.reshape(-1) for vector in vectors])
    lines = -(-flat.shape[0] // LANES)
    wide = -(-lines // rows)
    flat = jnp.pad(flat, (0, lines * LANES - flat.shape[0])).reshape(lines, LANES)
    flat = jnp.pad(flat, ((0, rows * wide - lines), (0, 0)))
    return flat.reshape(wide, rows, LANES).transpose(1, 0, 2).reshape(rows, wide * LANES)


def small_flat(block, owners):
    rows, wide = block.shape[0] // owners, block.shape[1] // LANES
    return block.reshape(owners, rows, wide, LANES).transpose(0, 2, 1, 3).reshape(owners, wide * rows * LANES)


def total_over(value, axis):
    count = lax.axis_size(axis)
    step = 1
    while step < count:
        value = value + lax.ppermute(value, axis, [(i, i ^ step) for i in range(count)])
        step = step * 2
    return value


def shards(inputs, segments, cotangent, norm_gain, w_main, w_dt, conv_weight, conv_bias, dt_bias, a_log, skip_d, gate_gain, w_out):
    first = lax.axis_index("section") == 0
    dp = lax.axis_size("dp")
    feat = inputs.shape[2]
    rows, width = w_main.shape[1:]
    heads = w_dt.shape[2]
    chans, own_inner = conv_weight.shape[2], gate_gain.shape[1]
    inner = own_inner * dp
    blocks = own_inner // rows

    small = small_rows((conv_weight[0], conv_bias[0], gate_gain[0], norm_gain[0]), rows)
    out_block = w_out[0].reshape(blocks, rows, feat).transpose(1, 0, 2).reshape(rows, inner)
    packed = jnp.concatenate([w_main[0], out_block, jnp.pad(w_dt[0], ((0, 0), (0, LANES - heads))), small], axis=1)
    whole = lax.all_gather(packed, "dp", axis=0, tiled=True)
    wm = whole[:, :width]
    wo = whole[:, width : width + inner].reshape(dp, rows, blocks, feat).transpose(0, 2, 1, 3).reshape(inner, feat)
    wdt = whole[:, width + inner : width + inner + LANES]
    flat = small_flat(whole[:, width + inner + LANES :], dp).astype(F32)
    marks = [TAPS * chans, (TAPS + 1) * chans, (TAPS + 1) * chans + own_inner, (TAPS + 1) * chans + own_inner + rows]
    cw = flat[:, : marks[0]].reshape(dp, TAPS, chans).transpose(1, 0, 2).reshape(TAPS, dp * chans)
    cb = flat[:, marks[0] : marks[1]].reshape(1, dp * chans)
    gg = flat[:, marks[1] : marks[2]].reshape(1, inner)
    gin = flat[:, marks[2] : marks[3]].reshape(1, feat)
    hp = jnp.pad(jnp.concatenate([dt_bias, a_log], axis=0), ((0, 6), (0, LANES - heads)))
    sk = jnp.repeat(skip_d, inner // heads, axis=1)
    weights = (wm, wdt, wo, gin, cw, cb, gg, hp, sk)

    def choose(one, other):
        return jnp.where(first, one, other)

    def seg_of(ids):
        return ids[:, None], ids[None, :]

    up = [(0, 1)]
    down = [(1, 0)]
    ids = (segments[0], choose(segments[1], segments[0]), segments[1])
    u0 = inputs[0]
    f0 = forward_layer(u0, *seg_of(ids[0]), weights)
    u1 = choose(inputs[1], lax.ppermute(f0[0], "section", up))
    f1 = forward_layer(u1, *seg_of(ids[1]), weights)
    u2 = choose(inputs[1], lax.ppermute(f1[0], "section", up))
    f2 = forward_layer(u2, *seg_of(ids[2]), weights)
    hidden = jnp.stack([choose(f0[0], f1[0]), choose(f1[0], f2[0])])[None]

    late = tuple(choose(one, other) for one, other in zip((u0,) + tuple(f0[1:]), (u2,) + tuple(f2[1:])))
    g0 = cotangent[0]
    b0 = backward_layer(g0, u1, *seg_of(ids[1]), weights, f1[2:5])
    g1 = choose(lax.ppermute(b0[0].astype(BF16), "section", down), cotangent[1])
    b1 = backward_layer(g1, late[0], *seg_of(choose(segments[0], segments[1])), weights, late[2:5])
    g2 = lax.ppermute(b1[0].astype(BF16), "section", down)
    b2 = backward_layer(g2, u1, *seg_of(segments[1]), weights, f1[2:5])
    grad_inputs = jnp.stack([choose(b1[0], b0[0]), choose(b2[0], b1[0])])[None]

    keep0 = jnp.where(first, 0.0, 1.0).astype(BF16)
    keep2 = jnp.where(first, 1.0, 0.0).astype(BF16)
    norms = jnp.concatenate([f1[1] * keep0, late[1], f1[1] * keep2], axis=0)
    mixes = jnp.concatenate([f1[5] * keep0, late[5], f1[5] * keep2], axis=0)
    dgg, dcw, dcb, dgin, dsk, dhp = tuple(choose(two, zero) + one for zero, one, two in zip(b0[3:], b1[3:], b2[3:]))
    own = [
        small_rows(
            (
                dcw[:, i * chans : (i + 1) * chans],
                dcb[:, i * chans : (i + 1) * chans],
                dgg[:, i * own_inner : (i + 1) * own_inner],
                dgin[:, i * rows : (i + 1) * rows],
            ),
            rows,
        )
        for i in range(dp)
    ]
    packed_grad = weight_terms(
        norms,
        mixes,
        jnp.concatenate([b0[1], b1[1], b2[1]], axis=0),
        jnp.concatenate([g0, g1, g2], axis=0),
        jnp.concatenate([b0[2], b1[2], b2[2]], axis=0),
        jnp.concatenate(own, axis=0).astype(BF16),
        rows,
    )
    summed = lax.psum_scatter(packed_grad, "dp", scatter_dimension=0, tiled=True).astype(F32)
    dskip = dsk.reshape(heads, inner // heads).sum(axis=1)
    heads_sum = total_over(jnp.concatenate([dhp[:2, :heads], dskip[None]], axis=0), "dp")
    got = small_flat(summed[:, width + inner + LANES :], 1)[0]
    return (
        hidden,
        grad_inputs,
        got[None, marks[2] : marks[3]],
        summed[None, :, :width],
        summed[None, :, width + inner : width + inner + heads],
        got[: marks[0]].reshape(1, TAPS, chans),
        got[None, marks[0] : marks[1]],
        heads_sum[0:1],
        heads_sum[1:2],
        heads_sum[2:3],
        got[None, marks[1] : marks[2]],
        summed[:, width : width + inner].reshape(rows, blocks, feat).transpose(1, 0, 2).reshape(1, own_inner, feat),
    )


def solution(mesh):
    placed = (
        P(None, "dp", None),
        P(None, "dp"),
        P(None, "dp", None),
        P("section", "dp"),
        P("section", "dp", None),
        P("section", "dp", None),
        P("section", None, "dp"),
        P("section", "dp"),
        P("section", None),
        P("section", None),
        P("section", None),
        P("section", "dp"),
        P("section", "dp", None),
    )
    return jax.shard_map(
        shards,
        mesh=mesh,
        in_specs=placed,
        out_specs=(
            P("section", None, "dp", None),
            P("section", None, "dp", None),
            P("section", "dp"),
            P("section", "dp", None),
            P("section", "dp", None),
            P("section", None, "dp"),
            P("section", "dp"),
            P("section", None),
            P("section", None),
            P("section", None),
            P("section", "dp"),
            P("section", "dp", None),
        ),
        check_vma=False,
    )
```

```python
import functools

import jax
import jax.numpy as jnp
from jax import lax
from jax.experimental import pallas as pl
from jax.experimental.pallas import tpu as pltpu
from jax.sharding import PartitionSpec as P

norm_eps = 1e-05
F32 = jnp.float32
BF16 = jnp.bfloat16
LANES = 128
TAPS = 4
VMEM_BYTES = 56 * 1024 * 1024


def dot_nn(a, b):
    return lax.dot_general(a, b, (((1,), (0,)), ((), ())), preferred_element_type=F32)


def dot_nt(a, b):
    return lax.dot_general(a, b, (((1,), (1,)), ((), ())), preferred_element_type=F32)


def dot_tn(a, b):
    return lax.dot_general(a, b, (((0,), (0,)), ((), ())), preferred_element_type=F32)


def split(a):
    high = a.astype(BF16)
    return high, (a - high.astype(F32)).astype(BF16)


def exact(dot, a, b):
    ah, al = split(a)
    bh, bl = split(b)
    return dot(ah, bh) + (dot(ah, bl) + dot(al, bh))


def near(dot, a, b):
    return exact(dot, a, b)


def triangle(lower):
    rows = lax.broadcasted_iota(jnp.int32, (LANES, LANES), 0)
    cols = lax.broadcasted_iota(jnp.int32, (LANES, LANES), 1)
    return jnp.where(rows >= cols if lower else rows <= cols, 1.0, 0.0).astype(BF16)


def running(tri, a):
    high = a.astype(BF16)
    rest = a - high.astype(F32)
    mid = rest.astype(BF16)
    low = (rest - mid.astype(F32)).astype(BF16)
    return dot_nn(tri, high) + (dot_nn(tri, mid) + dot_nn(tri, low))


def sigmoid(a):
    return 1.0 / (1.0 + jnp.exp(-a))


def softplus(a):
    return jnp.maximum(a, 0.0) + jnp.log1p(jnp.exp(-jnp.abs(a)))


def cols(j, width=LANES):
    return slice(j * width, (j + 1) * width)


def token_masks(ids):
    length = ids.shape[1]
    across = jnp.broadcast_to(ids, (length, length))
    wide = across.T
    rows = lax.broadcasted_iota(jnp.int32, (length, length), 0)
    lane = lax.broadcasted_iota(jnp.int32, (length, length), 1)
    linked = jnp.where((rows >= lane) & (wide == across), 1.0, 0.0)
    sees = [None]
    for k in range(1, TAPS):
        sees.append(jnp.where((rows >= k) & (pltpu.roll(wide, k, 0) == wide), 1.0, 0.0))
    return linked, sees


def take(which_ref, choices, into, sems):
    def start(choice):
        for i, ((ref, index), target) in enumerate(zip(choice, into)):
            pltpu.make_async_copy(ref if index is None else ref.at[index], target, sems.at[i]).start()

    if len(choices) == 1:
        start(choices[0])
        return
    for number, choice in enumerate(choices):
        pl.when(which_ref[0] == number)(functools.partial(start, choice))


def taken(into, sems, *numbers):
    for i in numbers:
        pltpu.make_async_copy(into[i], into[i], sems.at[i]).wait()


def conv_taps(v, sees):
    return [v] + [sees[k] * pltpu.roll(v, k, 0) for k in range(1, TAPS)]


def conv_sum(taps, cw_ref, cb_ref, at):
    total = cb_ref[:, at] + cw_ref[TAPS - 1 : TAPS, at] * taps[0]
    for k in range(1, TAPS):
        total = total + cw_ref[TAPS - 1 - k : TAPS - k, at] * taps[k]
    return total


def pair_of(values, j):
    lane = lax.broadcasted_iota(jnp.int32, (values.shape[0], LANES), 1)
    first = jnp.broadcast_to(values[:, 2 * j : 2 * j + 1], lane.shape)
    second = jnp.broadcast_to(values[:, 2 * j + 1 : 2 * j + 2], lane.shape)
    return jnp.where(lane < LANES // 2, first, second)


def halves(values):
    lane = lax.broadcasted_iota(jnp.int32, values.shape, 1)
    low = jnp.where(lane < LANES // 2, values, 0.0)
    return jnp.concatenate([low, values - low], axis=0)


def decay(cum, cum_t, linked, h):
    spread = cum[:, h : h + 1] - cum_t[h : h + 1, :]
    return linked * jnp.exp(jnp.minimum(spread, 0.0))


def fwd_kernel(plan, which_ref, ids_ref, wm_ref, wdt_ref, wo_ref, gin_ref, cw_ref, cb_ref, gg_ref, hp_ref, sk_ref, *refs):
    sources, refs = refs[: len(plan)], refs[len(plan) :]
    v_ref, n_ref, p_ref, dtr_ref, y_ref, mix_ref, g_scr, u_scr, sems = refs
    take(which_ref, [((source, index),) for source, index in zip(sources, plan)], (u_scr,), sems)
    inner = gg_ref.shape[1]
    pairs = inner // LANES
    linked, sees = token_masks(ids_ref[which_ref[1]])
    taken((u_scr,), sems, 0)
    u = u_scr[...].astype(F32)
    r = lax.rsqrt(jnp.mean(u * u, axis=-1, keepdims=True) + norm_eps)
    n = (u * r * gin_ref[...]).astype(BF16)
    n_ref[...] = n
    for c in range(wm_ref.shape[1] // 256):
        p_ref[:, cols(c, 256)] = dot_nn(n, wm_ref[:, cols(c, 256)])
    dtr = dot_nn(n, wdt_ref[...])
    dtr_ref[...] = dtr

    def conv(j):
        total = conv_sum(conv_taps(p_ref[:, inner + j * LANES : inner + (j + 1) * LANES], sees), cw_ref, cb_ref, cols(j))
        return total * sigmoid(total)

    b_state = conv(pairs)
    c_state = conv(pairs + 1)
    cross = exact(dot_nt, c_state, b_state)
    dt = softplus(dtr + hp_ref[0:1, :])
    cum = running(triangle(True), -dt * jnp.exp(hp_ref[1:2, :]))
    cum_t = cum.T
    squares = jnp.zeros((u.shape[0], LANES), F32)
    for j in range(pairs):
        at = cols(j)
        x = conv(j)
        m = jnp.concatenate([cross * decay(cum, cum_t, linked, 2 * j), cross * decay(cum, cum_t, linked, 2 * j + 1)], axis=1)
        y = near(dot_nn, m, halves(x * pair_of(dt, j))) + sk_ref[:, at] * x
        y_ref[:, at] = y
        z = p_ref[:, at]
        g = y * (z * sigmoid(z))
        g_scr[:, at] = g
        squares = squares + g * g
    r2 = lax.rsqrt(jnp.sum(squares, axis=-1, keepdims=True) / inner + norm_eps)
    for j in range(pairs):
        at = cols(j)
        mix_ref[:, at] = (g_scr[:, at] * r2 * gg_ref[:, at]).astype(BF16)
    mixed = mix_ref[...]
    for c in range(u.shape[1] // 256):
        at = cols(c, 256)
        v_ref[:, at] = (u[:, at] + dot_nn(mixed, wo_ref[:, at])).astype(BF16)


def bwd_kernel(plan, which_ref, ids_ref, wm_ref, wdt_ref, wo_ref, gin_ref, cw_ref, cb_ref, gg_ref, hp_ref, sk_ref, *refs):
    count = 5 * len(plan)
    sources, refs = refs[:count], refs[count:]
    gi_ref, gl_ref, gp_ref, gdt_ref, dch_ref, din_ref, dgin_ref, dhp_ref = refs[:8]
    g_scr, gm_scr, gv_ref, u_ref, p_ref, dtr_ref, y_ref, sems = refs[8:]
    into = (gv_ref, u_ref, p_ref, dtr_ref, y_ref)
    choices = [list(zip(sources[5 * i : 5 * i + 5], indices)) for i, indices in enumerate(plan)]
    take(which_ref, choices, into, sems)
    dch_ref[...] = jnp.zeros(dch_ref.shape, F32)
    din_ref[...] = jnp.zeros(din_ref.shape, F32)
    inner = gg_ref.shape[1]
    pairs = inner // LANES
    length = gv_ref.shape[0]
    linked, sees = token_masks(ids_ref[which_ref[1]])
    taken(into, sems, 0)
    gb = gv_ref[...]
    for c in range(inner // 256):
        gm_scr[:, cols(c, 256)] = dot_nt(gb, wo_ref[cols(c, 256), :])
    taken(into, sems, 1, 2, 3, 4)

    def conv(j):
        taps = conv_taps(p_ref[:, inner + j * LANES : inner + (j + 1) * LANES], sees)
        total = conv_sum(taps, cw_ref, cb_ref, cols(j))
        sig = sigmoid(total)
        return taps, total, sig

    def conv_back(j, taps, total, sig, grad):
        at = cols(j)
        ds = grad * (sig * (1.0 + total * (1.0 - sig)))
        dch_ref[TAPS : TAPS + 1, at] = jnp.sum(ds, axis=0, keepdims=True)
        dch_ref[TAPS - 1 : TAPS, at] = jnp.sum(ds * taps[0], axis=0, keepdims=True)
        dv = cw_ref[TAPS - 1 : TAPS, at] * ds
        for k in range(1, TAPS):
            row = slice(TAPS - 1 - k, TAPS - k)
            dch_ref[row, at] = jnp.sum(ds * taps[k], axis=0, keepdims=True)
            dv = dv + cw_ref[row, at] * pltpu.roll(sees[k] * ds, length - k, 0)
        gp_ref[:, inner + j * LANES : inner + (j + 1) * LANES] = dv.astype(BF16)

    squares = jnp.zeros((length, LANES), F32)
    inners = jnp.zeros((length, LANES), F32)
    for j in range(pairs):
        at = cols(j)
        z = p_ref[:, at]
        g = y_ref[:, at] * (z * sigmoid(z))
        g_scr[:, at] = g
        squares = squares + g * g
        inners = inners + gm_scr[:, at] * gg_ref[:, at] * g
    r2 = lax.rsqrt(jnp.sum(squares, axis=-1, keepdims=True) / inner + norm_eps)
    pull = r2 * r2 * r2 * (jnp.sum(inners, axis=-1, keepdims=True) / inner)

    tb, sb, gb_sig = conv(pairs)
    b_state = sb * gb_sig
    tc, sc, gc_sig = conv(pairs + 1)
    c_state = sc * gc_sig
    cross = exact(dot_nt, c_state, b_state)
    dt_arg = dtr_ref[...] + hp_ref[0:1, :]
    dt = softplus(dt_arg)
    rate = jnp.exp(hp_ref[1:2, :])
    cum = running(triangle(True), -dt * rate)
    cum_t = cum.T
    dcross = jnp.zeros((length, length), F32)
    dcum = jnp.zeros((length, LANES), F32)
    ddt = jnp.zeros((length, LANES), F32)
    lane = lax.broadcasted_iota(jnp.int32, (2 * LANES, LANES), 1)
    row = lax.broadcasted_iota(jnp.int32, (2 * LANES, LANES), 0)
    half = jnp.where((row % LANES) < LANES // 2, 0, 1)
    for j in range(pairs):
        at = cols(j)
        pick = jnp.where(lane == 2 * j + half, 1.0, 0.0).astype(BF16)
        gm = gm_scr[:, at]
        g = g_scr[:, at]
        din_ref[0:1, at] = jnp.sum(gm * (g * r2), axis=0, keepdims=True)
        dg = gm * gg_ref[:, at] * r2 - g * pull
        z = p_ref[:, at]
        sig = sigmoid(z)
        y = y_ref[:, at]
        dy = dg * (z * sig)
        gp_ref[:, at] = (dg * y * (sig * (1.0 + z * (1.0 - sig)))).astype(BF16)
        taps, total, tsig = conv(j)
        x = total * tsig
        dtp = pair_of(dt, j)
        xw = x * dtp
        dy_st = halves(dy)
        l1 = decay(cum, cum_t, linked, 2 * j)
        l2 = decay(cum, cum_t, linked, 2 * j + 1)
        dm = near(dot_nt, dy_st, xw)
        dcross = dcross + dm[:length] * l1 + dm[length:] * l2
        m = jnp.concatenate([cross * l1, cross * l2], axis=0)
        dxw = near(dot_tn, m, dy_st)
        skip = sk_ref[:, at]
        din_ref[1:2, at] = jnp.sum(dy * x, axis=0, keepdims=True)
        q = dy * (y - skip * x) - dxw * xw
        dcum = dcum + dot_nn(jnp.concatenate(split(q), axis=1), pick)
        ddt = ddt + dot_nn(jnp.concatenate(split(dxw * x), axis=1), pick)
        conv_back(j, taps, total, tsig, skip * dy + dxw * dtp)
    conv_back(pairs, tb, sb, gb_sig, exact(dot_tn, dcross, c_state))
    conv_back(pairs + 1, tc, sc, gc_sig, exact(dot_nn, dcross, b_state))
    dlog = running(triangle(False), dcum)
    draw = (ddt - rate * dlog) * sigmoid(dt_arg)
    gdt = draw.astype(BF16)
    gdt_ref[...] = gdt
    dhp_ref[0:1, :] = jnp.sum(draw, axis=0, keepdims=True)
    dhp_ref[1:2, :] = jnp.sum(dlog * (-dt * rate), axis=0, keepdims=True)
    dhp_ref[2:8, :] = jnp.zeros((6, LANES), F32)
    u = u_ref[...].astype(F32)
    gin = gin_ref[...]
    r = lax.rsqrt(jnp.mean(u * u, axis=-1, keepdims=True) + norm_eps)
    gp = gp_ref[...]
    gn = jnp.concatenate(
        [dot_nt(gp, wm_ref[cols(c, 256), :]) + dot_nt(gdt, wdt_ref[cols(c, 256), :]) for c in range(u.shape[1] // 256)], axis=1
    )
    dgin_ref[...] = jnp.broadcast_to(jnp.sum(gn * (u * r), axis=0, keepdims=True), dgin_ref.shape)
    gng = gn * gin
    back = r * r * r * jnp.mean(gng * u, axis=-1, keepdims=True)
    grad = gb.astype(F32) + (gng * r - u * back)
    gi_ref[...] = grad
    gl_ref[...] = grad.astype(BF16)


def shape_of(shape, dtype=F32):
    return jax.ShapeDtypeStruct(shape, dtype)


VMEM_SPEC = pl.BlockSpec(memory_space=pltpu.VMEM)
HBM_SPEC = pl.BlockSpec(memory_space=pl.ANY)
SMEM_SPEC = pl.BlockSpec(memory_space=pltpu.SMEM)
PARAMS = pltpu.CompilerParams(vmem_limit_bytes=VMEM_BYTES)


def weight_specs(weights):
    feat, inner, chans = weights[0].shape[0], weights[2].shape[0], weights[4].shape[1]
    width = inner + chans
    specs = [pl.BlockSpec((feat, width), lambda i: (0, 0)), pl.BlockSpec((feat, LANES), lambda i: (0, (width + inner) // LANES))]
    return specs + [VMEM_SPEC] * (len(weights) - 2)


def forward_layer(which, ids, weights, choices):
    tok, feat = ids.shape[2], weights[0].shape[0]
    inner, chans = weights[2].shape[0], weights[4].shape[1]
    width = inner + chans
    return pl.pallas_call(
        functools.partial(fwd_kernel, tuple(index for _, index in choices)),
        grid=(1,),
        in_specs=[SMEM_SPEC, VMEM_SPEC] + weight_specs(weights) + [HBM_SPEC] * len(choices),
        out_specs=[VMEM_SPEC] * 6,
        out_shape=(
            shape_of((tok, feat), BF16),
            shape_of((tok, feat), BF16),
            shape_of((tok, width)),
            shape_of((tok, LANES)),
            shape_of((tok, inner)),
            shape_of((tok, inner), BF16),
        ),
        scratch_shapes=[pltpu.VMEM((tok, inner), F32), pltpu.VMEM((tok, feat), BF16), pltpu.SemaphoreType.DMA((1,))],
        compiler_params=PARAMS,
        name="layer_forward",
    )(which, ids, *weights, *[source for source, _ in choices])


def backward_layer(which, ids, weights, choices):
    tok, feat = ids.shape[2], weights[0].shape[0]
    inner, chans = weights[2].shape[0], weights[4].shape[1]
    width = inner + chans
    return pl.pallas_call(
        functools.partial(bwd_kernel, tuple(tuple(index for _, index in choice) for choice in choices)),
        grid=(1,),
        in_specs=[SMEM_SPEC, VMEM_SPEC] + weight_specs(weights) + [HBM_SPEC] * (5 * len(choices)),
        out_specs=[VMEM_SPEC] * 8,
        out_shape=(
            shape_of((tok, feat)),
            shape_of((tok, feat), BF16),
            shape_of((tok, width), BF16),
            shape_of((tok, LANES), BF16),
            shape_of((8, chans)),
            shape_of((8, inner)),
            shape_of((8, feat)),
            shape_of((8, LANES)),
        ),
        scratch_shapes=[
            pltpu.VMEM((tok, inner), F32),
            pltpu.VMEM((tok, inner), F32),
            pltpu.VMEM((tok, feat), BF16),
            pltpu.VMEM((tok, feat), BF16),
            pltpu.VMEM((tok, width), F32),
            pltpu.VMEM((tok, LANES), F32),
            pltpu.VMEM((tok, inner), F32),
            pltpu.SemaphoreType.DMA((5,)),
        ],
        compiler_params=PARAMS,
        name="layer_backward",
    )(which, ids, *weights, *[source for choice in choices for source, _ in choice])


def lay(blocks, size, chunks):
    lane = lax.broadcasted_iota(jnp.int32, (8, LANES), 1)
    out = [jnp.zeros((8, LANES), F32) for _ in range(chunks)]
    for i, block in enumerate(blocks):
        chunk, shift = (i * size) // LANES, (i * size) % LANES
        turned = pltpu.roll(block, shift, 1) if shift else block
        out[chunk] = jnp.where((lane >= shift) & (lane < shift + size), turned, out[chunk])
        if shift + size > LANES:
            out[chunk + 1] = jnp.where(lane < shift + size - LANES, turned, out[chunk + 1])
    return out


def cut(chunks, size, i):
    lane = lax.broadcasted_iota(jnp.int32, (8, LANES), 1)
    chunk, shift = (i * size) // LANES, (i * size) % LANES
    turn = (LANES - shift) % LANES
    block = pltpu.roll(chunks[chunk], turn, 1) if turn else chunks[chunk]
    if shift + size > LANES:
        block = jnp.where(lane < LANES - shift, block, pltpu.roll(chunks[chunk + 1], turn, 1))
    return jnp.where(lane < size, block, 0.0)


def pack_kernel(wm_ref, wo_ref, wdt_ref, cw_ref, cb_ref, gg_ref, ng_ref, out_ref, line):
    rows, width = wm_ref.shape
    feat = wo_ref.shape[1]
    blocks = wo_ref.shape[0] // rows
    out_ref[:, :width] = wm_ref[...]
    for b in range(blocks):
        out_ref[:, width + b * feat : width + (b + 1) * feat] = wo_ref[b * rows : (b + 1) * rows, :]
    last = width + blocks * feat
    out_ref[:, last:] = jnp.zeros((rows, 2 * LANES), BF16)
    out_ref[:, last : last + wdt_ref.shape[1]] = wdt_ref[...]
    line[...] = jnp.zeros(line.shape, F32)
    line[0:TAPS, : cw_ref.shape[1]] = cw_ref[...].astype(F32)
    for k, ref in enumerate((cb_ref, gg_ref, ng_ref)):
        line[TAPS + k : TAPS + k + 1, : ref.shape[1]] = ref[...].astype(F32)
    out_ref[0:16, last + LANES :] = line[...].astype(BF16)


def pack_shard(wm, wo, wdt, cw, cb, gg, ng):
    rows, width = wm.shape
    full = width + wo.shape[0] // rows * wo.shape[1] + 2 * LANES
    return pl.pallas_call(
        pack_kernel,
        out_shape=shape_of((rows, full), BF16),
        scratch_shapes=[pltpu.VMEM((16, LANES), F32)],
        compiler_params=PARAMS,
        name="pack_shard",
    )(wm, wo, wdt, cw, cb, gg, ng)


def settle_kernel(width, chans, owners, in_hbm, wo_ref, cw_ref, cb_ref, gg_ref, gin_ref, in_ref, sem):
    copy = pltpu.make_async_copy(in_hbm.at[:, width:], in_ref, sem)
    copy.start()
    copy.wait()
    feat = wo_ref.shape[1]
    rows = in_ref.shape[0] // owners
    blocks = wo_ref.shape[0] // in_ref.shape[0]
    lines = []
    for i in range(owners):
        for b in range(blocks):
            to = (i * blocks + b) * rows
            wo_ref[to : to + rows, :] = in_ref[i * rows : (i + 1) * rows, b * feat : (b + 1) * feat]
        lines.append(in_ref[i * rows : i * rows + 16, blocks * feat + LANES :].astype(F32)[0:8])
    for c, chunk in enumerate(lay(lines, chans, cw_ref.shape[1] // LANES)):
        cw_ref[:, cols(c)] = chunk[0:TAPS]
        cb_ref[:, cols(c)] = chunk[TAPS : TAPS + 1]
    for c, chunk in enumerate(lay(lines, blocks * rows, gg_ref.shape[1] // LANES)):
        gg_ref[:, cols(c)] = chunk[TAPS + 1 : TAPS + 2]
    for c, chunk in enumerate(lay(lines, rows, gin_ref.shape[1] // LANES)):
        gin_ref[:, cols(c)] = chunk[TAPS + 2 : TAPS + 3]


def settle(whole, width, chans, owners):
    feat, full = whole.shape
    rest = full - width
    inner = rest - 2 * LANES
    return pl.pallas_call(
        functools.partial(settle_kernel, width, chans, owners),
        in_specs=[HBM_SPEC],
        out_specs=[VMEM_SPEC] * 5,
        out_shape=(
            shape_of((inner, feat), BF16),
            shape_of((TAPS, owners * chans)),
            shape_of((1, owners * chans)),
            shape_of((1, inner)),
            shape_of((1, feat)),
        ),
        scratch_shapes=[pltpu.VMEM((feat, rest), BF16), pltpu.SemaphoreType.DMA],
        compiler_params=PARAMS,
        name="settle_weights",
    )(whole)


def weight_kernel(rows, chans, which_ref, *refs):
    sources, smalls, out_ref, scratch, sems = refs[:20], refs[20:29], refs[29], refs[30:35], refs[35]
    tok = sources[0].shape[0]
    into = [ref.at[part * tok : (part + 1) * tok] for part in range(2) for ref in scratch]
    take(which_ref, [[(source, None) for source in sources[10 * i : 10 * i + 10]] for i in range(2)], into, sems)
    n_ref, mix_ref, gp_ref, gb_ref, gdt_ref = scratch
    feat, inner, width = n_ref.shape[1], mix_ref.shape[1], gp_ref.shape[1]
    blocks = inner // feat
    last = width + inner
    early = jnp.where(which_ref[0] == 0, 0.0, 1.0)
    sums = [one[...] + early * zero[...] + (1.0 - early) * two[...] for zero, one, two in zip(smalls[0::3], smalls[1::3], smalls[2::3])]
    pieces = [[total[:, cols(c)] for c in range(total.shape[1] // LANES)] for total in sums]
    line = lax.broadcasted_iota(jnp.int32, (8, LANES), 0)
    for i in range(feat // rows):
        block = cut(pieces[0], chans, i)
        block = jnp.where(line == TAPS + 1, jnp.broadcast_to(cut(pieces[1], blocks * rows, i)[0:1], block.shape), block)
        block = jnp.where(line == TAPS + 2, jnp.broadcast_to(cut(pieces[2], rows, i)[0:1], block.shape), block)
        out_ref[i * rows : i * rows + 16, last + LANES :] = jnp.concatenate([block, jnp.zeros_like(block)], axis=0).astype(BF16)
        out_ref[i * rows + 16 : (i + 1) * rows, last + LANES :] = jnp.zeros((rows - 16, LANES), BF16)
    taken(into, sems, 0, 5, 2, 7, 4, 9)
    turned = n_ref[...].T
    for c in range(width // 256):
        out_ref[:, cols(c, 256)] = dot_nn(turned, gp_ref[:, cols(c, 256)]).astype(BF16)
    out_ref[:, last : last + LANES] = dot_nn(turned, gdt_ref[...]).astype(BF16)
    taken(into, sems, 1, 6, 3, 8)
    gb = gb_ref[...]
    for e in range(inner // 256):
        term = dot_tn(mix_ref[:, cols(e, 256)], gb).astype(BF16)
        at = e * 256
        while at < (e + 1) * 256:
            owner, inside = at // (blocks * rows), at % (blocks * rows)
            block, row = inside // rows, inside % rows
            count = min(rows - row, (e + 1) * 256 - at)
            out_ref[owner * rows + row : owner * rows + row + count, width + block * feat : width + (block + 1) * feat] = term[
                at - e * 256 : at - e * 256 + count
            ]
            at = at + count


def weight_terms(which, one, other, smalls, rows, chans):
    tok, feat = one[0].shape
    inner, width = one[1].shape[1], one[2].shape[1]
    return pl.pallas_call(
        functools.partial(weight_kernel, rows, chans),
        in_specs=[SMEM_SPEC] + [HBM_SPEC] * 20 + [VMEM_SPEC] * 9,
        out_specs=VMEM_SPEC,
        out_shape=shape_of((feat, width + inner + 2 * LANES), BF16),
        scratch_shapes=[pltpu.VMEM((2 * tok, part.shape[1]), BF16) for part in one[:5]] + [pltpu.SemaphoreType.DMA((10,))],
        compiler_params=PARAMS,
        name="weight_gradients",
    )(which, *one, *other, *smalls)


def unpack_kernel(in_ref, wm_ref, wo_ref, wdt_ref, cw_ref, cb_ref, gg_ref, ng_ref):
    rows, width = wm_ref.shape
    feat = wo_ref.shape[1]
    blocks = wo_ref.shape[0] // rows
    wm_ref[...] = in_ref[:, :width].astype(F32)
    for b in range(blocks):
        wo_ref[b * rows : (b + 1) * rows, :] = in_ref[:, width + b * feat : width + (b + 1) * feat].astype(F32)
    last = width + blocks * feat
    wdt_ref[...] = in_ref[:, last : last + LANES].astype(F32)[:, : wdt_ref.shape[1]]
    line = in_ref[0:16, last + LANES :].astype(F32)
    cw_ref[...] = line[0:TAPS, : cw_ref.shape[1]]
    for k, ref in enumerate((cb_ref, gg_ref, ng_ref)):
        ref[...] = line[TAPS + k : TAPS + k + 1, : ref.shape[1]]


def unpack_sums(summed, wm, wo, wdt, cw, cb, gg, ng):
    return pl.pallas_call(
        unpack_kernel,
        out_shape=tuple(shape_of(part.shape) for part in (wm, wo, wdt, cw, cb, gg, ng)),
        compiler_params=PARAMS,
        name="unpack_sums",
    )(summed)


def small_rows(vectors, rows):
    flat = jnp.concatenate([vector.reshape(-1) for vector in vectors])
    lines = -(-flat.shape[0] // LANES)
    wide = -(-lines // rows)
    flat = jnp.pad(flat, (0, lines * LANES - flat.shape[0])).reshape(lines, LANES)
    flat = jnp.pad(flat, ((0, rows * wide - lines), (0, 0)))
    return flat.reshape(wide, rows, LANES).transpose(1, 0, 2).reshape(rows, wide * LANES)


def small_flat(block, owners):
    rows, wide = block.shape[0] // owners, block.shape[1] // LANES
    return block.reshape(owners, rows, wide, LANES).transpose(0, 2, 1, 3).reshape(owners, wide * rows * LANES)


def total_over(value, axis):
    count = lax.axis_size(axis)
    step = 1
    while step < count:
        value = value + lax.ppermute(value, axis, [(i, i ^ step) for i in range(count)])
        step = step * 2
    return value


def shards(inputs, segments, cotangent, norm_gain, w_main, w_dt, conv_weight, conv_bias, dt_bias, a_log, skip_d, gate_gain, w_out):
    first = lax.axis_index("section") == 0
    dp = lax.axis_size("dp")
    feat = inputs.shape[2]
    rows, width = w_main.shape[1:]
    heads = w_dt.shape[2]
    chans, own_inner = conv_weight.shape[2], gate_gain.shape[1]
    inner = own_inner * dp
    blocks = own_inner // rows

    owned = (w_main[0], w_out[0], w_dt[0], conv_weight[0], conv_bias, gate_gain, norm_gain)
    aligned = rows % 16 == 0
    if aligned:
        packed = pack_shard(*owned)
    else:
        small = small_rows((conv_weight[0], conv_bias[0], gate_gain[0], norm_gain[0]), rows)
        out_block = w_out[0].reshape(blocks, rows, feat).transpose(1, 0, 2).reshape(rows, inner)
        packed = jnp.concatenate([w_main[0], out_block, jnp.pad(w_dt[0], ((0, 0), (0, LANES - heads))), small], axis=1)
    whole = lax.all_gather(packed, "dp", axis=0, tiled=True)
    marks = [TAPS * chans, (TAPS + 1) * chans, (TAPS + 1) * chans + own_inner, (TAPS + 1) * chans + own_inner + rows]
    if aligned:
        wo, cw, cb, gg, gin = settle(whole, width, chans, dp)
    else:
        wo = whole[:, width : width + inner].reshape(dp, rows, blocks, feat).transpose(0, 2, 1, 3).reshape(inner, feat)
        flat = small_flat(whole[:, width + inner + LANES :], dp).astype(F32)
        cw = flat[:, : marks[0]].reshape(dp, TAPS, chans).transpose(1, 0, 2).reshape(TAPS, dp * chans)
        cb = flat[:, marks[0] : marks[1]].reshape(1, dp * chans)
        gg = flat[:, marks[1] : marks[2]].reshape(1, inner)
        gin = flat[:, marks[2] : marks[3]].reshape(1, feat)
    hp = jnp.pad(jnp.concatenate([dt_bias, a_log], axis=0), ((0, 6), (0, LANES - heads)))
    sk = jnp.repeat(skip_d, inner // heads, axis=1)
    weights = (whole, whole, wo, gin, cw, cb, gg, hp, sk)

    def choose(one, other):
        return jnp.where(first, one, other)

    up = [(0, 1)]
    down = [(1, 0)]
    ids = segments.astype(F32)[:, None, :]
    side = choose(0, 1).astype(jnp.int32)

    def tick(micro):
        return jnp.stack([side, jnp.asarray(micro, jnp.int32)])

    f0 = forward_layer(tick(0), ids, weights, [(inputs, 0)])
    r0 = lax.ppermute(f0[0], "section", up)
    f1 = forward_layer(tick(1 - side), ids, weights, [(inputs, 1), (r0, None)])
    r1 = lax.ppermute(f1[0], "section", up)
    f2 = forward_layer(tick(1), ids, weights, [(inputs, 1), (r1, None)])

    kept = [(part, None) for part in f1[2:5]]
    now = [[(cotangent, 0), (inputs, 1)] + kept, [(cotangent, 0), (r0, None)] + kept]
    b0 = backward_layer(tick(0), ids, weights, now)
    d0 = lax.ppermute(b0[1], "section", down)
    now = [
        [(d0, None), (inputs, 0)] + [(part, None) for part in f0[2:5]],
        [(cotangent, 1), (r1, None)] + [(part, None) for part in f2[2:5]],
    ]
    b1 = backward_layer(tick(side), ids, weights, now)
    d1 = lax.ppermute(b1[1], "section", down)
    b2 = backward_layer(tick(1), ids, weights, [[(d1, None), (inputs, 1)] + kept])
    hidden = jnp.stack([choose(f0[0], f1[0]), choose(f1[0], f2[0])])[None]
    grad_inputs = jnp.stack([choose(b1[0], b0[0]), choose(b2[0], b1[0])])[None]
    dch, din, dgin, dhp = tuple(choose(two, zero) + one for zero, one, two in zip(b0[4:], b1[4:], b2[4:]))
    on_first = (f0[1], f0[5], b1[2], d0, b1[3]), (f1[1], f1[5], b2[2], d1, b2[3])
    on_last = (f2[1], f2[5], b1[2], cotangent[1], b1[3]), (f1[1], f1[5], b0[2], cotangent[0], b0[3])
    if aligned:
        smalls = [part[i] for i in (4, 5, 6) for part in (b0, b1, b2)]
        packed_grad = weight_terms(side[None], on_first[0] + on_first[1], on_last[0] + on_last[1], smalls, rows, chans)
    else:
        n, mix, gp, gb, gdt = tuple(
            jnp.concatenate([choose(on_first[0][i], on_last[0][i]), choose(on_first[1][i], on_last[1][i])], axis=0) for i in range(5)
        )
        own = [
            small_rows(
                (
                    dch[:TAPS, i * chans : (i + 1) * chans],
                    dch[TAPS, i * chans : (i + 1) * chans],
                    din[0, i * own_inner : (i + 1) * own_inner],
                    dgin[0, i * rows : (i + 1) * rows],
                ),
                rows,
            )
            for i in range(dp)
        ]
        wide = dot_tn(mix, gb).reshape(dp, blocks, rows, feat).transpose(0, 2, 1, 3).reshape(feat, inner)
        parts = [dot_tn(n, gp), wide, dot_tn(n, gdt), jnp.concatenate(own, axis=0)]
        packed_grad = jnp.concatenate([part.astype(BF16) for part in parts], axis=1)
    summed = lax.psum_scatter(packed_grad, "dp", scatter_dimension=0, tiled=True)
    dskip = din[1].reshape(heads, inner // heads).sum(axis=1)
    heads_sum = total_over(jnp.concatenate([dhp[:2, :heads], dskip[None]], axis=0), "dp")
    if aligned:
        g_main, g_out, g_dt, g_cw, g_cb, g_gg, g_ng = unpack_sums(summed, *owned)
    else:
        summed = summed.astype(F32)
        got = small_flat(summed[:, width + inner + LANES :], 1)[0]
        g_main = summed[:, :width]
        g_out = summed[:, width : width + inner].reshape(rows, blocks, feat).transpose(1, 0, 2).reshape(own_inner, feat)
        g_dt = summed[:, width + inner : width + inner + heads]
        g_cw = got[: marks[0]].reshape(TAPS, chans)
        g_cb, g_gg, g_ng = (got[None, marks[i] : marks[i + 1]] for i in range(3))
    return (
        hidden,
        grad_inputs,
        g_ng,
        g_main[None],
        g_dt[None],
        g_cw[None],
        g_cb,
        heads_sum[0:1],
        heads_sum[1:2],
        heads_sum[2:3],
        g_gg,
        g_out[None],
    )


def solution(mesh):
    placed = (
        P(None, "dp", None),
        P(None, "dp"),
        P(None, "dp", None),
        P("section", "dp"),
        P("section", "dp", None),
        P("section", "dp", None),
        P("section", None, "dp"),
        P("section", "dp"),
        P("section", None),
        P("section", None),
        P("section", None),
        P("section", "dp"),
        P("section", "dp", None),
    )
    return jax.shard_map(
        shards,
        mesh=mesh,
        in_specs=placed,
        out_specs=(
            P("section", None, "dp", None),
            P("section", None, "dp", None),
            P("section", "dp"),
            P("section", "dp", None),
            P("section", "dp", None),
            P("section", None, "dp"),
            P("section", "dp"),
            P("section", None),
            P("section", None),
            P("section", None),
            P("section", "dp"),
            P("section", "dp", None),
        ),
        check_vma=False,
    )
```

```python
import functools

import jax
import jax.numpy as jnp
from jax import lax
from jax.experimental import pallas as pl
from jax.experimental.pallas import tpu as pltpu
from jax.sharding import PartitionSpec as P

norm_eps = 1e-05
F32 = jnp.float32
BF16 = jnp.bfloat16
LANES = 128
TAPS = 4
VMEM_BYTES = 56 * 1024 * 1024


def dot_nn(a, b):
    return lax.dot_general(a, b, (((1,), (0,)), ((), ())), preferred_element_type=F32)


def dot_nt(a, b):
    return lax.dot_general(a, b, (((1,), (1,)), ((), ())), preferred_element_type=F32)


def dot_tn(a, b):
    return lax.dot_general(a, b, (((0,), (0,)), ((), ())), preferred_element_type=F32)


def split(a):
    high = a.astype(BF16)
    return high, (a - high.astype(F32)).astype(BF16)


def exact(dot, a, b):
    ah, al = split(a)
    bh, bl = split(b)
    return dot(ah, bh) + (dot(ah, bl) + dot(al, bh))


def near(dot, a, b):
    return exact(dot, a, b)


def triangle(lower):
    rows = lax.broadcasted_iota(jnp.int32, (LANES, LANES), 0)
    cols = lax.broadcasted_iota(jnp.int32, (LANES, LANES), 1)
    return jnp.where(rows >= cols if lower else rows <= cols, 1.0, 0.0).astype(BF16)


def running(tri, a):
    high = a.astype(BF16)
    rest = a - high.astype(F32)
    mid = rest.astype(BF16)
    low = (rest - mid.astype(F32)).astype(BF16)
    return dot_nn(tri, high) + (dot_nn(tri, mid) + dot_nn(tri, low))


def sigmoid(a):
    return 1.0 / (1.0 + jnp.exp(-a))


def softplus(a):
    return jnp.maximum(a, 0.0) + jnp.log1p(jnp.exp(-jnp.abs(a)))


def cols(j, width=LANES):
    return slice(j * width, (j + 1) * width)


def token_masks(ids):
    length = ids.shape[1]
    across = jnp.broadcast_to(ids, (length, length))
    wide = across.T
    rows = lax.broadcasted_iota(jnp.int32, (length, length), 0)
    lane = lax.broadcasted_iota(jnp.int32, (length, length), 1)
    linked = jnp.where((rows >= lane) & (wide == across), 1.0, 0.0)
    sees = [None]
    for k in range(1, TAPS):
        sees.append(jnp.where((rows >= k) & (pltpu.roll(wide, k, 0) == wide), 1.0, 0.0))
    return linked, sees


def take(which_ref, choices, into, sems):
    def start(choice):
        for i, ((ref, index), target) in enumerate(zip(choice, into)):
            pltpu.make_async_copy(ref if index is None else ref.at[index], target, sems.at[i]).start()

    if len(choices) == 1:
        start(choices[0])
        return
    for number, choice in enumerate(choices):
        pl.when(which_ref[0] == number)(functools.partial(start, choice))


def taken(into, sems, *numbers):
    for i in numbers:
        pltpu.make_async_copy(into[i], into[i], sems.at[i]).wait()


def conv_taps(v, sees):
    return [v] + [sees[k] * pltpu.roll(v, k, 0) for k in range(1, TAPS)]


def conv_sum(taps, cw_ref, cb_ref, at):
    total = cb_ref[:, at] + cw_ref[TAPS - 1 : TAPS, at] * taps[0]
    for k in range(1, TAPS):
        total = total + cw_ref[TAPS - 1 - k : TAPS - k, at] * taps[k]
    return total


def pair_of(values, j):
    lane = lax.broadcasted_iota(jnp.int32, (values.shape[0], LANES), 1)
    first = jnp.broadcast_to(values[:, 2 * j : 2 * j + 1], lane.shape)
    second = jnp.broadcast_to(values[:, 2 * j + 1 : 2 * j + 2], lane.shape)
    return jnp.where(lane < LANES // 2, first, second)


def halves(values):
    lane = lax.broadcasted_iota(jnp.int32, values.shape, 1)
    low = jnp.where(lane < LANES // 2, values, 0.0)
    return jnp.concatenate([low, values - low], axis=0)


def decay(cum, cum_t, linked, h):
    spread = cum[:, h : h + 1] - cum_t[h : h + 1, :]
    return linked * jnp.exp(jnp.minimum(spread, 0.0))


def micro_of(which_ref, mode):
    return (0, 1, which_ref[0], 1 - which_ref[0])[mode]


def fwd_kernel(plan, mode, which_ref, ids_ref, wm_hbm, wo_hbm, gin_ref, cw_ref, cb_ref, gg_ref, hp_ref, sk_ref, *refs):
    sources, refs = refs[: len(plan)], refs[len(plan) :]
    v_ref, n_ref, p_ref, dtr_ref, y_ref, mix_ref, g_scr, u_scr, wm_ref, wo_ref, sems, wsems = refs
    take(which_ref, [((source, index),) for source, index in zip(sources, plan)], (u_scr,), sems)
    inner, width = gg_ref.shape[1], p_ref.shape[1]
    pairs = inner // LANES
    pieces = [cols(c, 256) for c in range(width // 256)] + [slice(width, width + LANES)]
    loads = [pltpu.make_async_copy(wm_hbm.at[:, at], wm_ref.at[:, at], wsems.at[i]) for i, at in enumerate(pieces)]
    loads.append(pltpu.make_async_copy(wo_hbm, wo_ref, wsems.at[len(pieces)]))
    for load in loads:
        load.start()
    linked, sees = token_masks(ids_ref[micro_of(which_ref, mode)])
    taken((u_scr,), sems, 0)
    u = u_scr[...].astype(F32)
    r = lax.rsqrt(jnp.mean(u * u, axis=-1, keepdims=True) + norm_eps)
    n = (u * r * gin_ref[...]).astype(BF16)
    n_ref[...] = n
    for c in range(width // 256):
        loads[c].wait()
        p_ref[:, cols(c, 256)] = dot_nn(n, wm_ref[:, cols(c, 256)])
    loads[-2].wait()
    dtr = dot_nn(n, wm_ref[:, width:])
    dtr_ref[...] = dtr

    def conv(j):
        total = conv_sum(conv_taps(p_ref[:, inner + j * LANES : inner + (j + 1) * LANES], sees), cw_ref, cb_ref, cols(j))
        return total * sigmoid(total)

    b_state = conv(pairs)
    c_state = conv(pairs + 1)
    cross = exact(dot_nt, c_state, b_state)
    dt = softplus(dtr + hp_ref[0:1, :])
    cum = running(triangle(True), -dt * jnp.exp(hp_ref[1:2, :]))
    cum_t = cum.T
    squares = jnp.zeros((u.shape[0], LANES), F32)
    for j in range(pairs):
        at = cols(j)
        x = conv(j)
        m = jnp.concatenate([cross * decay(cum, cum_t, linked, 2 * j), cross * decay(cum, cum_t, linked, 2 * j + 1)], axis=1)
        y = near(dot_nn, m, halves(x * pair_of(dt, j))) + sk_ref[:, at] * x
        y_ref[:, at] = y
        z = p_ref[:, at]
        g = y * (z * sigmoid(z))
        g_scr[:, at] = g
        squares = squares + g * g
    r2 = lax.rsqrt(jnp.sum(squares, axis=-1, keepdims=True) / inner + norm_eps)
    for j in range(pairs):
        at = cols(j)
        mix_ref[:, at] = (g_scr[:, at] * r2 * gg_ref[:, at]).astype(BF16)
    mixed = mix_ref[...]
    loads[-1].wait()
    for c in range(u.shape[1] // 256):
        at = cols(c, 256)
        v_ref[:, at] = (u[:, at] + dot_nn(mixed, wo_ref[:, at])).astype(BF16)


def bwd_kernel(plan, mode, which_ref, ids_ref, wm_hbm, wo_hbm, gin_ref, cw_ref, cb_ref, gg_ref, hp_ref, sk_ref, *refs):
    count = 5 * len(plan)
    sources, refs = refs[:count], refs[count:]
    gi_ref, gl_ref, gp_ref, gdt_ref, dch_ref, din_ref, dgin_ref, dhp_ref = refs[:8]
    g_scr, gm_scr, gv_ref, u_ref, p_ref, dtr_ref, y_ref, wm_ref, wo_ref, sems, wsems = refs[8:]
    load_out = pltpu.make_async_copy(wo_hbm, wo_ref, wsems.at[0])
    load_main = pltpu.make_async_copy(wm_hbm, wm_ref, wsems.at[1])
    into = (gv_ref, u_ref, p_ref, dtr_ref, y_ref)
    choices = [list(zip(sources[5 * i : 5 * i + 5], indices)) for i, indices in enumerate(plan)]
    take(which_ref, choices, into[:1], sems)
    load_out.start()
    take(which_ref, [choice[1:] for choice in choices], into[1:], sems.at[1:])
    load_main.start()
    dch_ref[...] = jnp.zeros(dch_ref.shape, F32)
    din_ref[...] = jnp.zeros(din_ref.shape, F32)
    inner = gg_ref.shape[1]
    pairs = inner // LANES
    length = gv_ref.shape[0]
    linked, sees = token_masks(ids_ref[micro_of(which_ref, mode)])
    taken(into, sems, 0)
    load_out.wait()
    gb = gv_ref[...]
    for c in range(inner // 256):
        gm_scr[:, cols(c, 256)] = dot_nt(gb, wo_ref[cols(c, 256), :])
    taken(into, sems, 1, 2, 3, 4)

    def conv(j):
        taps = conv_taps(p_ref[:, inner + j * LANES : inner + (j + 1) * LANES], sees)
        total = conv_sum(taps, cw_ref, cb_ref, cols(j))
        sig = sigmoid(total)
        return taps, total, sig

    def conv_back(j, taps, total, sig, grad):
        at = cols(j)
        ds = grad * (sig * (1.0 + total * (1.0 - sig)))
        dch_ref[TAPS : TAPS + 1, at] = jnp.sum(ds, axis=0, keepdims=True)
        dch_ref[TAPS - 1 : TAPS, at] = jnp.sum(ds * taps[0], axis=0, keepdims=True)
        dv = cw_ref[TAPS - 1 : TAPS, at] * ds
        for k in range(1, TAPS):
            row = slice(TAPS - 1 - k, TAPS - k)
            dch_ref[row, at] = jnp.sum(ds * taps[k], axis=0, keepdims=True)
            dv = dv + cw_ref[row, at] * pltpu.roll(sees[k] * ds, length - k, 0)
        gp_ref[:, inner + j * LANES : inner + (j + 1) * LANES] = dv.astype(BF16)

    squares = jnp.zeros((length, LANES), F32)
    inners = jnp.zeros((length, LANES), F32)
    for j in range(pairs):
        at = cols(j)
        z = p_ref[:, at]
        g = y_ref[:, at] * (z * sigmoid(z))
        g_scr[:, at] = g
        squares = squares + g * g
        inners = inners + gm_scr[:, at] * gg_ref[:, at] * g
    r2 = lax.rsqrt(jnp.sum(squares, axis=-1, keepdims=True) / inner + norm_eps)
    pull = r2 * r2 * r2 * (jnp.sum(inners, axis=-1, keepdims=True) / inner)

    tb, sb, gb_sig = conv(pairs)
    b_state = sb * gb_sig
    tc, sc, gc_sig = conv(pairs + 1)
    c_state = sc * gc_sig
    cross = exact(dot_nt, c_state, b_state)
    dt_arg = dtr_ref[...] + hp_ref[0:1, :]
    dt = softplus(dt_arg)
    rate = jnp.exp(hp_ref[1:2, :])
    cum = running(triangle(True), -dt * rate)
    cum_t = cum.T
    dcross = jnp.zeros((length, length), F32)
    dcum = jnp.zeros((length, LANES), F32)
    ddt = jnp.zeros((length, LANES), F32)
    lane = lax.broadcasted_iota(jnp.int32, (2 * LANES, LANES), 1)
    row = lax.broadcasted_iota(jnp.int32, (2 * LANES, LANES), 0)
    half = jnp.where((row % LANES) < LANES // 2, 0, 1)
    for j in range(pairs):
        at = cols(j)
        pick = jnp.where(lane == 2 * j + half, 1.0, 0.0).astype(BF16)
        gm = gm_scr[:, at]
        g = g_scr[:, at]
        din_ref[0:1, at] = jnp.sum(gm * (g * r2), axis=0, keepdims=True)
        dg = gm * gg_ref[:, at] * r2 - g * pull
        z = p_ref[:, at]
        sig = sigmoid(z)
        y = y_ref[:, at]
        dy = dg * (z * sig)
        gp_ref[:, at] = (dg * y * (sig * (1.0 + z * (1.0 - sig)))).astype(BF16)
        taps, total, tsig = conv(j)
        x = total * tsig
        dtp = pair_of(dt, j)
        xw = x * dtp
        dy_st = halves(dy)
        l1 = decay(cum, cum_t, linked, 2 * j)
        l2 = decay(cum, cum_t, linked, 2 * j + 1)
        dm = near(dot_nt, dy_st, xw)
        dcross = dcross + dm[:length] * l1 + dm[length:] * l2
        m = jnp.concatenate([cross * l1, cross * l2], axis=0)
        dxw = near(dot_tn, m, dy_st)
        skip = sk_ref[:, at]
        din_ref[1:2, at] = jnp.sum(dy * x, axis=0, keepdims=True)
        q = dy * (y - skip * x) - dxw * xw
        dcum = dcum + dot_nn(jnp.concatenate(split(q), axis=1), pick)
        ddt = ddt + dot_nn(jnp.concatenate(split(dxw * x), axis=1), pick)
        conv_back(j, taps, total, tsig, skip * dy + dxw * dtp)
    conv_back(pairs, tb, sb, gb_sig, exact(dot_tn, dcross, c_state))
    conv_back(pairs + 1, tc, sc, gc_sig, exact(dot_nn, dcross, b_state))
    dlog = running(triangle(False), dcum)
    draw = (ddt - rate * dlog) * sigmoid(dt_arg)
    gdt = draw.astype(BF16)
    gdt_ref[...] = gdt
    dhp_ref[0:1, :] = jnp.sum(draw, axis=0, keepdims=True)
    dhp_ref[1:2, :] = jnp.sum(dlog * (-dt * rate), axis=0, keepdims=True)
    dhp_ref[2:8, :] = jnp.zeros((6, LANES), F32)
    u = u_ref[...].astype(F32)
    gin = gin_ref[...]
    r = lax.rsqrt(jnp.mean(u * u, axis=-1, keepdims=True) + norm_eps)
    gp = gp_ref[...]
    width = gp.shape[1]
    load_main.wait()
    gn = jnp.concatenate(
        [dot_nt(gp, wm_ref[cols(c, 256), :width]) + dot_nt(gdt, wm_ref[cols(c, 256), width:]) for c in range(u.shape[1] // 256)], axis=1
    )
    dgin_ref[...] = jnp.broadcast_to(jnp.sum(gn * (u * r), axis=0, keepdims=True), dgin_ref.shape)
    gng = gn * gin
    back = r * r * r * jnp.mean(gng * u, axis=-1, keepdims=True)
    grad = gb.astype(F32) + (gng * r - u * back)
    gi_ref[...] = grad
    gl_ref[...] = grad.astype(BF16)


def shape_of(shape, dtype=F32):
    return jax.ShapeDtypeStruct(shape, dtype)


VMEM_SPEC = pl.BlockSpec(memory_space=pltpu.VMEM)
HBM_SPEC = pl.BlockSpec(memory_space=pltpu.HBM)
SMEM_SPEC = pl.BlockSpec(memory_space=pltpu.SMEM)
PARAMS = pltpu.CompilerParams(vmem_limit_bytes=VMEM_BYTES)


def layer_sizes(weights):
    return weights[0].shape[0], weights[1].shape[0], weights[0].shape[1] - LANES


def forward_layer(mode, which, ids, weights, choices):
    tok = ids.shape[2]
    feat, inner, width = layer_sizes(weights)
    return pl.pallas_call(
        functools.partial(fwd_kernel, tuple(index for _, index in choices), mode),
        in_specs=[SMEM_SPEC, VMEM_SPEC] + [HBM_SPEC] * 2 + [VMEM_SPEC] * 6 + [HBM_SPEC] * len(choices),
        out_specs=[VMEM_SPEC] * 6,
        out_shape=(
            shape_of((tok, feat), BF16),
            shape_of((tok, feat), BF16),
            shape_of((tok, width)),
            shape_of((tok, LANES)),
            shape_of((tok, inner)),
            shape_of((tok, inner), BF16),
        ),
        scratch_shapes=[
            pltpu.VMEM((tok, inner), F32),
            pltpu.VMEM((tok, feat), BF16),
            pltpu.VMEM(weights[0].shape, BF16),
            pltpu.VMEM(weights[1].shape, BF16),
            pltpu.SemaphoreType.DMA((1,)),
            pltpu.SemaphoreType.DMA((width // 256 + 2,)),
        ],
        compiler_params=PARAMS,
        name="layer_forward",
    )(which, ids, *weights, *[source for source, _ in choices])


def backward_layer(mode, which, ids, weights, choices):
    tok = ids.shape[2]
    feat, inner, width = layer_sizes(weights)
    return pl.pallas_call(
        functools.partial(bwd_kernel, tuple(tuple(index for _, index in choice) for choice in choices), mode),
        in_specs=[SMEM_SPEC, VMEM_SPEC] + [HBM_SPEC] * 2 + [VMEM_SPEC] * 6 + [HBM_SPEC] * (5 * len(choices)),
        out_specs=[VMEM_SPEC] * 8,
        out_shape=(
            shape_of((tok, feat)),
            shape_of((tok, feat), BF16),
            shape_of((tok, width), BF16),
            shape_of((tok, LANES), BF16),
            shape_of((8, width - inner)),
            shape_of((8, inner)),
            shape_of((8, feat)),
            shape_of((8, LANES)),
        ),
        scratch_shapes=[
            pltpu.VMEM((tok, inner), F32),
            pltpu.VMEM((tok, inner), F32),
            pltpu.VMEM((tok, feat), BF16),
            pltpu.VMEM((tok, feat), BF16),
            pltpu.VMEM((tok, width), F32),
            pltpu.VMEM((tok, LANES), F32),
            pltpu.VMEM((tok, inner), F32),
            pltpu.VMEM(weights[0].shape, BF16),
            pltpu.VMEM(weights[1].shape, BF16),
            pltpu.SemaphoreType.DMA((5,)),
            pltpu.SemaphoreType.DMA((2,)),
        ],
        compiler_params=PARAMS,
        name="layer_backward",
    )(which, ids, *weights, *[source for choice in choices for source, _ in choice])


def lay(blocks, size, chunks):
    lane = lax.broadcasted_iota(jnp.int32, (8, LANES), 1)
    out = [jnp.zeros((8, LANES), F32) for _ in range(chunks)]
    for i, block in enumerate(blocks):
        chunk, shift = (i * size) // LANES, (i * size) % LANES
        turned = pltpu.roll(block, shift, 1) if shift else block
        out[chunk] = jnp.where((lane >= shift) & (lane < shift + size), turned, out[chunk])
        if shift + size > LANES:
            out[chunk + 1] = jnp.where(lane < shift + size - LANES, turned, out[chunk + 1])
    return out


def cut(chunks, size, i):
    lane = lax.broadcasted_iota(jnp.int32, (8, LANES), 1)
    chunk, shift = (i * size) // LANES, (i * size) % LANES
    turn = (LANES - shift) % LANES
    block = pltpu.roll(chunks[chunk], turn, 1) if turn else chunks[chunk]
    if shift + size > LANES:
        block = jnp.where(lane < LANES - shift, block, pltpu.roll(chunks[chunk + 1], turn, 1))
    return jnp.where(lane < size, block, 0.0)


def pack_kernel(wm_ref, wo_ref, wdt_ref, cw_ref, cb_ref, gg_ref, ng_ref, out_ref, line):
    rows, width = wm_ref.shape
    feat = wo_ref.shape[1]
    blocks = wo_ref.shape[0] // rows
    out_ref[:, :width] = wm_ref[...]
    for b in range(blocks):
        out_ref[:, width + b * feat : width + (b + 1) * feat] = wo_ref[b * rows : (b + 1) * rows, :]
    last = width + blocks * feat
    out_ref[:, last:] = jnp.zeros((rows, 2 * LANES), BF16)
    out_ref[:, last : last + wdt_ref.shape[1]] = wdt_ref[...]
    line[...] = jnp.zeros(line.shape, F32)
    line[0:TAPS, : cw_ref.shape[1]] = cw_ref[...].astype(F32)
    for k, ref in enumerate((cb_ref, gg_ref, ng_ref)):
        line[TAPS + k : TAPS + k + 1, : ref.shape[1]] = ref[...].astype(F32)
    out_ref[0:16, last + LANES :] = line[...].astype(BF16)


def pack_shard(wm, wo, wdt, cw, cb, gg, ng):
    rows, width = wm.shape
    full = width + wo.shape[0] // rows * wo.shape[1] + 2 * LANES
    return pl.pallas_call(
        pack_kernel,
        out_shape=shape_of((rows, full), BF16),
        scratch_shapes=[pltpu.VMEM((16, LANES), F32)],
        compiler_params=PARAMS,
        name="pack_shard",
    )(wm, wo, wdt, cw, cb, gg, ng)


Z_CHIPS = 4


def spot(z, y, c):
    return (z * 2 + y) * 2 + c


def routed(value, move):
    pairs = []
    for z in range(Z_CHIPS):
        for y in range(2):
            for c in range(2):
                target = move(z, y, c)
                if target is not None:
                    pairs.append((spot(z, y, c), spot(*target)))
    return lax.ppermute(value, "dp", pairs)


def to_core(z, y, c):
    return z, y, 1 - c


def to_y(z, y, c):
    return z, 1 - y, c


def to_near(z, y, c):
    return z ^ 1, y, c


def to_middle(z, y, c):
    return (3 - z, y, c) if z in (1, 2) else None


def to_ends(z, y, c):
    return (z ^ 1, y, c) if z in (1, 2) else None


def from_ends(z, y, c):
    return (z ^ 1, y, c) if z in (0, 3) else None


def slot_places(z):
    return (z, z + 1 - 2 * lax.rem(z, 2), jnp.where(z < 2, 2, 1), jnp.where(z < 2, 3, 0))


def gather_slots(own):
    near = routed(own, to_near)
    second = routed(own, to_middle)
    last = routed(near, to_middle)
    second = second + routed(second, to_ends)
    last = last + routed(last, to_ends)
    mine = [jnp.concatenate([routed(block, to_y), block], axis=0) for block in (own, near, second, last)]
    return mine + [routed(pair, to_core) for pair in mine]


def scatter_slots(kept, sent):
    rows = kept[0].shape[0] // 2
    parts = [None] * 4
    for slot in (3, 2, 1, 0):
        total = kept[slot].astype(F32) + routed(sent[slot], to_core).astype(F32)
        parts[slot] = total[rows:] + routed(total[:rows].astype(BF16), to_y).astype(F32)
    own, near, second, last = parts
    last = last + routed(last.astype(BF16), from_ends).astype(F32)
    second = second + routed(second.astype(BF16), from_ends).astype(F32)
    near = near + routed(last.astype(BF16), to_middle).astype(F32)
    return own, routed(second.astype(BF16), to_middle), routed(near.astype(BF16), to_near)


def owners_of(where_ref):
    z, y, c = where_ref[1], where_ref[2], where_ref[3]
    return [(spot(at, 1 - y, core), spot(at, y, core)) for core in (c, 1 - c) for at in slot_places(z)]


def settle_kernel(chans, where_ref, *refs):
    pairs, (wm_ref, wo_ref, cw_ref, cb_ref, gg_ref, gin_ref, line_ref, sem) = refs[:8], refs[8:]
    rows = pairs[0].shape[0] // 2
    feat = wo_ref.shape[1]
    width = wm_ref.shape[1] - LANES
    inner = wo_ref.shape[0]
    last = width + inner
    copies = []
    for pair, owners in zip(pairs, owners_of(where_ref)):
        for half, owner in enumerate(owners):
            mine = pl.ds(half * rows, rows)
            to = pl.ds(pl.multiple_of(owner * rows, 16), rows)
            copies.append((pair.at[pl.ds(half * rows, 16), pl.ds(last + LANES, LANES)], line_ref.at[owner]))
            copies.append((pair.at[mine, pl.ds(0, width)], wm_ref.at[to, pl.ds(0, width)]))
            copies.append((pair.at[mine, pl.ds(last, LANES)], wm_ref.at[to, pl.ds(width, LANES)]))
            for b in range(inner // wm_ref.shape[0]):
                into = pl.ds(pl.multiple_of((owner * (inner // wm_ref.shape[0]) + b) * rows, 16), rows)
                copies.append((pair.at[mine, pl.ds(width + b * feat, feat)], wo_ref.at[into]))
    for source, target in copies:
        pltpu.make_async_copy(source, target, sem).start()
    for whole in (wm_ref, wo_ref, line_ref):
        pltpu.make_async_copy(whole, whole, sem).wait()
    lines = [line_ref[i].astype(F32)[0:8] for i in range(line_ref.shape[0])]
    for c, chunk in enumerate(lay(lines, chans, cw_ref.shape[1] // LANES)):
        cw_ref[:, cols(c)] = chunk[0:TAPS]
        cb_ref[:, cols(c)] = chunk[TAPS : TAPS + 1]
    for c, chunk in enumerate(lay(lines, inner // len(lines), gg_ref.shape[1] // LANES)):
        gg_ref[:, cols(c)] = chunk[TAPS + 1 : TAPS + 2]
    for c, chunk in enumerate(lay(lines, rows, gin_ref.shape[1] // LANES)):
        gin_ref[:, cols(c)] = chunk[TAPS + 2 : TAPS + 3]


def settle(where, pairs, width, chans, feat):
    rows, full = pairs[0].shape[0] // 2, pairs[0].shape[1]
    owners, inner = feat // rows, full - width - 2 * LANES
    return pl.pallas_call(
        functools.partial(settle_kernel, chans),
        in_specs=[SMEM_SPEC] + [HBM_SPEC] * 8,
        out_specs=[VMEM_SPEC] * 6,
        out_shape=(
            shape_of((feat, width + LANES), BF16),
            shape_of((inner, feat), BF16),
            shape_of((TAPS, owners * chans)),
            shape_of((1, owners * chans)),
            shape_of((1, inner)),
            shape_of((1, feat)),
        ),
        scratch_shapes=[pltpu.VMEM((owners, 16, LANES), BF16), pltpu.SemaphoreType.DMA],
        compiler_params=PARAMS,
        name="settle_weights",
    )(where, *pairs)


def weight_kernel(rows, chans, which_ref, *refs):
    sources, smalls, pairs, scratch, sems, out_ref, out_sem = refs[:20], refs[20:29], refs[29:37], refs[37:42], refs[42], refs[43], refs[44]
    tok = sources[0].shape[0]
    into = [ref.at[part * tok : (part + 1) * tok] for part in range(2) for ref in scratch]
    take(which_ref, [[(source, None) for source in sources[10 * i : 10 * i + 10]] for i in range(2)], into, sems)
    n_ref, mix_ref, gp_ref, gb_ref, gdt_ref = scratch
    feat, inner, width = n_ref.shape[1], mix_ref.shape[1], gp_ref.shape[1]
    blocks = inner // feat
    last = width + inner
    early = jnp.where(which_ref[0] == 0, 0.0, 1.0)
    sums = [one[...] + early * zero[...] + (1.0 - early) * two[...] for zero, one, two in zip(smalls[0::3], smalls[1::3], smalls[2::3])]
    pieces = [[total[:, cols(c)] for c in range(total.shape[1] // LANES)] for total in sums]
    line = lax.broadcasted_iota(jnp.int32, (8, LANES), 0)
    for i in range(feat // rows):
        block = cut(pieces[0], chans, i)
        block = jnp.where(line == TAPS + 1, jnp.broadcast_to(cut(pieces[1], blocks * rows, i)[0:1], block.shape), block)
        block = jnp.where(line == TAPS + 2, jnp.broadcast_to(cut(pieces[2], rows, i)[0:1], block.shape), block)
        out_ref[i * rows : i * rows + 16, last + LANES :] = jnp.concatenate([block, jnp.zeros_like(block)], axis=0).astype(BF16)
        out_ref[i * rows + 16 : (i + 1) * rows, last + LANES :] = jnp.zeros((rows - 16, LANES), BF16)
    taken(into, sems, 0, 5, 2, 7, 4, 9)
    turned = n_ref[...].T
    for c in range(width // 256):
        out_ref[:, cols(c, 256)] = dot_nn(turned, gp_ref[:, cols(c, 256)]).astype(BF16)
    out_ref[:, last : last + LANES] = dot_nn(turned, gdt_ref[...]).astype(BF16)
    taken(into, sems, 1, 6, 3, 8)
    gb = gb_ref[...]
    for e in range(inner // 256):
        term = dot_tn(mix_ref[:, cols(e, 256)], gb).astype(BF16)
        at = e * 256
        while at < (e + 1) * 256:
            owner, inside = at // (blocks * rows), at % (blocks * rows)
            block, row = inside // rows, inside % rows
            count = min(rows - row, (e + 1) * 256 - at)
            out_ref[owner * rows + row : owner * rows + row + count, width + block * feat : width + (block + 1) * feat] = term[
                at - e * 256 : at - e * 256 + count
            ]
            at = at + count
    for pair, owners in reversed(list(zip(pairs, owners_of(which_ref)))):
        for half, owner in enumerate(owners):
            source = out_ref.at[pl.ds(pl.multiple_of(owner * rows, 16), rows)]
            pltpu.make_async_copy(source, pair.at[pl.ds(half * rows, rows)], out_sem).start()
    pltpu.make_async_copy(out_ref, out_ref, out_sem).wait()


def weight_terms(which, one, other, smalls, rows, chans):
    tok, feat = one[0].shape
    inner, width = one[1].shape[1], one[2].shape[1]
    full = width + inner + 2 * LANES
    return pl.pallas_call(
        functools.partial(weight_kernel, rows, chans),
        in_specs=[SMEM_SPEC] + [HBM_SPEC] * 20 + [VMEM_SPEC] * 9,
        out_specs=[HBM_SPEC] * 8,
        out_shape=(shape_of((2 * rows, full), BF16),) * 8,
        scratch_shapes=[pltpu.VMEM((2 * tok, part.shape[1]), BF16) for part in one[:5]]
        + [pltpu.SemaphoreType.DMA((10,)), pltpu.VMEM((feat, full), BF16), pltpu.SemaphoreType.DMA],
        compiler_params=PARAMS,
        name="weight_gradients",
    )(which, *one, *other, *smalls)


def unpack_kernel(own_ref, second_ref, near_ref, wm_ref, wo_ref, wdt_ref, cw_ref, cb_ref, gg_ref, ng_ref):
    rows, width = wm_ref.shape
    feat = wo_ref.shape[1]
    blocks = wo_ref.shape[0] // rows
    last = width + blocks * feat

    def total(at, count):
        some = slice(0, count)
        return own_ref[some, at] + (second_ref[some, at].astype(F32) + near_ref[some, at].astype(F32))

    for c in range(width // 256):
        wm_ref[:, cols(c, 256)] = total(cols(c, 256), rows)
    for b in range(blocks):
        wo_ref[b * rows : (b + 1) * rows, :] = total(slice(width + b * feat, width + (b + 1) * feat), rows)
    wdt_ref[...] = total(slice(last, last + LANES), rows)[:, : wdt_ref.shape[1]]
    line = total(slice(last + LANES, last + 2 * LANES), 16)
    cw_ref[...] = line[0:TAPS, : cw_ref.shape[1]]
    for k, ref in enumerate((cb_ref, gg_ref, ng_ref)):
        ref[...] = line[TAPS + k : TAPS + k + 1, : ref.shape[1]]


def unpack_sums(terms, wm, wo, wdt, cw, cb, gg, ng):
    return pl.pallas_call(
        unpack_kernel,
        out_shape=tuple(shape_of(part.shape) for part in (wm, wo, wdt, cw, cb, gg, ng)),
        compiler_params=PARAMS,
        name="unpack_sums",
    )(*terms)


def small_rows(vectors, rows):
    flat = jnp.concatenate([vector.reshape(-1) for vector in vectors])
    lines = -(-flat.shape[0] // LANES)
    wide = -(-lines // rows)
    flat = jnp.pad(flat, (0, lines * LANES - flat.shape[0])).reshape(lines, LANES)
    flat = jnp.pad(flat, ((0, rows * wide - lines), (0, 0)))
    return flat.reshape(wide, rows, LANES).transpose(1, 0, 2).reshape(rows, wide * LANES)


def small_flat(block, owners):
    rows, wide = block.shape[0] // owners, block.shape[1] // LANES
    return block.reshape(owners, rows, wide, LANES).transpose(0, 2, 1, 3).reshape(owners, wide * rows * LANES)


def total_over(value, axis):
    count = lax.axis_size(axis)
    step = 1
    while step < count:
        value = value + lax.ppermute(value, axis, [(i, i ^ step) for i in range(count)])
        step = step * 2
    return value


def shards(inputs, segments, cotangent, norm_gain, w_main, w_dt, conv_weight, conv_bias, dt_bias, a_log, skip_d, gate_gain, w_out):
    first = lax.axis_index("section") == 0
    dp = lax.axis_size("dp")
    feat = inputs.shape[2]
    rows, width = w_main.shape[1:]
    heads = w_dt.shape[2]
    chans, own_inner = conv_weight.shape[2], gate_gain.shape[1]
    inner = own_inner * dp
    blocks = own_inner // rows

    owned = (w_main[0], w_out[0], w_dt[0], conv_weight[0], conv_bias, gate_gain, norm_gain)
    aligned = rows % 16 == 0 and dp == 4 * Z_CHIPS
    side = lax.axis_index("section")
    place = lax.axis_index("dp")
    where = jnp.stack([side, place // 4, place // 2 % 2, place % 2]).astype(jnp.int32)
    if aligned:
        wm, wo, cw, cb, gg, gin = settle(where, gather_slots(pack_shard(*owned)), width, chans, feat)
    else:
        small = small_rows((conv_weight[0], conv_bias[0], gate_gain[0], norm_gain[0]), rows)
        out_block = w_out[0].reshape(blocks, rows, feat).transpose(1, 0, 2).reshape(rows, inner)
        packed = jnp.concatenate([w_main[0], out_block, jnp.pad(w_dt[0], ((0, 0), (0, LANES - heads))), small], axis=1)
        whole = lax.all_gather(packed, "dp", axis=0, tiled=True)
    marks = [TAPS * chans, (TAPS + 1) * chans, (TAPS + 1) * chans + own_inner, (TAPS + 1) * chans + own_inner + rows]
    if not aligned:
        wm = jnp.concatenate([whole[:, :width], whole[:, width + inner : width + inner + LANES]], axis=1)
        wo = whole[:, width : width + inner].reshape(dp, rows, blocks, feat).transpose(0, 2, 1, 3).reshape(inner, feat)
        flat = small_flat(whole[:, width + inner + LANES :], dp).astype(F32)
        cw = flat[:, : marks[0]].reshape(dp, TAPS, chans).transpose(1, 0, 2).reshape(TAPS, dp * chans)
        cb = flat[:, marks[0] : marks[1]].reshape(1, dp * chans)
        gg = flat[:, marks[1] : marks[2]].reshape(1, inner)
        gin = flat[:, marks[2] : marks[3]].reshape(1, feat)
    hp = jnp.pad(jnp.concatenate([dt_bias, a_log], axis=0), ((0, 6), (0, LANES - heads)))
    sk = jnp.repeat(skip_d, inner // heads, axis=1)
    weights = (wm, wo, gin, cw, cb, gg, hp, sk)

    def choose(one, other):
        return jnp.where(first, one, other)

    up = [(0, 1)]
    down = [(1, 0)]
    ids = segments.astype(F32)[:, None, :]
    f0 = forward_layer(0, where, ids, weights, [(inputs, 0)])
    r0 = lax.ppermute(f0[0], "section", up)
    f1 = forward_layer(3, where, ids, weights, [(inputs, 1), (r0, None)])
    r1 = lax.ppermute(f1[0], "section", up)
    f2 = forward_layer(1, where, ids, weights, [(inputs, 1), (r1, None)])

    kept = [(part, None) for part in f1[2:5]]
    now = [[(cotangent, 0), (inputs, 1)] + kept, [(cotangent, 0), (r0, None)] + kept]
    b0 = backward_layer(0, where, ids, weights, now)
    d0 = lax.ppermute(b0[1], "section", down)
    now = [
        [(d0, None), (inputs, 0)] + [(part, None) for part in f0[2:5]],
        [(cotangent, 1), (r1, None)] + [(part, None) for part in f2[2:5]],
    ]
    b1 = backward_layer(2, where, ids, weights, now)
    d1 = lax.ppermute(b1[1], "section", down)
    b2 = backward_layer(1, where, ids, weights, [[(d1, None), (inputs, 1)] + kept])
    hidden = jnp.stack([choose(f0[0], f1[0]), choose(f1[0], f2[0])])[None]
    grad_inputs = jnp.stack([choose(b1[0], b0[0]), choose(b2[0], b1[0])])[None]
    dch, din, dgin, dhp = tuple(choose(two, zero) + one for zero, one, two in zip(b0[4:], b1[4:], b2[4:]))
    on_first = (f0[1], f0[5], b1[2], d0, b1[3]), (f1[1], f1[5], b2[2], d1, b2[3])
    on_last = (f2[1], f2[5], b1[2], cotangent[1], b1[3]), (f1[1], f1[5], b0[2], cotangent[0], b0[3])
    if aligned:
        smalls = [part[i] for i in (4, 5, 6) for part in (b0, b1, b2)]
        blocks_out = weight_terms(where, on_first[0] + on_first[1], on_last[0] + on_last[1], smalls, rows, chans)
    else:
        n, mix, gp, gb, gdt = tuple(
            jnp.concatenate([choose(on_first[0][i], on_last[0][i]), choose(on_first[1][i], on_last[1][i])], axis=0) for i in range(5)
        )
        own = [
            small_rows(
                (
                    dch[:TAPS, i * chans : (i + 1) * chans],
                    dch[TAPS, i * chans : (i + 1) * chans],
                    din[0, i * own_inner : (i + 1) * own_inner],
                    dgin[0, i * rows : (i + 1) * rows],
                ),
                rows,
            )
            for i in range(dp)
        ]
        wide = dot_tn(mix, gb).reshape(dp, blocks, rows, feat).transpose(0, 2, 1, 3).reshape(feat, inner)
        parts = [dot_tn(n, gp), wide, dot_tn(n, gdt), jnp.concatenate(own, axis=0)]
        packed_grad = jnp.concatenate([part.astype(BF16) for part in parts], axis=1)
    if aligned:
        terms = scatter_slots(blocks_out[:4], blocks_out[4:])
    else:
        summed = lax.psum_scatter(packed_grad, "dp", scatter_dimension=0, tiled=True)
    dskip = din[1].reshape(heads, inner // heads).sum(axis=1)
    heads_sum = total_over(jnp.concatenate([dhp[:2, :heads], dskip[None]], axis=0), "dp")
    if aligned:
        g_main, g_out, g_dt, g_cw, g_cb, g_gg, g_ng = unpack_sums(terms, *owned)
    else:
        summed = summed.astype(F32)
        got = small_flat(summed[:, width + inner + LANES :], 1)[0]
        g_main = summed[:, :width]
        g_out = summed[:, width : width + inner].reshape(rows, blocks, feat).transpose(1, 0, 2).reshape(own_inner, feat)
        g_dt = summed[:, width + inner : width + inner + heads]
        g_cw = got[: marks[0]].reshape(TAPS, chans)
        g_cb, g_gg, g_ng = (got[None, marks[i] : marks[i + 1]] for i in range(3))
    return (
        hidden,
        grad_inputs,
        g_ng,
        g_main[None],
        g_dt[None],
        g_cw[None],
        g_cb,
        heads_sum[0:1],
        heads_sum[1:2],
        heads_sum[2:3],
        g_gg,
        g_out[None],
    )


def solution(mesh):
    placed = (
        P(None, "dp", None),
        P(None, "dp"),
        P(None, "dp", None),
        P("section", "dp"),
        P("section", "dp", None),
        P("section", "dp", None),
        P("section", None, "dp"),
        P("section", "dp"),
        P("section", None),
        P("section", None),
        P("section", None),
        P("section", "dp"),
        P("section", "dp", None),
    )
    return jax.shard_map(
        shards,
        mesh=mesh,
        in_specs=placed,
        out_specs=(
            P("section", None, "dp", None),
            P("section", None, "dp", None),
            P("section", "dp"),
            P("section", "dp", None),
            P("section", "dp", None),
            P("section", None, "dp"),
            P("section", "dp"),
            P("section", None),
            P("section", None),
            P("section", None),
            P("section", "dp"),
            P("section", "dp", None),
        ),
        check_vma=False,
    )
```

```python
import functools

import jax
import jax.numpy as jnp
from jax import lax
from jax.experimental import pallas as pl
from jax.experimental.pallas import tpu as pltpu
from jax.sharding import PartitionSpec as P

norm_eps = 1e-05
F32 = jnp.float32
BF16 = jnp.bfloat16
LANES = 128
TAPS = 4
VMEM_BYTES = 28 * 1024 * 1024


def dot_nn(a, b):
    return lax.dot_general(a, b, (((1,), (0,)), ((), ())), preferred_element_type=F32)


def dot_nt(a, b):
    return lax.dot_general(a, b, (((1,), (1,)), ((), ())), preferred_element_type=F32)


def dot_tn(a, b):
    return lax.dot_general(a, b, (((0,), (0,)), ((), ())), preferred_element_type=F32)


def split(a):
    high = a.astype(BF16)
    return high, (a - high.astype(F32)).astype(BF16)


def exact(dot, a, b):
    ah, al = split(a)
    bh, bl = split(b)
    return dot(ah, bh) + (dot(ah, bl) + dot(al, bh))


def near(dot, a, b):
    return exact(dot, a, b)


def triangle(lower):
    rows = lax.broadcasted_iota(jnp.int32, (LANES, LANES), 0)
    cols = lax.broadcasted_iota(jnp.int32, (LANES, LANES), 1)
    return jnp.where(rows >= cols if lower else rows <= cols, 1.0, 0.0).astype(BF16)


def running(tri, a):
    high = a.astype(BF16)
    rest = a - high.astype(F32)
    mid = rest.astype(BF16)
    low = (rest - mid.astype(F32)).astype(BF16)
    return dot_nn(tri, high) + (dot_nn(tri, mid) + dot_nn(tri, low))


def sigmoid(a):
    return 1.0 / (1.0 + jnp.exp(-a))


def softplus(a):
    return jnp.maximum(a, 0.0) + jnp.log1p(jnp.exp(-jnp.abs(a)))


def cols(j, width=LANES):
    return slice(j * width, (j + 1) * width)


def token_masks(ids):
    length = ids.shape[1]
    across = jnp.broadcast_to(ids, (length, length))
    wide = across.T
    rows = lax.broadcasted_iota(jnp.int32, (length, length), 0)
    lane = lax.broadcasted_iota(jnp.int32, (length, length), 1)
    linked = jnp.where((rows >= lane) & (wide == across), 1.0, 0.0)
    sees = [None]
    for k in range(1, TAPS):
        sees.append(jnp.where((rows >= k) & (pltpu.roll(wide, k, 0) == wide), 1.0, 0.0))
    return linked, sees


def take(which_ref, choices, into, sems):
    def start(choice):
        for i, ((ref, index), target) in enumerate(zip(choice, into)):
            pltpu.make_async_copy(ref if index is None else ref.at[index], target, sems.at[i]).start()

    if len(choices) == 1:
        start(choices[0])
        return
    for number, choice in enumerate(choices):
        pl.when(which_ref[0] == number)(functools.partial(start, choice))


def taken(into, sems, *numbers):
    for i in numbers:
        pltpu.make_async_copy(into[i], into[i], sems.at[i]).wait()


def conv_taps(v, sees):
    return [v] + [sees[k] * pltpu.roll(v, k, 0) for k in range(1, TAPS)]


def conv_sum(taps, cw_ref, cb_ref, at):
    total = cb_ref[:, at] + cw_ref[TAPS - 1 : TAPS, at] * taps[0]
    for k in range(1, TAPS):
        total = total + cw_ref[TAPS - 1 - k : TAPS - k, at] * taps[k]
    return total


def pair_of(values, j):
    lane = lax.broadcasted_iota(jnp.int32, (values.shape[0], LANES), 1)
    first = jnp.broadcast_to(values[:, 2 * j : 2 * j + 1], lane.shape)
    second = jnp.broadcast_to(values[:, 2 * j + 1 : 2 * j + 2], lane.shape)
    return jnp.where(lane < LANES // 2, first, second)


def halves(values):
    lane = lax.broadcasted_iota(jnp.int32, values.shape, 1)
    low = jnp.where(lane < LANES // 2, values, 0.0)
    return jnp.concatenate([low, values - low], axis=0)


def decay(cum, cum_t, linked, h):
    spread = cum[:, h : h + 1] - cum_t[h : h + 1, :]
    return linked * jnp.exp(jnp.minimum(spread, 0.0))


def micro_of(which_ref, mode):
    return (0, 1, which_ref[0], 1 - which_ref[0])[mode]


def fwd_kernel(plan, mode, which_ref, ids_ref, wm_ref, wo_ref, gin_ref, cw_ref, cb_ref, gg_ref, hp_ref, sk_ref, *refs):
    sources, refs = refs[: len(plan)], refs[len(plan) :]
    v_ref, n_ref, p_ref, dtr_ref, y_ref, mix_ref, g_scr, u_scr, sems = refs
    take(which_ref, [((source, index),) for source, index in zip(sources, plan)], (u_scr,), sems)
    inner, width = gg_ref.shape[1], p_ref.shape[1]
    pairs = inner // LANES
    linked, sees = token_masks(ids_ref[micro_of(which_ref, mode)])
    taken((u_scr,), sems, 0)
    u = u_scr[...].astype(F32)
    r = lax.rsqrt(jnp.mean(u * u, axis=-1, keepdims=True) + norm_eps)
    n = (u * r * gin_ref[...]).astype(BF16)
    n_ref[...] = n
    for c in range(width // 256):
        p_ref[:, cols(c, 256)] = dot_nn(n, wm_ref[:, cols(c, 256)])
    dtr = dot_nn(n, wm_ref[:, width:])
    dtr_ref[...] = dtr

    def conv(j):
        total = conv_sum(conv_taps(p_ref[:, inner + j * LANES : inner + (j + 1) * LANES], sees), cw_ref, cb_ref, cols(j))
        return total * sigmoid(total)

    b_state = conv(pairs)
    c_state = conv(pairs + 1)
    cross = exact(dot_nt, c_state, b_state)
    dt = softplus(dtr + hp_ref[0:1, :])
    cum = running(triangle(True), -dt * jnp.exp(hp_ref[1:2, :]))
    cum_t = cum.T
    squares = jnp.zeros((u.shape[0], LANES), F32)
    for j in range(pairs):
        at = cols(j)
        x = conv(j)
        m = jnp.concatenate([cross * decay(cum, cum_t, linked, 2 * j), cross * decay(cum, cum_t, linked, 2 * j + 1)], axis=1)
        y = near(dot_nn, m, halves(x * pair_of(dt, j))) + sk_ref[:, at] * x
        y_ref[:, at] = y
        z = p_ref[:, at]
        g = y * (z * sigmoid(z))
        g_scr[:, at] = g
        squares = squares + g * g
    r2 = lax.rsqrt(jnp.sum(squares, axis=-1, keepdims=True) / inner + norm_eps)
    for j in range(pairs):
        at = cols(j)
        mix_ref[:, at] = (g_scr[:, at] * r2 * gg_ref[:, at]).astype(BF16)
    mixed = mix_ref[...]
    for c in range(u.shape[1] // 256):
        at = cols(c, 256)
        v_ref[:, at] = (u[:, at] + dot_nn(mixed, wo_ref[:, at])).astype(BF16)


def bwd_kernel(plan, mode, which_ref, ids_ref, wm_ref, wo_ref, gin_ref, cw_ref, cb_ref, gg_ref, hp_ref, sk_ref, *refs):
    count = 5 * len(plan)
    sources, refs = refs[:count], refs[count:]
    gi_ref, gl_ref, gp_ref, gdt_ref, dch_ref, din_ref, dgin_ref, dhp_ref = refs[:8]
    g_scr, gm_scr, gv_ref, u_ref, p_ref, dtr_ref, y_ref, sems = refs[8:]
    into = (gv_ref, u_ref, p_ref, dtr_ref, y_ref)
    choices = [list(zip(sources[5 * i : 5 * i + 5], indices)) for i, indices in enumerate(plan)]
    take(which_ref, choices, into[:1], sems)
    take(which_ref, [choice[1:] for choice in choices], into[1:], sems.at[1:])
    dch_ref[...] = jnp.zeros(dch_ref.shape, F32)
    din_ref[...] = jnp.zeros(din_ref.shape, F32)
    inner = gg_ref.shape[1]
    pairs = inner // LANES
    length = gv_ref.shape[0]
    linked, sees = token_masks(ids_ref[micro_of(which_ref, mode)])
    taken(into, sems, 0)
    gb = gv_ref[...]
    for c in range(inner // 256):
        gm_scr[:, cols(c, 256)] = dot_nt(gb, wo_ref[cols(c, 256), :])
    taken(into, sems, 1, 2, 3, 4)

    def conv(j):
        taps = conv_taps(p_ref[:, inner + j * LANES : inner + (j + 1) * LANES], sees)
        total = conv_sum(taps, cw_ref, cb_ref, cols(j))
        sig = sigmoid(total)
        return taps, total, sig

    def conv_back(j, taps, total, sig, grad):
        at = cols(j)
        ds = grad * (sig * (1.0 + total * (1.0 - sig)))
        dch_ref[TAPS : TAPS + 1, at] = jnp.sum(ds, axis=0, keepdims=True)
        dch_ref[TAPS - 1 : TAPS, at] = jnp.sum(ds * taps[0], axis=0, keepdims=True)
        dv = cw_ref[TAPS - 1 : TAPS, at] * ds
        for k in range(1, TAPS):
            row = slice(TAPS - 1 - k, TAPS - k)
            dch_ref[row, at] = jnp.sum(ds * taps[k], axis=0, keepdims=True)
            dv = dv + cw_ref[row, at] * pltpu.roll(sees[k] * ds, length - k, 0)
        gp_ref[:, inner + j * LANES : inner + (j + 1) * LANES] = dv.astype(BF16)

    squares = jnp.zeros((length, LANES), F32)
    inners = jnp.zeros((length, LANES), F32)
    for j in range(pairs):
        at = cols(j)
        z = p_ref[:, at]
        g = y_ref[:, at] * (z * sigmoid(z))
        g_scr[:, at] = g
        squares = squares + g * g
        inners = inners + gm_scr[:, at] * gg_ref[:, at] * g
    r2 = lax.rsqrt(jnp.sum(squares, axis=-1, keepdims=True) / inner + norm_eps)
    pull = r2 * r2 * r2 * (jnp.sum(inners, axis=-1, keepdims=True) / inner)

    tb, sb, gb_sig = conv(pairs)
    b_state = sb * gb_sig
    tc, sc, gc_sig = conv(pairs + 1)
    c_state = sc * gc_sig
    cross = exact(dot_nt, c_state, b_state)
    dt_arg = dtr_ref[...] + hp_ref[0:1, :]
    dt = softplus(dt_arg)
    rate = jnp.exp(hp_ref[1:2, :])
    cum = running(triangle(True), -dt * rate)
    cum_t = cum.T
    dcross = jnp.zeros((length, length), F32)
    dcum = jnp.zeros((length, LANES), F32)
    ddt = jnp.zeros((length, LANES), F32)
    lane = lax.broadcasted_iota(jnp.int32, (2 * LANES, LANES), 1)
    row = lax.broadcasted_iota(jnp.int32, (2 * LANES, LANES), 0)
    half = jnp.where((row % LANES) < LANES // 2, 0, 1)
    for j in range(pairs):
        at = cols(j)
        pick = jnp.where(lane == 2 * j + half, 1.0, 0.0).astype(BF16)
        gm = gm_scr[:, at]
        g = g_scr[:, at]
        din_ref[0:1, at] = jnp.sum(gm * (g * r2), axis=0, keepdims=True)
        dg = gm * gg_ref[:, at] * r2 - g * pull
        z = p_ref[:, at]
        sig = sigmoid(z)
        y = y_ref[:, at]
        dy = dg * (z * sig)
        gp_ref[:, at] = (dg * y * (sig * (1.0 + z * (1.0 - sig)))).astype(BF16)
        taps, total, tsig = conv(j)
        x = total * tsig
        dtp = pair_of(dt, j)
        xw = x * dtp
        dy_st = halves(dy)
        l1 = decay(cum, cum_t, linked, 2 * j)
        l2 = decay(cum, cum_t, linked, 2 * j + 1)
        dm = near(dot_nt, dy_st, xw)
        dcross = dcross + dm[:length] * l1 + dm[length:] * l2
        m = jnp.concatenate([cross * l1, cross * l2], axis=0)
        dxw = near(dot_tn, m, dy_st)
        skip = sk_ref[:, at]
        din_ref[1:2, at] = jnp.sum(dy * x, axis=0, keepdims=True)
        q = dy * (y - skip * x) - dxw * xw
        dcum = dcum + dot_nn(jnp.concatenate(split(q), axis=1), pick)
        ddt = ddt + dot_nn(jnp.concatenate(split(dxw * x), axis=1), pick)
        conv_back(j, taps, total, tsig, skip * dy + dxw * dtp)
    conv_back(pairs, tb, sb, gb_sig, exact(dot_tn, dcross, c_state))
    conv_back(pairs + 1, tc, sc, gc_sig, exact(dot_nn, dcross, b_state))
    dlog = running(triangle(False), dcum)
    draw = (ddt - rate * dlog) * sigmoid(dt_arg)
    gdt = draw.astype(BF16)
    gdt_ref[...] = gdt
    dhp_ref[0:1, :] = jnp.sum(draw, axis=0, keepdims=True)
    dhp_ref[1:2, :] = jnp.sum(dlog * (-dt * rate), axis=0, keepdims=True)
    dhp_ref[2:8, :] = jnp.zeros((6, LANES), F32)
    u = u_ref[...].astype(F32)
    gin = gin_ref[...]
    r = lax.rsqrt(jnp.mean(u * u, axis=-1, keepdims=True) + norm_eps)
    gp = gp_ref[...]
    width = gp.shape[1]
    gn = jnp.concatenate(
        [dot_nt(gp, wm_ref[cols(c, 256), :width]) + dot_nt(gdt, wm_ref[cols(c, 256), width:]) for c in range(u.shape[1] // 256)], axis=1
    )
    dgin_ref[...] = jnp.broadcast_to(jnp.sum(gn * (u * r), axis=0, keepdims=True), dgin_ref.shape)
    gng = gn * gin
    back = r * r * r * jnp.mean(gng * u, axis=-1, keepdims=True)
    grad = gb.astype(F32) + (gng * r - u * back)
    gi_ref[...] = grad
    gl_ref[...] = grad.astype(BF16)


def shape_of(shape, dtype=F32):
    return jax.ShapeDtypeStruct(shape, dtype)


VMEM_SPEC = pl.BlockSpec(memory_space=pltpu.VMEM)
HBM_SPEC = pl.BlockSpec(memory_space=pltpu.HBM)
SMEM_SPEC = pl.BlockSpec(memory_space=pltpu.SMEM)
PARAMS = pltpu.CompilerParams(vmem_limit_bytes=VMEM_BYTES)


def layer_sizes(weights):
    return weights[0].shape[0], weights[1].shape[0], weights[0].shape[1] - LANES


def forward_layer(mode, which, ids, weights, choices):
    tok = ids.shape[2]
    feat, inner, width = layer_sizes(weights)
    return pl.pallas_call(
        functools.partial(fwd_kernel, tuple(index for _, index in choices), mode),
        in_specs=[SMEM_SPEC, VMEM_SPEC] + [VMEM_SPEC] * 8 + [HBM_SPEC] * len(choices),
        out_specs=[VMEM_SPEC] * 6,
        out_shape=(
            shape_of((tok, feat), BF16),
            shape_of((tok, feat), BF16),
            shape_of((tok, width)),
            shape_of((tok, LANES)),
            shape_of((tok, inner)),
            shape_of((tok, inner), BF16),
        ),
        scratch_shapes=[
            pltpu.VMEM((tok, inner), F32),
            pltpu.VMEM((tok, feat), BF16),
            pltpu.SemaphoreType.DMA((1,)),
        ],
        compiler_params=PARAMS,
        name="layer_forward",
    )(which, ids, *weights, *[source for source, _ in choices])


def backward_layer(mode, which, ids, weights, choices):
    tok = ids.shape[2]
    feat, inner, width = layer_sizes(weights)
    return pl.pallas_call(
        functools.partial(bwd_kernel, tuple(tuple(index for _, index in choice) for choice in choices), mode),
        in_specs=[SMEM_SPEC, VMEM_SPEC] + [VMEM_SPEC] * 8 + [HBM_SPEC] * (5 * len(choices)),
        out_specs=[VMEM_SPEC] * 8,
        out_shape=(
            shape_of((tok, feat)),
            shape_of((tok, feat), BF16),
            shape_of((tok, width), BF16),
            shape_of((tok, LANES), BF16),
            shape_of((8, width - inner)),
            shape_of((8, inner)),
            shape_of((8, feat)),
            shape_of((8, LANES)),
        ),
        scratch_shapes=[
            pltpu.VMEM((tok, inner), F32),
            pltpu.VMEM((tok, inner), F32),
            pltpu.VMEM((tok, feat), BF16),
            pltpu.VMEM((tok, feat), BF16),
            pltpu.VMEM((tok, width), F32),
            pltpu.VMEM((tok, LANES), F32),
            pltpu.VMEM((tok, inner), F32),
            pltpu.SemaphoreType.DMA((5,)),
        ],
        compiler_params=PARAMS,
        name="layer_backward",
    )(which, ids, *weights, *[source for choice in choices for source, _ in choice])


def lay(blocks, size, chunks):
    lane = lax.broadcasted_iota(jnp.int32, (8, LANES), 1)
    out = [jnp.zeros((8, LANES), F32) for _ in range(chunks)]
    for i, block in enumerate(blocks):
        chunk, shift = (i * size) // LANES, (i * size) % LANES
        turned = pltpu.roll(block, shift, 1) if shift else block
        out[chunk] = jnp.where((lane >= shift) & (lane < shift + size), turned, out[chunk])
        if shift + size > LANES:
            out[chunk + 1] = jnp.where(lane < shift + size - LANES, turned, out[chunk + 1])
    return out


def cut(chunks, size, i):
    lane = lax.broadcasted_iota(jnp.int32, (8, LANES), 1)
    chunk, shift = (i * size) // LANES, (i * size) % LANES
    turn = (LANES - shift) % LANES
    block = pltpu.roll(chunks[chunk], turn, 1) if turn else chunks[chunk]
    if shift + size > LANES:
        block = jnp.where(lane < LANES - shift, block, pltpu.roll(chunks[chunk + 1], turn, 1))
    return jnp.where(lane < size, block, 0.0)


def pack_kernel(wm_ref, wo_ref, wdt_ref, cw_ref, cb_ref, gg_ref, ng_ref, out_ref, line):
    rows, width = wm_ref.shape
    feat = wo_ref.shape[1]
    blocks = wo_ref.shape[0] // rows
    out_ref[:, :width] = wm_ref[...]
    for b in range(blocks):
        out_ref[:, width + b * feat : width + (b + 1) * feat] = wo_ref[b * rows : (b + 1) * rows, :]
    last = width + blocks * feat
    out_ref[:, last:] = jnp.zeros((rows, 2 * LANES), BF16)
    out_ref[:, last : last + wdt_ref.shape[1]] = wdt_ref[...]
    line[...] = jnp.zeros(line.shape, F32)
    line[0:TAPS, : cw_ref.shape[1]] = cw_ref[...].astype(F32)
    for k, ref in enumerate((cb_ref, gg_ref, ng_ref)):
        line[TAPS + k : TAPS + k + 1, : ref.shape[1]] = ref[...].astype(F32)
    out_ref[0:16, last + LANES :] = line[...].astype(BF16)


def pack_shard(wm, wo, wdt, cw, cb, gg, ng):
    rows, width = wm.shape
    full = width + wo.shape[0] // rows * wo.shape[1] + 2 * LANES
    return pl.pallas_call(
        pack_kernel,
        out_shape=shape_of((rows, full), BF16),
        scratch_shapes=[pltpu.VMEM((16, LANES), F32)],
        compiler_params=PARAMS,
        name="pack_shard",
    )(wm, wo, wdt, cw, cb, gg, ng)


Z_CHIPS = 4


def spot(z, y, c):
    return (z * 2 + y) * 2 + c


def routed(value, move):
    pairs = []
    for z in range(Z_CHIPS):
        for y in range(2):
            for c in range(2):
                target = move(z, y, c)
                if target is not None:
                    pairs.append((spot(z, y, c), spot(*target)))
    return lax.ppermute(value, "dp", pairs)


def to_core(z, y, c):
    return z, y, 1 - c


def to_y(z, y, c):
    return z, 1 - y, c


def to_near(z, y, c):
    return z ^ 1, y, c


def to_middle(z, y, c):
    return (3 - z, y, c) if z in (1, 2) else None


def to_ends(z, y, c):
    return (z ^ 1, y, c) if z in (1, 2) else None


def from_ends(z, y, c):
    return (z ^ 1, y, c) if z in (0, 3) else None


def slot_places(z):
    return (z, z + 1 - 2 * lax.rem(z, 2), jnp.where(z < 2, 2, 1), jnp.where(z < 2, 3, 0))


def behind(value, other):
    return lax.optimization_barrier((value, other))[0]


def gather_slots(own):
    def pair(block, across):
        return jnp.concatenate([across, block], axis=0)

    near, second, own_y = lax.optimization_barrier((routed(own, to_near), routed(own, to_middle), routed(own, to_y)))
    own_pair = pair(own, own_y)
    own_core = routed(own_pair, to_core)
    last, ends, near_y = lax.optimization_barrier((routed(near, to_middle), routed(second, to_ends), routed(near, to_y)))
    second = second + ends
    near_pair = pair(near, near_y)
    near_core = routed(near_pair, to_core)
    ends, second_y = lax.optimization_barrier((routed(last, to_ends), routed(second, to_y)))
    last = last + ends
    second_pair = pair(second, second_y)
    second_core = routed(second_pair, to_core)
    last_pair = pair(last, routed(last, to_y))
    return [own_pair, near_pair, second_pair, last_pair, own_core, near_core, second_core, routed(last_pair, to_core)]


def scatter_slots(kept, sent, vectors):
    rows = kept[0].shape[0] // 2

    def met(slot, value):
        total = kept[slot].astype(F32) + value.astype(F32)
        return total[:rows].astype(BF16), total[rows:]

    def low(value):
        return value.astype(BF16)

    def summed(step):
        return vectors + lax.ppermute(vectors, "dp", [(i, i ^ step) for i in range(4 * Z_CHIPS)])

    far, last = met(3, routed(sent[3], to_core))
    others = [behind(sent[slot], far) for slot in (0, 1, 2)]
    came, over, vectors = lax.optimization_barrier((routed(far, to_y), routed(others[2], to_core), vectors))
    last = last + came.astype(F32)
    far, second = met(2, over)
    came, line, over, vectors = lax.optimization_barrier(
        (routed(far, to_y), routed(low(last), from_ends), routed(others[1], to_core), summed(1))
    )
    second, last = second + came.astype(F32), last + line.astype(F32)
    far, near = met(1, over)
    came, line, first, over, vectors = lax.optimization_barrier(
        (routed(far, to_y), routed(low(last), to_middle), routed(low(second), from_ends), routed(others[0], to_core), summed(2))
    )
    near, second = near + came.astype(F32) + line.astype(F32), second + first.astype(F32)
    far, own = met(0, over)
    vectors = summed(4)
    terms = own + routed(far, to_y).astype(F32), routed(low(second), to_middle), routed(low(near), to_near)
    return terms, summed(8)


def owners_of(where_ref):
    z, y, c = where_ref[1], where_ref[2], where_ref[3]
    return [(spot(at, 1 - y, core), spot(at, y, core)) for core in (c, 1 - c) for at in slot_places(z)]


def settle_kernel(chans, where_ref, *refs):
    pairs, (wm_ref, wo_ref, cw_ref, cb_ref, gg_ref, gin_ref, line_ref, sem) = refs[:8], refs[8:]
    rows = pairs[0].shape[0] // 2
    feat = wo_ref.shape[1]
    width = wm_ref.shape[1] - LANES
    inner = wo_ref.shape[0]
    last = width + inner
    copies = []
    for pair, owners in zip(pairs, owners_of(where_ref)):
        for half, owner in enumerate(owners):
            mine = pl.ds(half * rows, rows)
            to = pl.ds(pl.multiple_of(owner * rows, 16), rows)
            copies.append((pair.at[pl.ds(half * rows, 16), pl.ds(last + LANES, LANES)], line_ref.at[owner]))
            copies.append((pair.at[mine, pl.ds(0, width)], wm_ref.at[to, pl.ds(0, width)]))
            copies.append((pair.at[mine, pl.ds(last, LANES)], wm_ref.at[to, pl.ds(width, LANES)]))
            for b in range(inner // wm_ref.shape[0]):
                into = pl.ds(pl.multiple_of((owner * (inner // wm_ref.shape[0]) + b) * rows, 16), rows)
                copies.append((pair.at[mine, pl.ds(width + b * feat, feat)], wo_ref.at[into]))
    for source, target in copies:
        pltpu.make_async_copy(source, target, sem).start()
    for whole in (wm_ref, wo_ref, line_ref):
        pltpu.make_async_copy(whole, whole, sem).wait()
    lines = [line_ref[i].astype(F32)[0:8] for i in range(line_ref.shape[0])]
    for c, chunk in enumerate(lay(lines, chans, cw_ref.shape[1] // LANES)):
        cw_ref[:, cols(c)] = chunk[0:TAPS]
        cb_ref[:, cols(c)] = chunk[TAPS : TAPS + 1]
    for c, chunk in enumerate(lay(lines, inner // len(lines), gg_ref.shape[1] // LANES)):
        gg_ref[:, cols(c)] = chunk[TAPS + 1 : TAPS + 2]
    for c, chunk in enumerate(lay(lines, rows, gin_ref.shape[1] // LANES)):
        gin_ref[:, cols(c)] = chunk[TAPS + 2 : TAPS + 3]


def settle(where, pairs, width, chans, feat):
    rows, full = pairs[0].shape[0] // 2, pairs[0].shape[1]
    owners, inner = feat // rows, full - width - 2 * LANES
    return pl.pallas_call(
        functools.partial(settle_kernel, chans),
        in_specs=[SMEM_SPEC] + [HBM_SPEC] * 8,
        out_specs=[VMEM_SPEC] * 6,
        out_shape=(
            shape_of((feat, width + LANES), BF16),
            shape_of((inner, feat), BF16),
            shape_of((TAPS, owners * chans)),
            shape_of((1, owners * chans)),
            shape_of((1, inner)),
            shape_of((1, feat)),
        ),
        scratch_shapes=[pltpu.VMEM((owners, 16, LANES), BF16), pltpu.SemaphoreType.DMA],
        compiler_params=PARAMS,
        name="settle_weights",
    )(where, *pairs)


def weight_kernel(rows, chans, which_ref, *refs):
    sources, smalls, pairs, scratch, sems, out_ref, out_sem = refs[:20], refs[20:29], refs[29:37], refs[37:42], refs[42], refs[43], refs[44]
    tok = sources[0].shape[0]
    into = [ref.at[part * tok : (part + 1) * tok] for part in range(2) for ref in scratch]
    take(which_ref, [[(source, None) for source in sources[10 * i : 10 * i + 10]] for i in range(2)], into, sems)
    n_ref, mix_ref, gp_ref, gb_ref, gdt_ref = scratch
    feat, inner, width = n_ref.shape[1], mix_ref.shape[1], gp_ref.shape[1]
    blocks = inner // feat
    last = width + inner
    early = jnp.where(which_ref[0] == 0, 0.0, 1.0)
    sums = [one[...] + early * zero[...] + (1.0 - early) * two[...] for zero, one, two in zip(smalls[0::3], smalls[1::3], smalls[2::3])]
    pieces = [[total[:, cols(c)] for c in range(total.shape[1] // LANES)] for total in sums]
    line = lax.broadcasted_iota(jnp.int32, (8, LANES), 0)
    for i in range(feat // rows):
        block = cut(pieces[0], chans, i)
        block = jnp.where(line == TAPS + 1, jnp.broadcast_to(cut(pieces[1], blocks * rows, i)[0:1], block.shape), block)
        block = jnp.where(line == TAPS + 2, jnp.broadcast_to(cut(pieces[2], rows, i)[0:1], block.shape), block)
        out_ref[i * rows : i * rows + 16, last + LANES :] = jnp.concatenate([block, jnp.zeros_like(block)], axis=0).astype(BF16)
        out_ref[i * rows + 16 : (i + 1) * rows, last + LANES :] = jnp.zeros((rows - 16, LANES), BF16)
    taken(into, sems, 0, 5, 2, 7, 4, 9)
    turned = n_ref[...].T
    for c in range(width // 256):
        out_ref[:, cols(c, 256)] = dot_nn(turned, gp_ref[:, cols(c, 256)]).astype(BF16)
    out_ref[:, last : last + LANES] = dot_nn(turned, gdt_ref[...]).astype(BF16)
    taken(into, sems, 1, 6, 3, 8)
    gb = gb_ref[...]
    for e in range(inner // 256):
        term = dot_tn(mix_ref[:, cols(e, 256)], gb).astype(BF16)
        at = e * 256
        while at < (e + 1) * 256:
            owner, inside = at // (blocks * rows), at % (blocks * rows)
            block, row = inside // rows, inside % rows
            count = min(rows - row, (e + 1) * 256 - at)
            out_ref[owner * rows + row : owner * rows + row + count, width + block * feat : width + (block + 1) * feat] = term[
                at - e * 256 : at - e * 256 + count
            ]
            at = at + count
    for pair, owners in reversed(list(zip(pairs, owners_of(which_ref)))):
        for half, owner in enumerate(owners):
            source = out_ref.at[pl.ds(pl.multiple_of(owner * rows, 16), rows)]
            pltpu.make_async_copy(source, pair.at[pl.ds(half * rows, rows)], out_sem).start()
    pltpu.make_async_copy(out_ref, out_ref, out_sem).wait()


def weight_terms(which, one, other, smalls, rows, chans):
    tok, feat = one[0].shape
    inner, width = one[1].shape[1], one[2].shape[1]
    full = width + inner + 2 * LANES
    return pl.pallas_call(
        functools.partial(weight_kernel, rows, chans),
        in_specs=[SMEM_SPEC] + [HBM_SPEC] * 20 + [VMEM_SPEC] * 9,
        out_specs=[HBM_SPEC] * 8,
        out_shape=(shape_of((2 * rows, full), BF16),) * 8,
        scratch_shapes=[pltpu.VMEM((2 * tok, part.shape[1]), BF16) for part in one[:5]]
        + [pltpu.SemaphoreType.DMA((10,)), pltpu.VMEM((feat, full), BF16), pltpu.SemaphoreType.DMA],
        compiler_params=PARAMS,
        name="weight_gradients",
    )(which, *one, *other, *smalls)


def unpack_kernel(own_ref, second_ref, near_ref, wm_ref, wo_ref, wdt_ref, cw_ref, cb_ref, gg_ref, ng_ref):
    rows, width = wm_ref.shape
    feat = wo_ref.shape[1]
    blocks = wo_ref.shape[0] // rows
    last = width + blocks * feat

    def total(at, count):
        some = slice(0, count)
        return own_ref[some, at] + (second_ref[some, at].astype(F32) + near_ref[some, at].astype(F32))

    for c in range(width // 256):
        wm_ref[:, cols(c, 256)] = total(cols(c, 256), rows)
    for b in range(blocks):
        wo_ref[b * rows : (b + 1) * rows, :] = total(slice(width + b * feat, width + (b + 1) * feat), rows)
    wdt_ref[...] = total(slice(last, last + LANES), rows)[:, : wdt_ref.shape[1]]
    line = total(slice(last + LANES, last + 2 * LANES), 16)
    cw_ref[...] = line[0:TAPS, : cw_ref.shape[1]]
    for k, ref in enumerate((cb_ref, gg_ref, ng_ref)):
        ref[...] = line[TAPS + k : TAPS + k + 1, : ref.shape[1]]


def unpack_sums(terms, wm, wo, wdt, cw, cb, gg, ng):
    return pl.pallas_call(
        unpack_kernel,
        out_shape=tuple(shape_of(part.shape) for part in (wm, wo, wdt, cw, cb, gg, ng)),
        compiler_params=PARAMS,
        name="unpack_sums",
    )(*terms)


def small_rows(vectors, rows):
    flat = jnp.concatenate([vector.reshape(-1) for vector in vectors])
    lines = -(-flat.shape[0] // LANES)
    wide = -(-lines // rows)
    flat = jnp.pad(flat, (0, lines * LANES - flat.shape[0])).reshape(lines, LANES)
    flat = jnp.pad(flat, ((0, rows * wide - lines), (0, 0)))
    return flat.reshape(wide, rows, LANES).transpose(1, 0, 2).reshape(rows, wide * LANES)


def small_flat(block, owners):
    rows, wide = block.shape[0] // owners, block.shape[1] // LANES
    return block.reshape(owners, rows, wide, LANES).transpose(0, 2, 1, 3).reshape(owners, wide * rows * LANES)


def total_over(value, axis):
    count = lax.axis_size(axis)
    step = 1
    while step < count:
        value = value + lax.ppermute(value, axis, [(i, i ^ step) for i in range(count)])
        step = step * 2
    return value


def shards(inputs, segments, cotangent, norm_gain, w_main, w_dt, conv_weight, conv_bias, dt_bias, a_log, skip_d, gate_gain, w_out):
    first = lax.axis_index("section") == 0
    dp = lax.axis_size("dp")
    feat = inputs.shape[2]
    rows, width = w_main.shape[1:]
    heads = w_dt.shape[2]
    chans, own_inner = conv_weight.shape[2], gate_gain.shape[1]
    inner = own_inner * dp
    blocks = own_inner // rows

    owned = (w_main[0], w_out[0], w_dt[0], conv_weight[0], conv_bias, gate_gain, norm_gain)
    aligned = rows % 16 == 0 and dp == 4 * Z_CHIPS
    side = lax.axis_index("section")
    place = lax.axis_index("dp")
    where = jnp.stack([side, place // 4, place // 2 % 2, place % 2]).astype(jnp.int32)
    if aligned:
        wm, wo, cw, cb, gg, gin = settle(where, gather_slots(pack_shard(*owned)), width, chans, feat)
    else:
        small = small_rows((conv_weight[0], conv_bias[0], gate_gain[0], norm_gain[0]), rows)
        out_block = w_out[0].reshape(blocks, rows, feat).transpose(1, 0, 2).reshape(rows, inner)
        packed = jnp.concatenate([w_main[0], out_block, jnp.pad(w_dt[0], ((0, 0), (0, LANES - heads))), small], axis=1)
        whole = lax.all_gather(packed, "dp", axis=0, tiled=True)
    marks = [TAPS * chans, (TAPS + 1) * chans, (TAPS + 1) * chans + own_inner, (TAPS + 1) * chans + own_inner + rows]
    if not aligned:
        wm = jnp.concatenate([whole[:, :width], whole[:, width + inner : width + inner + LANES]], axis=1)
        wo = whole[:, width : width + inner].reshape(dp, rows, blocks, feat).transpose(0, 2, 1, 3).reshape(inner, feat)
        flat = small_flat(whole[:, width + inner + LANES :], dp).astype(F32)
        cw = flat[:, : marks[0]].reshape(dp, TAPS, chans).transpose(1, 0, 2).reshape(TAPS, dp * chans)
        cb = flat[:, marks[0] : marks[1]].reshape(1, dp * chans)
        gg = flat[:, marks[1] : marks[2]].reshape(1, inner)
        gin = flat[:, marks[2] : marks[3]].reshape(1, feat)
    hp = jnp.pad(jnp.concatenate([dt_bias, a_log], axis=0), ((0, 6), (0, LANES - heads)))
    sk = jnp.repeat(skip_d, inner // heads, axis=1)
    weights = (wm, wo, gin, cw, cb, gg, hp, sk)

    def choose(one, other):
        return jnp.where(first, one, other)

    up = [(0, 1)]
    down = [(1, 0)]
    ids = segments.astype(F32)[:, None, :]
    f0 = forward_layer(0, where, ids, weights, [(inputs, 0)])
    r0 = lax.ppermute(f0[0], "section", up)
    f1 = forward_layer(3, where, ids, weights, [(inputs, 1), (r0, None)])
    r1 = lax.ppermute(f1[0], "section", up)
    f2 = forward_layer(1, where, ids, weights, [(inputs, 1), (r1, None)])

    kept = [(part, None) for part in f1[2:5]]
    now = [[(cotangent, 0), (inputs, 1)] + kept, [(cotangent, 0), (r0, None)] + kept]
    b0 = backward_layer(0, where, ids, weights, now)
    d0 = lax.ppermute(b0[1], "section", down)
    now = [
        [(d0, None), (inputs, 0)] + [(part, None) for part in f0[2:5]],
        [(cotangent, 1), (r1, None)] + [(part, None) for part in f2[2:5]],
    ]
    b1 = backward_layer(2, where, ids, weights, now)
    d1 = lax.ppermute(b1[1], "section", down)
    b2 = backward_layer(1, where, ids, weights, [[(d1, None), (inputs, 1)] + kept])
    hidden = jnp.stack([choose(f0[0], f1[0]), choose(f1[0], f2[0])])[None]
    grad_inputs = jnp.stack([choose(b1[0], b0[0]), choose(b2[0], b1[0])])[None]
    dch, din, dgin, dhp = tuple(choose(two, zero) + one for zero, one, two in zip(b0[4:], b1[4:], b2[4:]))
    on_first = (f0[1], f0[5], b1[2], d0, b1[3]), (f1[1], f1[5], b2[2], d1, b2[3])
    on_last = (f2[1], f2[5], b1[2], cotangent[1], b1[3]), (f1[1], f1[5], b0[2], cotangent[0], b0[3])
    if aligned:
        smalls = [part[i] for i in (4, 5, 6) for part in (b0, b1, b2)]
        blocks_out = weight_terms(where, on_first[0] + on_first[1], on_last[0] + on_last[1], smalls, rows, chans)
    else:
        n, mix, gp, gb, gdt = tuple(
            jnp.concatenate([choose(on_first[0][i], on_last[0][i]), choose(on_first[1][i], on_last[1][i])], axis=0) for i in range(5)
        )
        own = [
            small_rows(
                (
                    dch[:TAPS, i * chans : (i + 1) * chans],
                    dch[TAPS, i * chans : (i + 1) * chans],
                    din[0, i * own_inner : (i + 1) * own_inner],
                    dgin[0, i * rows : (i + 1) * rows],
                ),
                rows,
            )
            for i in range(dp)
        ]
        wide = dot_tn(mix, gb).reshape(dp, blocks, rows, feat).transpose(0, 2, 1, 3).reshape(feat, inner)
        parts = [dot_tn(n, gp), wide, dot_tn(n, gdt), jnp.concatenate(own, axis=0)]
        packed_grad = jnp.concatenate([part.astype(BF16) for part in parts], axis=1)
    dskip = din[1].reshape(heads, inner // heads).sum(axis=1)
    vectors = jnp.concatenate([dhp[:2, :heads], dskip[None]], axis=0)
    if aligned:
        terms, heads_sum = scatter_slots(blocks_out[:4], blocks_out[4:], vectors)
    else:
        summed = lax.psum_scatter(packed_grad, "dp", scatter_dimension=0, tiled=True)
        heads_sum = total_over(vectors, "dp")
    if aligned:
        g_main, g_out, g_dt, g_cw, g_cb, g_gg, g_ng = unpack_sums(terms, *owned)
    else:
        summed = summed.astype(F32)
        got = small_flat(summed[:, width + inner + LANES :], 1)[0]
        g_main = summed[:, :width]
        g_out = summed[:, width : width + inner].reshape(rows, blocks, feat).transpose(1, 0, 2).reshape(own_inner, feat)
        g_dt = summed[:, width + inner : width + inner + heads]
        g_cw = got[: marks[0]].reshape(TAPS, chans)
        g_cb, g_gg, g_ng = (got[None, marks[i] : marks[i + 1]] for i in range(3))
    return (
        hidden,
        grad_inputs,
        g_ng,
        g_main[None],
        g_dt[None],
        g_cw[None],
        g_cb,
        heads_sum[0:1],
        heads_sum[1:2],
        heads_sum[2:3],
        g_gg,
        g_out[None],
    )


def solution(mesh):
    placed = (
        P(None, "dp", None),
        P(None, "dp"),
        P(None, "dp", None),
        P("section", "dp"),
        P("section", "dp", None),
        P("section", "dp", None),
        P("section", None, "dp"),
        P("section", "dp"),
        P("section", None),
        P("section", None),
        P("section", None),
        P("section", "dp"),
        P("section", "dp", None),
    )
    return jax.shard_map(
        shards,
        mesh=mesh,
        in_specs=placed,
        out_specs=(
            P("section", None, "dp", None),
            P("section", None, "dp", None),
            P("section", "dp"),
            P("section", "dp", None),
            P("section", "dp", None),
            P("section", None, "dp"),
            P("section", "dp"),
            P("section", None),
            P("section", None),
            P("section", None),
            P("section", "dp"),
            P("section", "dp", None),
        ),
        check_vma=False,
    )
```

```python
import functools

import jax
import jax.numpy as jnp
from jax import lax
from jax.experimental import pallas as pl
from jax.experimental.pallas import tpu as pltpu
from jax.sharding import PartitionSpec as P

norm_eps = 1e-05
F32 = jnp.float32
BF16 = jnp.bfloat16
LANES = 128
TAPS = 4
VMEM_BYTES = 28 * 1024 * 1024


def dot_nn(a, b):
    return lax.dot_general(a, b, (((1,), (0,)), ((), ())), preferred_element_type=F32)


def dot_nt(a, b):
    return lax.dot_general(a, b, (((1,), (1,)), ((), ())), preferred_element_type=F32)


def dot_tn(a, b):
    return lax.dot_general(a, b, (((0,), (0,)), ((), ())), preferred_element_type=F32)


def split(a):
    high = a.astype(BF16)
    return high, (a - high.astype(F32)).astype(BF16)


def exact(dot, a, b):
    ah, al = split(a)
    bh, bl = split(b)
    return dot(ah, bh) + (dot(ah, bl) + dot(al, bh))


def near(dot, a, b):
    return exact(dot, a, b)


def triangle(lower):
    rows = lax.broadcasted_iota(jnp.int32, (LANES, LANES), 0)
    cols = lax.broadcasted_iota(jnp.int32, (LANES, LANES), 1)
    return jnp.where(rows >= cols if lower else rows <= cols, 1.0, 0.0).astype(BF16)


def running(tri, a):
    high = a.astype(BF16)
    rest = a - high.astype(F32)
    mid = rest.astype(BF16)
    low = (rest - mid.astype(F32)).astype(BF16)
    return dot_nn(tri, high) + (dot_nn(tri, mid) + dot_nn(tri, low))


def sigmoid(a):
    return 1.0 / (1.0 + jnp.exp(-a))


def softplus(a):
    return jnp.maximum(a, 0.0) + jnp.log1p(jnp.exp(-jnp.abs(a)))


def cols(j, width=LANES):
    return slice(j * width, (j + 1) * width)


def token_masks(ids):
    length = ids.shape[1]
    across = jnp.broadcast_to(ids, (length, length))
    wide = across.T
    rows = lax.broadcasted_iota(jnp.int32, (length, length), 0)
    lane = lax.broadcasted_iota(jnp.int32, (length, length), 1)
    linked = jnp.where((rows >= lane) & (wide == across), 1.0, 0.0)
    sees = [None]
    for k in range(1, TAPS):
        sees.append(jnp.where((rows >= k) & (pltpu.roll(wide, k, 0) == wide), 1.0, 0.0))
    return linked, sees


def take(which_ref, choices, into, sems):
    def start(choice):
        for i, ((ref, index), target) in enumerate(zip(choice, into)):
            pltpu.make_async_copy(ref if index is None else ref.at[index], target, sems.at[i]).start()

    if len(choices) == 1:
        start(choices[0])
        return
    for number, choice in enumerate(choices):
        pl.when(which_ref[0] == number)(functools.partial(start, choice))


def taken(into, sems, *numbers):
    for i in numbers:
        pltpu.make_async_copy(into[i], into[i], sems.at[i]).wait()


def conv_taps(v, sees):
    return [v] + [sees[k] * pltpu.roll(v, k, 0) for k in range(1, TAPS)]


def conv_sum(taps, cw_ref, cb_ref, at):
    total = cb_ref[:, at] + cw_ref[TAPS - 1 : TAPS, at] * taps[0]
    for k in range(1, TAPS):
        total = total + cw_ref[TAPS - 1 - k : TAPS - k, at] * taps[k]
    return total


def pair_of(values, j):
    lane = lax.broadcasted_iota(jnp.int32, (values.shape[0], LANES), 1)
    first = jnp.broadcast_to(values[:, 2 * j : 2 * j + 1], lane.shape)
    second = jnp.broadcast_to(values[:, 2 * j + 1 : 2 * j + 2], lane.shape)
    return jnp.where(lane < LANES // 2, first, second)


def halves(values):
    lane = lax.broadcasted_iota(jnp.int32, values.shape, 1)
    low = jnp.where(lane < LANES // 2, values, 0.0)
    return jnp.concatenate([low, values - low], axis=0)


def decay(cum, cum_t, linked, h):
    spread = cum[:, h : h + 1] - cum_t[h : h + 1, :]
    return linked * jnp.exp(jnp.minimum(spread, 0.0))


def micro_of(which_ref, mode):
    return (0, 1, which_ref[0], 1 - which_ref[0])[mode]


def fwd_kernel(plan, mode, which_ref, ids_ref, wm_ref, wo_ref, gin_ref, cw_ref, cb_ref, gg_ref, hp_ref, sk_ref, *refs):
    sources, refs = refs[: len(plan)], refs[len(plan) :]
    v_ref, n_ref, p_ref, dtr_ref, y_ref, mix_ref, g_scr, u_scr, sems = refs
    take(which_ref, [((source, index),) for source, index in zip(sources, plan)], (u_scr,), sems)
    inner, width = gg_ref.shape[1], p_ref.shape[1]
    pairs = inner // LANES
    linked, sees = token_masks(ids_ref[micro_of(which_ref, mode)])
    taken((u_scr,), sems, 0)
    u = u_scr[...].astype(F32)
    r = lax.rsqrt(jnp.mean(u * u, axis=-1, keepdims=True) + norm_eps)
    n = (u * r * gin_ref[...]).astype(BF16)
    n_ref[...] = n
    for c in range(width // 256):
        p_ref[:, cols(c, 256)] = dot_nn(n, wm_ref[:, cols(c, 256)])
    dtr = dot_nn(n, wm_ref[:, width:])
    dtr_ref[...] = dtr

    def conv(j):
        total = conv_sum(conv_taps(p_ref[:, inner + j * LANES : inner + (j + 1) * LANES], sees), cw_ref, cb_ref, cols(j))
        return total * sigmoid(total)

    b_state = conv(pairs)
    c_state = conv(pairs + 1)
    cross = exact(dot_nt, c_state, b_state)
    dt = softplus(dtr + hp_ref[0:1, :])
    cum = running(triangle(True), -dt * jnp.exp(hp_ref[1:2, :]))
    cum_t = cum.T
    squares = jnp.zeros((u.shape[0], LANES), F32)
    for j in range(pairs):
        at = cols(j)
        x = conv(j)
        m = jnp.concatenate([cross * decay(cum, cum_t, linked, 2 * j), cross * decay(cum, cum_t, linked, 2 * j + 1)], axis=1)
        y = near(dot_nn, m, halves(x * pair_of(dt, j))) + sk_ref[:, at] * x
        y_ref[:, at] = y
        z = p_ref[:, at]
        g = y * (z * sigmoid(z))
        g_scr[:, at] = g
        squares = squares + g * g
    r2 = lax.rsqrt(jnp.sum(squares, axis=-1, keepdims=True) / inner + norm_eps)
    for j in range(pairs):
        at = cols(j)
        mix_ref[:, at] = (g_scr[:, at] * r2 * gg_ref[:, at]).astype(BF16)
    mixed = mix_ref[...]
    for c in range(u.shape[1] // 256):
        at = cols(c, 256)
        v_ref[:, at] = (u[:, at] + dot_nn(mixed, wo_ref[:, at])).astype(BF16)


def bwd_kernel(plan, mode, which_ref, ids_ref, wm_ref, wo_ref, gin_ref, cw_ref, cb_ref, gg_ref, hp_ref, sk_ref, *refs):
    count = 5 * len(plan)
    sources, refs = refs[:count], refs[count:]
    gi_ref, gl_ref, gp_ref, gdt_ref, dch_ref, din_ref, dgin_ref, dhp_ref = refs[:8]
    g_scr, gm_scr, gv_ref, u_ref, p_ref, dtr_ref, y_ref, sems = refs[8:]
    into = (gv_ref, u_ref, p_ref, dtr_ref, y_ref)
    choices = [list(zip(sources[5 * i : 5 * i + 5], indices)) for i, indices in enumerate(plan)]
    take(which_ref, choices, into[:1], sems)
    take(which_ref, [choice[1:] for choice in choices], into[1:], sems.at[1:])
    dch_ref[...] = jnp.zeros(dch_ref.shape, F32)
    din_ref[...] = jnp.zeros(din_ref.shape, F32)
    inner = gg_ref.shape[1]
    pairs = inner // LANES
    length = gv_ref.shape[0]
    linked, sees = token_masks(ids_ref[micro_of(which_ref, mode)])
    taken(into, sems, 0)
    gb = gv_ref[...]
    for c in range(inner // 256):
        gm_scr[:, cols(c, 256)] = dot_nt(gb, wo_ref[cols(c, 256), :])
    taken(into, sems, 1, 2, 3, 4)

    def conv(j):
        taps = conv_taps(p_ref[:, inner + j * LANES : inner + (j + 1) * LANES], sees)
        total = conv_sum(taps, cw_ref, cb_ref, cols(j))
        sig = sigmoid(total)
        return taps, total, sig

    def conv_back(j, taps, total, sig, grad):
        at = cols(j)
        ds = grad * (sig * (1.0 + total * (1.0 - sig)))
        dch_ref[TAPS : TAPS + 1, at] = jnp.sum(ds, axis=0, keepdims=True)
        dch_ref[TAPS - 1 : TAPS, at] = jnp.sum(ds * taps[0], axis=0, keepdims=True)
        dv = cw_ref[TAPS - 1 : TAPS, at] * ds
        for k in range(1, TAPS):
            row = slice(TAPS - 1 - k, TAPS - k)
            dch_ref[row, at] = jnp.sum(ds * taps[k], axis=0, keepdims=True)
            dv = dv + cw_ref[row, at] * pltpu.roll(sees[k] * ds, length - k, 0)
        gp_ref[:, inner + j * LANES : inner + (j + 1) * LANES] = dv.astype(BF16)

    squares = jnp.zeros((length, LANES), F32)
    inners = jnp.zeros((length, LANES), F32)
    for j in range(pairs):
        at = cols(j)
        z = p_ref[:, at]
        g = y_ref[:, at] * (z * sigmoid(z))
        g_scr[:, at] = g
        squares = squares + g * g
        inners = inners + gm_scr[:, at] * gg_ref[:, at] * g
    r2 = lax.rsqrt(jnp.sum(squares, axis=-1, keepdims=True) / inner + norm_eps)
    pull = r2 * r2 * r2 * (jnp.sum(inners, axis=-1, keepdims=True) / inner)

    tb, sb, gb_sig = conv(pairs)
    b_state = sb * gb_sig
    tc, sc, gc_sig = conv(pairs + 1)
    c_state = sc * gc_sig
    cross = exact(dot_nt, c_state, b_state)
    dt_arg = dtr_ref[...] + hp_ref[0:1, :]
    dt = softplus(dt_arg)
    rate = jnp.exp(hp_ref[1:2, :])
    cum = running(triangle(True), -dt * rate)
    cum_t = cum.T
    dcross = jnp.zeros((length, length), F32)
    dcum = jnp.zeros((length, LANES), F32)
    ddt = jnp.zeros((length, LANES), F32)
    dskip = jnp.zeros((8, LANES), F32)
    lane = lax.broadcasted_iota(jnp.int32, (2 * LANES, LANES), 1)
    row = lax.broadcasted_iota(jnp.int32, (2 * LANES, LANES), 0)
    half = jnp.where((row % LANES) < LANES // 2, 0, 1)
    for j in range(pairs):
        at = cols(j)
        pick = jnp.where(lane == 2 * j + half, 1.0, 0.0).astype(BF16)
        gm = gm_scr[:, at]
        g = g_scr[:, at]
        din_ref[0:1, at] = jnp.sum(gm * (g * r2), axis=0, keepdims=True)
        dg = gm * gg_ref[:, at] * r2 - g * pull
        z = p_ref[:, at]
        sig = sigmoid(z)
        y = y_ref[:, at]
        dy = dg * (z * sig)
        gp_ref[:, at] = (dg * y * (sig * (1.0 + z * (1.0 - sig)))).astype(BF16)
        taps, total, tsig = conv(j)
        x = total * tsig
        dtp = pair_of(dt, j)
        xw = x * dtp
        dy_st = halves(dy)
        l1 = decay(cum, cum_t, linked, 2 * j)
        l2 = decay(cum, cum_t, linked, 2 * j + 1)
        dm = near(dot_nt, dy_st, xw)
        dcross = dcross + dm[:length] * l1 + dm[length:] * l2
        m = jnp.concatenate([cross * l1, cross * l2], axis=0)
        dxw = near(dot_tn, m, dy_st)
        skip = sk_ref[:, at]
        lanes = jnp.broadcast_to(jnp.sum(dy * x, axis=0, keepdims=True), (8, LANES))
        dskip = dskip + dot_nn(jnp.concatenate(split(lanes), axis=1), pick)
        q = dy * (y - skip * x) - dxw * xw
        dcum = dcum + dot_nn(jnp.concatenate(split(q), axis=1), pick)
        ddt = ddt + dot_nn(jnp.concatenate(split(dxw * x), axis=1), pick)
        conv_back(j, taps, total, tsig, skip * dy + dxw * dtp)
    conv_back(pairs, tb, sb, gb_sig, exact(dot_tn, dcross, c_state))
    conv_back(pairs + 1, tc, sc, gc_sig, exact(dot_nn, dcross, b_state))
    dlog = running(triangle(False), dcum)
    draw = (ddt - rate * dlog) * sigmoid(dt_arg)
    gdt = draw.astype(BF16)
    gdt_ref[...] = gdt
    dhp_ref[0:1, :] = jnp.sum(draw, axis=0, keepdims=True)
    dhp_ref[1:2, :] = jnp.sum(dlog * (-dt * rate), axis=0, keepdims=True)
    dhp_ref[2:3, :] = dskip[0:1]
    dhp_ref[3:8, :] = jnp.zeros((5, LANES), F32)
    u = u_ref[...].astype(F32)
    gin = gin_ref[...]
    r = lax.rsqrt(jnp.mean(u * u, axis=-1, keepdims=True) + norm_eps)
    gp = gp_ref[...]
    width = gp.shape[1]
    gn = jnp.concatenate(
        [dot_nt(gp, wm_ref[cols(c, 256), :width]) + dot_nt(gdt, wm_ref[cols(c, 256), width:]) for c in range(u.shape[1] // 256)], axis=1
    )
    dgin_ref[...] = jnp.broadcast_to(jnp.sum(gn * (u * r), axis=0, keepdims=True), dgin_ref.shape)
    gng = gn * gin
    back = r * r * r * jnp.mean(gng * u, axis=-1, keepdims=True)
    grad = gb.astype(F32) + (gng * r - u * back)
    gi_ref[...] = grad
    gl_ref[...] = grad.astype(BF16)


def shape_of(shape, dtype=F32):
    return jax.ShapeDtypeStruct(shape, dtype)


VMEM_SPEC = pl.BlockSpec(memory_space=pltpu.VMEM)
HBM_SPEC = pl.BlockSpec(memory_space=pltpu.HBM)
SMEM_SPEC = pl.BlockSpec(memory_space=pltpu.SMEM)
PARAMS = pltpu.CompilerParams(vmem_limit_bytes=VMEM_BYTES)


def layer_sizes(weights):
    return weights[0].shape[0], weights[1].shape[0], weights[0].shape[1] - LANES


def forward_layer(mode, which, ids, weights, choices):
    tok = ids.shape[2]
    feat, inner, width = layer_sizes(weights)
    return pl.pallas_call(
        functools.partial(fwd_kernel, tuple(index for _, index in choices), mode),
        in_specs=[SMEM_SPEC, VMEM_SPEC] + [VMEM_SPEC] * 8 + [HBM_SPEC] * len(choices),
        out_specs=[VMEM_SPEC] * 6,
        out_shape=(
            shape_of((tok, feat), BF16),
            shape_of((tok, feat), BF16),
            shape_of((tok, width)),
            shape_of((tok, LANES)),
            shape_of((tok, inner)),
            shape_of((tok, inner), BF16),
        ),
        scratch_shapes=[
            pltpu.VMEM((tok, inner), F32),
            pltpu.VMEM((tok, feat), BF16),
            pltpu.SemaphoreType.DMA((1,)),
        ],
        compiler_params=PARAMS,
        name="layer_forward",
    )(which, ids, *weights, *[source for source, _ in choices])


def backward_layer(mode, which, ids, weights, choices):
    tok = ids.shape[2]
    feat, inner, width = layer_sizes(weights)
    return pl.pallas_call(
        functools.partial(bwd_kernel, tuple(tuple(index for _, index in choice) for choice in choices), mode),
        in_specs=[SMEM_SPEC, VMEM_SPEC] + [VMEM_SPEC] * 8 + [HBM_SPEC] * (5 * len(choices)),
        out_specs=[VMEM_SPEC] * 8,
        out_shape=(
            shape_of((tok, feat)),
            shape_of((tok, feat), BF16),
            shape_of((tok, width), BF16),
            shape_of((tok, LANES), BF16),
            shape_of((8, width - inner)),
            shape_of((8, inner)),
            shape_of((8, feat)),
            shape_of((8, LANES)),
        ),
        scratch_shapes=[
            pltpu.VMEM((tok, inner), F32),
            pltpu.VMEM((tok, inner), F32),
            pltpu.VMEM((tok, feat), BF16),
            pltpu.VMEM((tok, feat), BF16),
            pltpu.VMEM((tok, width), F32),
            pltpu.VMEM((tok, LANES), F32),
            pltpu.VMEM((tok, inner), F32),
            pltpu.SemaphoreType.DMA((5,)),
        ],
        compiler_params=PARAMS,
        name="layer_backward",
    )(which, ids, *weights, *[source for choice in choices for source, _ in choice])


def lay(blocks, size, chunks):
    lane = lax.broadcasted_iota(jnp.int32, (8, LANES), 1)
    out = [jnp.zeros((8, LANES), F32) for _ in range(chunks)]
    for i, block in enumerate(blocks):
        chunk, shift = (i * size) // LANES, (i * size) % LANES
        turned = pltpu.roll(block, shift, 1) if shift else block
        out[chunk] = jnp.where((lane >= shift) & (lane < shift + size), turned, out[chunk])
        if shift + size > LANES:
            out[chunk + 1] = jnp.where(lane < shift + size - LANES, turned, out[chunk + 1])
    return out


def cut(chunks, size, i):
    lane = lax.broadcasted_iota(jnp.int32, (8, LANES), 1)
    chunk, shift = (i * size) // LANES, (i * size) % LANES
    turn = (LANES - shift) % LANES
    block = pltpu.roll(chunks[chunk], turn, 1) if turn else chunks[chunk]
    if shift + size > LANES:
        block = jnp.where(lane < LANES - shift, block, pltpu.roll(chunks[chunk + 1], turn, 1))
    return jnp.where(lane < size, block, 0.0)


def pack_kernel(wm_ref, wo_ref, wdt_ref, cw_ref, cb_ref, gg_ref, ng_ref, out_ref, line, square):
    rows, width = wm_ref.shape
    feat = wo_ref.shape[1]
    blocks = wo_ref.shape[0] // rows
    out_ref[:, :width] = wm_ref[...]
    for b in range(blocks):
        out_ref[:, width + b * feat : width + (b + 1) * feat] = wo_ref[b * rows : (b + 1) * rows, :]
    last = width + blocks * feat
    out_ref[:, last + LANES :] = jnp.zeros((rows, LANES), BF16)
    square[...] = jnp.zeros(square.shape, F32)
    square[: wdt_ref.shape[0], :rows] = wdt_ref[...].astype(F32)
    out_ref[:, last : last + LANES] = square[...].T[:rows].astype(BF16)
    line[...] = jnp.zeros(line.shape, F32)
    line[0:TAPS, : cw_ref.shape[1]] = cw_ref[...].astype(F32)
    for k, ref in enumerate((cb_ref, gg_ref, ng_ref)):
        line[TAPS + k : TAPS + k + 1, : ref.shape[1]] = ref[...].astype(F32)
    out_ref[0:16, last + LANES :] = line[...].astype(BF16)


def pack_shard(wm, wo, wdt, cw, cb, gg, ng):
    rows, width = wm.shape
    full = width + wo.shape[0] // rows * wo.shape[1] + 2 * LANES
    return pl.pallas_call(
        pack_kernel,
        out_shape=shape_of((rows, full), BF16),
        scratch_shapes=[pltpu.VMEM((16, LANES), F32), pltpu.VMEM((LANES, LANES), F32)],
        compiler_params=pltpu.CompilerParams(vmem_limit_bytes=2 * VMEM_BYTES),
        name="pack_shard",
    )(wm, wo, wdt, cw, cb, gg, ng)


Z_CHIPS = 4


def spot(z, y, c):
    return (z * 2 + y) * 2 + c


def routed(value, move):
    pairs = []
    for z in range(Z_CHIPS):
        for y in range(2):
            for c in range(2):
                target = move(z, y, c)
                if target is not None:
                    pairs.append((spot(z, y, c), spot(*target)))
    return lax.ppermute(value, "dp", pairs)


def to_core(z, y, c):
    return z, y, 1 - c


def to_y(z, y, c):
    return z, 1 - y, c


def to_near(z, y, c):
    return z ^ 1, y, c


def to_middle(z, y, c):
    return (3 - z, y, c) if z in (1, 2) else None


def to_ends(z, y, c):
    return (z ^ 1, y, c) if z in (1, 2) else None


def from_ends(z, y, c):
    return (z ^ 1, y, c) if z in (0, 3) else None


def slot_places(z):
    return (z, z + 1 - 2 * lax.rem(z, 2), jnp.where(z < 2, 2, 1), jnp.where(z < 2, 3, 0))


def behind(value, other):
    return lax.optimization_barrier((value, other))[0]


def gather_slots(own):
    def pair(block, across):
        return jnp.concatenate([across, block], axis=0)

    near, second, own_y = lax.optimization_barrier((routed(own, to_near), routed(own, to_middle), routed(own, to_y)))
    own_pair = pair(own, own_y)
    own_core = routed(own_pair, to_core)
    last, ends, near_y = lax.optimization_barrier((routed(near, to_middle), routed(second, to_ends), routed(near, to_y)))
    second = second + ends
    near_pair = pair(near, near_y)
    near_core = routed(near_pair, to_core)
    ends, second_y = lax.optimization_barrier((routed(last, to_ends), routed(second, to_y)))
    last = last + ends
    second_pair = pair(second, second_y)
    second_core = routed(second_pair, to_core)
    last_pair = pair(last, routed(last, to_y))
    return [own_pair, near_pair, second_pair, last_pair, own_core, near_core, second_core, routed(last_pair, to_core)]


def scatter_slots(first_pair, rest, vectors):
    rows = first_pair[0].shape[0] // 2

    def met(kept, value):
        total = kept.astype(F32) + value.astype(F32)
        return total[:rows].astype(BF16), total[rows:]

    def low(value):
        return value.astype(BF16)

    def summed(step):
        return vectors + lax.ppermute(vectors, "dp", [(i, i ^ step) for i in range(4 * Z_CHIPS)])

    far, last = met(first_pair[0], routed(first_pair[1], to_core))
    kept, sent = rest(far)
    came = routed(far, to_y)
    over = [routed(block, to_core) for block in sent]
    far, second = met(kept[2], over[2])
    vectors = behind(vectors, came)
    started = came
    came, last = routed(behind(far, came), to_y), last + came.astype(F32)
    line = routed(low(last), from_ends)
    vectors = summed(1)
    far, near = met(kept[1], over[1])
    came, line, vectors = lax.optimization_barrier((came, line, vectors))
    last, second = last + line.astype(F32), second + came.astype(F32)
    came, line, ends = routed(behind(far, came), to_y), routed(low(last), to_middle), routed(low(second), from_ends)
    vectors = summed(2)
    far, own = met(kept[0], over[0])
    came, line, ends, vectors = lax.optimization_barrier((came, line, ends, vectors))
    near, second = near + came.astype(F32) + line.astype(F32), second + ends.astype(F32)
    came = routed(behind(far, came), to_y)
    near, second = routed(low(near), to_near), routed(low(second), to_middle)
    vectors = summed(4)
    vectors = summed(8)
    return (own + came.astype(F32), second, near), vectors, started


def owners_of(where_ref):
    z, y, c = where_ref[1], where_ref[2], where_ref[3]
    return [(spot(at, 1 - y, core), spot(at, y, core)) for core in (c, 1 - c) for at in slot_places(z)]


def settle_kernel(chans, where_ref, *refs):
    pairs, (wm_ref, wo_ref, cw_ref, cb_ref, gg_ref, gin_ref, line_ref, sem) = refs[:8], refs[8:]
    rows = pairs[0].shape[0] // 2
    feat = wo_ref.shape[1]
    width = wm_ref.shape[1] - LANES
    inner = wo_ref.shape[0]
    last = width + inner
    copies = []
    for pair, owners in zip(pairs, owners_of(where_ref)):
        for half, owner in enumerate(owners):
            mine = pl.ds(half * rows, rows)
            to = pl.ds(pl.multiple_of(owner * rows, 16), rows)
            copies.append((pair.at[pl.ds(half * rows, 16), pl.ds(last + LANES, LANES)], line_ref.at[owner]))
            copies.append((pair.at[mine, pl.ds(0, width)], wm_ref.at[to, pl.ds(0, width)]))
            copies.append((pair.at[mine, pl.ds(last, LANES)], wm_ref.at[to, pl.ds(width, LANES)]))
            for b in range(inner // wm_ref.shape[0]):
                into = pl.ds(pl.multiple_of((owner * (inner // wm_ref.shape[0]) + b) * rows, 16), rows)
                copies.append((pair.at[mine, pl.ds(width + b * feat, feat)], wo_ref.at[into]))
    for source, target in copies:
        pltpu.make_async_copy(source, target, sem).start()
    for whole in (wm_ref, wo_ref, line_ref):
        pltpu.make_async_copy(whole, whole, sem).wait()
    lines = [line_ref[i].astype(F32)[0:8] for i in range(line_ref.shape[0])]
    for c, chunk in enumerate(lay(lines, chans, cw_ref.shape[1] // LANES)):
        cw_ref[:, cols(c)] = chunk[0:TAPS]
        cb_ref[:, cols(c)] = chunk[TAPS : TAPS + 1]
    for c, chunk in enumerate(lay(lines, inner // len(lines), gg_ref.shape[1] // LANES)):
        gg_ref[:, cols(c)] = chunk[TAPS + 1 : TAPS + 2]
    for c, chunk in enumerate(lay(lines, rows, gin_ref.shape[1] // LANES)):
        gin_ref[:, cols(c)] = chunk[TAPS + 2 : TAPS + 3]


def settle(where, pairs, width, chans, feat):
    rows, full = pairs[0].shape[0] // 2, pairs[0].shape[1]
    owners, inner = feat // rows, full - width - 2 * LANES
    return pl.pallas_call(
        functools.partial(settle_kernel, chans),
        in_specs=[SMEM_SPEC] + [HBM_SPEC] * 8,
        out_specs=[VMEM_SPEC] * 6,
        out_shape=(
            shape_of((feat, width + LANES), BF16),
            shape_of((inner, feat), BF16),
            shape_of((TAPS, owners * chans)),
            shape_of((1, owners * chans)),
            shape_of((1, inner)),
            shape_of((1, feat)),
        ),
        scratch_shapes=[pltpu.VMEM((owners, 16, LANES), BF16), pltpu.SemaphoreType.DMA],
        compiler_params=PARAMS,
        name="settle_weights",
    )(where, *pairs)


def slot_blocks(where_ref):
    owners = owners_of(where_ref)
    return [owner for slot in range(4) for pair in (owners[slot], owners[4 + slot]) for owner in pair]


def write_slot(slot, turned, mixed, gp_ref, gb_ref, gdt_ref, line_ref, kept_ref, sent_ref, where_ref):
    rows, width, feat = kept_ref.shape[0] // 2, gp_ref.shape[1], gb_ref.shape[1]
    blocks = mixed.shape[0] // turned.shape[0]
    last = width + blocks * feat
    mine = turned[4 * slot * rows : 4 * (slot + 1) * rows, :]

    def put(at, term):
        kept_ref[:, at] = term[: 2 * rows].astype(BF16)
        sent_ref[:, at] = term[2 * rows :].astype(BF16)

    for c in range(width // 256):
        put(cols(c, 256), dot_nn(mine, gp_ref[:, cols(c, 256)]))
    put(slice(last, last + LANES), dot_nn(mine, gdt_ref[...]))
    owners = slot_blocks(where_ref)[4 * slot : 4 * slot + 4]
    for part, owner in enumerate(owners):
        ref, to = (kept_ref, sent_ref)[part // 2], part % 2 * rows
        for b in range(blocks):
            start = ((4 * slot + part) * blocks + b) * rows
            at = slice(width + b * feat, width + (b + 1) * feat)
            ref[to : to + rows, at] = dot_nn(mixed[start : start + rows, :], gb_ref[...]).astype(BF16)
        line = line_ref[owner]
        ref[to : to + 16, last + LANES :] = jnp.concatenate([line, jnp.zeros_like(line)], axis=0).astype(BF16)
        ref[to + 16 : to + rows, last + LANES :] = jnp.zeros((rows - 16, LANES), BF16)


def first_weight_kernel(rows, chans, where_ref, *refs):
    sources, smalls, outs, scratch = refs[:20], refs[20:32], refs[32:41], refs[41:]
    kept_ref, sent_ref, vec_ref, turned_ref, mixed_ref, gp_ref, gb_ref, gdt_ref, line_ref = outs
    n_ref, mix_ref, flat_ref, wide_ref, sems = scratch
    tok, feat, inner = sources[0].shape[0], n_ref.shape[1], mix_ref.shape[1]
    blocks = inner // feat
    into = [ref.at[part * tok : (part + 1) * tok] for part in range(2) for ref in (n_ref, mix_ref, gp_ref, gb_ref, gdt_ref)]
    take(where_ref, [[(source, None) for source in sources[10 * i : 10 * i + 10]] for i in range(2)], into, sems)
    early = jnp.where(where_ref[0] == 0, 0.0, 1.0)
    sums = [one[...] + early * zero[...] + (1.0 - early) * two[...] for zero, one, two in zip(smalls[0::3], smalls[1::3], smalls[2::3])]
    vec_ref[...] = sums[3]
    pieces = [[total[:, cols(c)] for c in range(total.shape[1] // LANES)] for total in sums]
    row = lax.broadcasted_iota(jnp.int32, (8, LANES), 0)
    for i in range(feat // rows):
        block = cut(pieces[0], chans, i)
        block = jnp.where(row == TAPS + 1, jnp.broadcast_to(cut(pieces[1], blocks * rows, i)[0:1], block.shape), block)
        line_ref[i] = jnp.where(row == TAPS + 2, jnp.broadcast_to(cut(pieces[2], rows, i)[0:1], block.shape), block)
    owners = slot_blocks(where_ref)
    taken(into, sems, 0, 5)
    flat_ref[...] = n_ref[...].T
    for i, owner in enumerate(owners):
        turned_ref[i * rows : (i + 1) * rows, :] = flat_ref[pl.ds(pl.multiple_of(owner * rows, 16), rows), :]
    taken(into, sems, 1, 6)
    wide_ref[...] = mix_ref[...].T
    many = blocks * rows
    for i, owner in enumerate(owners):
        mixed_ref[i * many : (i + 1) * many, :] = wide_ref[pl.ds(pl.multiple_of(owner * many, 16), many), :]
    taken(into, sems, 2, 7, 3, 8, 4, 9)
    write_slot(3, turned_ref, mixed_ref, gp_ref, gb_ref, gdt_ref, line_ref, kept_ref, sent_ref, where_ref)


def rest_weight_kernel(where_ref, turned_ref, mixed_ref, gp_ref, gb_ref, gdt_ref, line_ref, *outs):
    for slot in (2, 1, 0):
        write_slot(slot, turned_ref, mixed_ref, gp_ref, gb_ref, gdt_ref, line_ref, outs[slot], outs[3 + slot], where_ref)


def weight_terms(where, one, other, smalls, rows, chans):
    tok, feat = one[0].shape
    inner, width = one[1].shape[1], one[2].shape[1]
    pair = shape_of((2 * rows, width + inner + 2 * LANES), BF16)
    shared = (
        shape_of((feat, 2 * tok), BF16),
        shape_of((inner, 2 * tok), BF16),
        shape_of((2 * tok, width), BF16),
        shape_of((2 * tok, feat), BF16),
        shape_of((2 * tok, LANES), BF16),
        shape_of((feat // rows, 8, LANES)),
    )
    kept, sent, vectors, *common = pl.pallas_call(
        functools.partial(first_weight_kernel, rows, chans),
        in_specs=[SMEM_SPEC] + [HBM_SPEC] * 20 + [VMEM_SPEC] * 12,
        out_specs=[VMEM_SPEC] * 9,
        out_shape=(pair, pair, shape_of((8, LANES))) + shared,
        scratch_shapes=[
            pltpu.VMEM((2 * tok, feat), BF16),
            pltpu.VMEM((2 * tok, inner), BF16),
            pltpu.VMEM((feat, 2 * tok), BF16),
            pltpu.VMEM((inner, 2 * tok), BF16),
            pltpu.SemaphoreType.DMA((10,)),
        ],
        compiler_params=PARAMS,
        name="weight_gradients_first",
    )(where, *one, *other, *smalls)

    def rest(after):
        outs = pl.pallas_call(
            rest_weight_kernel,
            in_specs=[SMEM_SPEC] + [VMEM_SPEC] * 6,
            out_specs=[VMEM_SPEC] * 6,
            out_shape=(pair,) * 6,
            compiler_params=PARAMS,
            name="weight_gradients_rest",
        )(where, behind(common[0], after), *common[1:])
        return outs[:3], outs[3:]

    return (kept, sent), vectors, rest


def unpack_kernel(own_ref, second_ref, near_ref, wm_ref, wo_ref, wdt_ref, cw_ref, cb_ref, gg_ref, ng_ref, square):
    rows, width = wm_ref.shape
    feat = wo_ref.shape[1]
    blocks = wo_ref.shape[0] // rows
    last = width + blocks * feat

    def total(at, count):
        some = slice(0, count)
        return own_ref[some, at] + (second_ref[some, at].astype(F32) + near_ref[some, at].astype(F32))

    for c in range(width // 256):
        wm_ref[:, cols(c, 256)] = total(cols(c, 256), rows)
    for b in range(blocks):
        wo_ref[b * rows : (b + 1) * rows, :] = total(slice(width + b * feat, width + (b + 1) * feat), rows)
    square[...] = jnp.zeros(square.shape, F32)
    square[:rows, :] = total(slice(last, last + LANES), rows)
    wdt_ref[...] = square[...].T[: wdt_ref.shape[0], :rows]
    line = total(slice(last + LANES, last + 2 * LANES), 16)
    cw_ref[...] = line[0:TAPS, : cw_ref.shape[1]]
    for k, ref in enumerate((cb_ref, gg_ref, ng_ref)):
        ref[...] = line[TAPS + k : TAPS + k + 1, : ref.shape[1]]


def unpack_sums(terms, wm, wo, wdt, cw, cb, gg, ng):
    return pl.pallas_call(
        unpack_kernel,
        out_shape=tuple(shape_of(part.shape) for part in (wm, wo, wdt, cw, cb, gg, ng)),
        scratch_shapes=[pltpu.VMEM((LANES, LANES), F32)],
        compiler_params=PARAMS,
        name="unpack_sums",
    )(*terms)


def small_rows(vectors, rows):
    flat = jnp.concatenate([vector.reshape(-1) for vector in vectors])
    lines = -(-flat.shape[0] // LANES)
    wide = -(-lines // rows)
    flat = jnp.pad(flat, (0, lines * LANES - flat.shape[0])).reshape(lines, LANES)
    flat = jnp.pad(flat, ((0, rows * wide - lines), (0, 0)))
    return flat.reshape(wide, rows, LANES).transpose(1, 0, 2).reshape(rows, wide * LANES)


def small_flat(block, owners):
    rows, wide = block.shape[0] // owners, block.shape[1] // LANES
    return block.reshape(owners, rows, wide, LANES).transpose(0, 2, 1, 3).reshape(owners, wide * rows * LANES)


def total_over(value, axis):
    count = lax.axis_size(axis)
    step = 1
    while step < count:
        value = value + lax.ppermute(value, axis, [(i, i ^ step) for i in range(count)])
        step = step * 2
    return value


def shards(inputs, segments, cotangent, norm_gain, w_main, w_dt, conv_weight, conv_bias, dt_bias, a_log, skip_d, gate_gain, w_out):
    first = lax.axis_index("section") == 0
    dp = lax.axis_size("dp")
    feat = inputs.shape[2]
    rows, width = w_main.shape[1:]
    heads = w_dt.shape[2]
    chans, own_inner = conv_weight.shape[2], gate_gain.shape[1]
    inner = own_inner * dp
    blocks = own_inner // rows

    owned = (w_main[0], w_out[0], jnp.swapaxes(w_dt[0], 0, 1), conv_weight[0], conv_bias, gate_gain, norm_gain)
    aligned = rows % 16 == 0 and dp == 4 * Z_CHIPS
    side = lax.axis_index("section")
    place = lax.axis_index("dp")
    where = jnp.stack([side, place // 4, place // 2 % 2, place % 2]).astype(jnp.int32)
    if aligned:
        wm, wo, cw, cb, gg, gin = settle(where, gather_slots(pack_shard(*owned)), width, chans, feat)
    else:
        small = small_rows((conv_weight[0], conv_bias[0], gate_gain[0], norm_gain[0]), rows)
        out_block = w_out[0].reshape(blocks, rows, feat).transpose(1, 0, 2).reshape(rows, inner)
        packed = jnp.concatenate([w_main[0], out_block, jnp.pad(w_dt[0], ((0, 0), (0, LANES - heads))), small], axis=1)
        whole = lax.all_gather(packed, "dp", axis=0, tiled=True)
    marks = [TAPS * chans, (TAPS + 1) * chans, (TAPS + 1) * chans + own_inner, (TAPS + 1) * chans + own_inner + rows]
    if not aligned:
        wm = jnp.concatenate([whole[:, :width], whole[:, width + inner : width + inner + LANES]], axis=1)
        wo = whole[:, width : width + inner].reshape(dp, rows, blocks, feat).transpose(0, 2, 1, 3).reshape(inner, feat)
        flat = small_flat(whole[:, width + inner + LANES :], dp).astype(F32)
        cw = flat[:, : marks[0]].reshape(dp, TAPS, chans).transpose(1, 0, 2).reshape(TAPS, dp * chans)
        cb = flat[:, marks[0] : marks[1]].reshape(1, dp * chans)
        gg = flat[:, marks[1] : marks[2]].reshape(1, inner)
        gin = flat[:, marks[2] : marks[3]].reshape(1, feat)
    hp = jnp.pad(jnp.concatenate([dt_bias, a_log], axis=0), ((0, 6), (0, LANES - heads)))
    sk = jnp.repeat(skip_d, inner // heads, axis=1)
    weights = (wm, wo, gin, cw, cb, gg, hp, sk)

    def choose(one, other):
        return jnp.where(first, one, other)

    up = [(0, 1)]
    down = [(1, 0)]
    ids = segments.astype(F32)[:, None, :]
    f0 = forward_layer(0, where, ids, weights, [(inputs, 0)])
    r0 = lax.ppermute(f0[0], "section", up)
    f1 = forward_layer(3, where, ids, weights, [(inputs, 1), (r0, None)])
    r1 = lax.ppermute(f1[0], "section", up)
    f2 = forward_layer(1, where, ids, weights, [(inputs, 1), (r1, None)])

    kept = [(part, None) for part in f1[2:5]]
    now = [[(cotangent, 0), (inputs, 1)] + kept, [(cotangent, 0), (r0, None)] + kept]
    b0 = backward_layer(0, where, ids, weights, now)
    d0 = lax.ppermute(b0[1], "section", down)
    now = [
        [(d0, None), (inputs, 0)] + [(part, None) for part in f0[2:5]],
        [(cotangent, 1), (r1, None)] + [(part, None) for part in f2[2:5]],
    ]
    b1 = backward_layer(2, where, ids, weights, now)
    d1 = lax.ppermute(b1[1], "section", down)
    b2 = backward_layer(1, where, ids, weights, [[(d1, None), (inputs, 1)] + kept])
    dch, din, dgin, dhp = tuple(choose(two, zero) + one for zero, one, two in zip(b0[4:], b1[4:], b2[4:]))
    on_first = (f0[1], f0[5], b1[2], d0, b1[3]), (f1[1], f1[5], b2[2], d1, b2[3])
    on_last = (f2[1], f2[5], b1[2], cotangent[1], b1[3]), (f1[1], f1[5], b0[2], cotangent[0], b0[3])
    if aligned:
        smalls = [part[i] for i in (4, 5, 6, 7) for part in (b0, b1, b2)]
        first_pair, vectors, rest = weight_terms(where, on_first[0] + on_first[1], on_last[0] + on_last[1], smalls, rows, chans)
    else:
        n, mix, gp, gb, gdt = tuple(
            jnp.concatenate([choose(on_first[0][i], on_last[0][i]), choose(on_first[1][i], on_last[1][i])], axis=0) for i in range(5)
        )
        own = [
            small_rows(
                (
                    dch[:TAPS, i * chans : (i + 1) * chans],
                    dch[TAPS, i * chans : (i + 1) * chans],
                    din[0, i * own_inner : (i + 1) * own_inner],
                    dgin[0, i * rows : (i + 1) * rows],
                ),
                rows,
            )
            for i in range(dp)
        ]
        wide = dot_tn(mix, gb).reshape(dp, blocks, rows, feat).transpose(0, 2, 1, 3).reshape(feat, inner)
        parts = [dot_tn(n, gp), wide, dot_tn(n, gdt), jnp.concatenate(own, axis=0)]
        packed_grad = jnp.concatenate([part.astype(BF16) for part in parts], axis=1)
    if aligned:
        terms, vectors, started = scatter_slots(first_pair, rest, vectors)
        heads_sum = vectors[:, :heads]
    else:
        summed = lax.psum_scatter(packed_grad, "dp", scatter_dimension=0, tiled=True)
        heads_sum = total_over(dhp[:3, :heads], "dp")
        started = summed
    if aligned:
        g_main, g_out, g_dt, g_cw, g_cb, g_gg, g_ng = unpack_sums(terms, *owned)
        g_dt = jnp.swapaxes(g_dt, 0, 1)
    else:
        summed = summed.astype(F32)
        got = small_flat(summed[:, width + inner + LANES :], 1)[0]
        g_main = summed[:, :width]
        g_out = summed[:, width : width + inner].reshape(rows, blocks, feat).transpose(1, 0, 2).reshape(own_inner, feat)
        g_dt = summed[:, width + inner : width + inner + heads]
        g_cw = got[: marks[0]].reshape(TAPS, chans)
        g_cb, g_gg, g_ng = (got[None, marks[i] : marks[i + 1]] for i in range(3))
    outs = [part[0] for part in (f0, f1, f2, b0, b1, b2)]
    outs = lax.optimization_barrier((*outs, started))
    hidden = jnp.stack([choose(outs[0], outs[1]), choose(outs[1], outs[2])])[None]
    grad_inputs = jnp.stack([choose(outs[4], outs[3]), choose(outs[5], outs[4])])[None]
    return (
        hidden,
        grad_inputs,
        g_ng,
        g_main[None],
        g_dt[None],
        g_cw[None],
        g_cb,
        heads_sum[0:1],
        heads_sum[1:2],
        heads_sum[2:3],
        g_gg,
        g_out[None],
    )


def solution(mesh):
    placed = (
        P(None, "dp", None),
        P(None, "dp"),
        P(None, "dp", None),
        P("section", "dp"),
        P("section", "dp", None),
        P("section", "dp", None),
        P("section", None, "dp"),
        P("section", "dp"),
        P("section", None),
        P("section", None),
        P("section", None),
        P("section", "dp"),
        P("section", "dp", None),
    )
    return jax.shard_map(
        shards,
        mesh=mesh,
        in_specs=placed,
        out_specs=(
            P("section", None, "dp", None),
            P("section", None, "dp", None),
            P("section", "dp"),
            P("section", "dp", None),
            P("section", "dp", None),
            P("section", None, "dp"),
            P("section", "dp"),
            P("section", None),
            P("section", None),
            P("section", None),
            P("section", "dp"),
            P("section", "dp", None),
        ),
        check_vma=False,
    )
```

```python
import functools

import jax
import jax.numpy as jnp
from jax import lax
from jax.experimental import pallas as pl
from jax.experimental.pallas import tpu as pltpu
from jax.sharding import PartitionSpec as P

norm_eps = 1e-05
F32 = jnp.float32
BF16 = jnp.bfloat16
LANES = 128
TAPS = 4
VMEM_BYTES = 28 * 1024 * 1024


def dot_nn(a, b):
    return lax.dot_general(a, b, (((1,), (0,)), ((), ())), preferred_element_type=F32)


def dot_nt(a, b):
    return lax.dot_general(a, b, (((1,), (1,)), ((), ())), preferred_element_type=F32)


def dot_tn(a, b):
    return lax.dot_general(a, b, (((0,), (0,)), ((), ())), preferred_element_type=F32)


def split(a):
    high = a.astype(BF16)
    return high, (a - high.astype(F32)).astype(BF16)


def exact(dot, a, b):
    ah, al = split(a)
    bh, bl = split(b)
    return dot(ah, bh) + (dot(ah, bl) + dot(al, bh))


def near(dot, a, b):
    return exact(dot, a, b)


def triangle(lower):
    rows = lax.broadcasted_iota(jnp.int32, (LANES, LANES), 0)
    cols = lax.broadcasted_iota(jnp.int32, (LANES, LANES), 1)
    return jnp.where(rows >= cols if lower else rows <= cols, 1.0, 0.0).astype(BF16)


def running(tri, a):
    high = a.astype(BF16)
    rest = a - high.astype(F32)
    mid = rest.astype(BF16)
    low = (rest - mid.astype(F32)).astype(BF16)
    return dot_nn(tri, high) + (dot_nn(tri, mid) + dot_nn(tri, low))


def sigmoid(a):
    return 0.5 * jnp.tanh(0.5 * a) + 0.5


def softplus(a):
    return jnp.maximum(a, 0.0) + jnp.log1p(jnp.exp(-jnp.abs(a)))


def cols(j, width=LANES):
    return slice(j * width, (j + 1) * width)


def token_masks(ids):
    length = ids.shape[1]
    across = jnp.broadcast_to(ids, (length, length))
    wide = across.T
    rows = lax.broadcasted_iota(jnp.int32, (length, length), 0)
    lane = lax.broadcasted_iota(jnp.int32, (length, length), 1)
    linked = jnp.where((rows >= lane) & (wide == across), 1.0, 0.0)
    sees = [None]
    for k in range(1, TAPS):
        sees.append(jnp.where((rows >= k) & (pltpu.roll(wide, k, 0) == wide), 1.0, 0.0))
    return linked, sees


def take(which_ref, choices, into, sems):
    def start(choice):
        for i, ((ref, index), target) in enumerate(zip(choice, into)):
            pltpu.make_async_copy(ref if index is None else ref.at[index], target, sems.at[i]).start()

    if len(choices) == 1:
        start(choices[0])
        return
    for number, choice in enumerate(choices):
        pl.when(which_ref[0] == number)(functools.partial(start, choice))


def taken(into, sems, *numbers):
    for i in numbers:
        pltpu.make_async_copy(into[i], into[i], sems.at[i]).wait()


def conv_taps(v, sees):
    return [v] + [sees[k] * pltpu.roll(v, k, 0) for k in range(1, TAPS)]


def conv_sum(taps, cw_ref, cb_ref, at):
    total = cb_ref[:, at] + cw_ref[TAPS - 1 : TAPS, at] * taps[0]
    for k in range(1, TAPS):
        total = total + cw_ref[TAPS - 1 - k : TAPS - k, at] * taps[k]
    return total


def pair_of(values, j):
    lane = lax.broadcasted_iota(jnp.int32, (values.shape[0], LANES), 1)
    first = jnp.broadcast_to(values[:, 2 * j : 2 * j + 1], lane.shape)
    second = jnp.broadcast_to(values[:, 2 * j + 1 : 2 * j + 2], lane.shape)
    return jnp.where(lane < LANES // 2, first, second)


def halves(values):
    lane = lax.broadcasted_iota(jnp.int32, values.shape, 1)
    low = jnp.where(lane < LANES // 2, values, 0.0)
    return jnp.concatenate([low, values - low], axis=0)


def decay(cum, cum_t, linked, h):
    spread = cum[:, h : h + 1] - cum_t[h : h + 1, :]
    return linked * jnp.exp(jnp.minimum(spread, 0.0))


def micro_of(which_ref, mode):
    return (0, 1, which_ref[0], 1 - which_ref[0])[mode]


def held(which_ref, options, indices):
    refs = [ref if index is None else ref.at[index] for ref, index in zip(options, indices)]

    def read(at=slice(None)):
        values = [ref[:, at] for ref in refs]
        return values[0] if len(values) == 1 else jnp.where(which_ref[0] == 0, values[0], values[1])

    return read


KEPT = 8


def fwd_kernel(plan, mode, which_ref, ids_ref, wm_ref, wo_ref, gin_ref, cw_ref, cb_ref, gg_ref, hp_ref, sk_ref, *refs):
    sources, refs = refs[: len(plan)], refs[len(plan) :]
    v_ref, n_ref, p_ref, dtr_ref, y_ref, mix_ref, total_ref, g_ref, r2_ref = refs
    inner, width = gg_ref.shape[1], p_ref.shape[1]
    pairs = inner // LANES
    linked, sees = token_masks(ids_ref[micro_of(which_ref, mode)])
    u = held(which_ref, sources, plan)().astype(F32)
    r = lax.rsqrt(jnp.mean(u * u, axis=-1, keepdims=True) + norm_eps)
    n = (u * r * gin_ref[...]).astype(BF16)
    n_ref[...] = n
    for c in range(width // 256):
        p_ref[:, cols(c, 256)] = dot_nn(n, wm_ref[:, cols(c, 256)])
    dtr = dot_nn(n, wm_ref[:, width:])
    dtr_ref[...] = dtr

    def conv(j):
        total = conv_sum(conv_taps(p_ref[:, inner + j * LANES : inner + (j + 1) * LANES], sees), cw_ref, cb_ref, cols(j))
        total_ref[:, cols(j)] = total
        return total * sigmoid(total)

    b_state = conv(pairs)
    c_state = conv(pairs + 1)
    cross = exact(dot_nt, c_state, b_state)
    dt = softplus(dtr + hp_ref[0:1, :])
    cum = running(triangle(True), -dt * jnp.exp(hp_ref[1:2, :]))
    cum_t = cum.T
    squares = jnp.zeros((u.shape[0], LANES), F32)
    for j in range(pairs):
        at = cols(j)
        x = conv(j)
        m = jnp.concatenate([cross * decay(cum, cum_t, linked, 2 * j), cross * decay(cum, cum_t, linked, 2 * j + 1)], axis=1)
        y = near(dot_nn, m, halves(x * pair_of(dt, j))) + sk_ref[:, at] * x
        y_ref[:, at] = y
        z = p_ref[:, at]
        g = y * (z * sigmoid(z))
        g_ref[:, at] = g
        squares = squares + g * g
    r2 = lax.rsqrt(jnp.sum(squares, axis=-1, keepdims=True) / inner + norm_eps)
    for j in range(pairs):
        at = cols(j)
        mix_ref[:, at] = (g_ref[:, at] * r2 * gg_ref[:, at]).astype(BF16)
    r2_ref[...] = jnp.broadcast_to(r2, r2_ref.shape)
    mixed = mix_ref[...]
    for c in range(u.shape[1] // 256):
        at = cols(c, 256)
        v_ref[:, at] = (u[:, at] + dot_nn(mixed, wo_ref[:, at])).astype(BF16)


def bwd_kernel(plan, mode, which_ref, ids_ref, wm_ref, wo_ref, gin_ref, cw_ref, cb_ref, gg_ref, hp_ref, sk_ref, *refs):
    count = KEPT * len(plan)
    sources, refs = refs[:count], refs[count:]
    gi_ref, gl_ref, gp_ref, gdt_ref, dch_ref, din_ref, dgin_ref, dhp_ref, gm_scr = refs
    gv, u_low, p, dtr, y_kept, totals, g_kept, r2_kept = [
        held(which_ref, [sources[KEPT * k + i] for k in range(len(plan))], [indices[i] for indices in plan]) for i in range(KEPT)
    ]
    dch_ref[...] = jnp.zeros(dch_ref.shape, F32)
    din_ref[...] = jnp.zeros(din_ref.shape, F32)
    inner = gg_ref.shape[1]
    pairs = inner // LANES
    length = gm_scr.shape[0]
    linked, sees = token_masks(ids_ref[micro_of(which_ref, mode)])
    gb = gv()
    inners = jnp.zeros((length, 256), F32)
    for c in range(inner // 256):
        at = cols(c, 256)
        gm = dot_nt(gb, wo_ref[at, :])
        gm_scr[:, at] = gm
        inners = inners + gm * gg_ref[:, at] * g_kept(at)
    r2 = r2_kept()[:, 0:1]
    pull = r2 * r2 * r2 * (jnp.sum(inners, axis=-1, keepdims=True) / inner)

    def conv(j):
        total = totals(cols(j))
        return total, sigmoid(total)

    def conv_back(j, total, sig, grad):
        at = cols(j)
        v = p(slice(inner + j * LANES, inner + (j + 1) * LANES))
        ds = grad * (sig * (1.0 + total * (1.0 - sig)))
        dch_ref[TAPS : TAPS + 1, at] = jnp.sum(ds, axis=0, keepdims=True)
        dch_ref[TAPS - 1 : TAPS, at] = jnp.sum(ds * v, axis=0, keepdims=True)
        dv = cw_ref[TAPS - 1 : TAPS, at] * ds
        for k in range(1, TAPS):
            row = slice(TAPS - 1 - k, TAPS - k)
            moved = pltpu.roll(sees[k] * ds, length - k, 0)
            dch_ref[row, at] = jnp.sum(moved * v, axis=0, keepdims=True)
            dv = dv + cw_ref[row, at] * moved
        gp_ref[:, inner + j * LANES : inner + (j + 1) * LANES] = dv.astype(BF16)

    sb, gb_sig = conv(pairs)
    b_state = sb * gb_sig
    sc, gc_sig = conv(pairs + 1)
    c_state = sc * gc_sig
    cross = exact(dot_nt, c_state, b_state)
    dt_arg = dtr() + hp_ref[0:1, :]
    dt = softplus(dt_arg)
    rate = jnp.exp(hp_ref[1:2, :])
    cum = running(triangle(True), -dt * rate)
    cum_t = cum.T
    dcross = jnp.zeros((length, length), F32)
    dcum = jnp.zeros((length, LANES), F32)
    ddt = jnp.zeros((length, LANES), F32)
    dskip = jnp.zeros((8, LANES), F32)
    lane = lax.broadcasted_iota(jnp.int32, (2 * LANES, LANES), 1)
    row = lax.broadcasted_iota(jnp.int32, (2 * LANES, LANES), 0)
    half = jnp.where((row % LANES) < LANES // 2, 0, 1)
    for j in range(pairs):
        at = cols(j)
        pick = jnp.where(lane == 2 * j + half, 1.0, 0.0).astype(BF16)
        gm = gm_scr[:, at]
        g = g_kept(at)
        din_ref[0:1, at] = jnp.sum(gm * (g * r2), axis=0, keepdims=True)
        dg = gm * gg_ref[:, at] * r2 - g * pull
        z = p(at)
        sig = sigmoid(z)
        y = y_kept(at)
        dy = dg * (z * sig)
        gp_ref[:, at] = (dg * y * (sig * (1.0 + z * (1.0 - sig)))).astype(BF16)
        total, tsig = conv(j)
        x = total * tsig
        dtp = pair_of(dt, j)
        xw = x * dtp
        dy_st = halves(dy)
        l1 = decay(cum, cum_t, linked, 2 * j)
        l2 = decay(cum, cum_t, linked, 2 * j + 1)
        dm = near(dot_nt, dy_st, xw)
        dcross = dcross + dm[:length] * l1 + dm[length:] * l2
        m = jnp.concatenate([cross * l1, cross * l2], axis=0)
        dxw = near(dot_tn, m, dy_st)
        skip = sk_ref[:, at]
        lanes = jnp.broadcast_to(jnp.sum(dy * x, axis=0, keepdims=True), (8, LANES))
        dskip = dskip + dot_nn(jnp.concatenate(split(lanes), axis=1), pick)
        q = dy * (y - skip * x) - dxw * xw
        dcum = dcum + dot_nn(jnp.concatenate(split(q), axis=1), pick)
        ddt = ddt + dot_nn(jnp.concatenate(split(dxw * x), axis=1), pick)
        conv_back(j, total, tsig, skip * dy + dxw * dtp)
    conv_back(pairs, sb, gb_sig, exact(dot_tn, dcross, c_state))
    conv_back(pairs + 1, sc, gc_sig, exact(dot_nn, dcross, b_state))
    dlog = running(triangle(False), dcum)
    draw = (ddt - rate * dlog) * sigmoid(dt_arg)
    gdt = draw.astype(BF16)
    gdt_ref[...] = gdt
    dhp_ref[0:1, :] = jnp.sum(draw, axis=0, keepdims=True)
    dhp_ref[1:2, :] = jnp.sum(dlog * (-dt * rate), axis=0, keepdims=True)
    dhp_ref[2:3, :] = dskip[0:1]
    dhp_ref[3:8, :] = jnp.zeros((5, LANES), F32)
    u = u_low().astype(F32)
    gin = gin_ref[...]
    r = lax.rsqrt(jnp.mean(u * u, axis=-1, keepdims=True) + norm_eps)
    gp = gp_ref[...]
    width = gp.shape[1]
    gn = jnp.concatenate(
        [dot_nt(gp, wm_ref[cols(c, 256), :width]) + dot_nt(gdt, wm_ref[cols(c, 256), width:]) for c in range(u.shape[1] // 256)], axis=1
    )
    dgin_ref[...] = jnp.broadcast_to(jnp.sum(gn * (u * r), axis=0, keepdims=True), dgin_ref.shape)
    gng = gn * gin
    back = r * r * r * jnp.mean(gng * u, axis=-1, keepdims=True)
    grad = gb.astype(F32) + (gng * r - u * back)
    gi_ref[...] = grad
    gl_ref[...] = grad.astype(BF16)


def shape_of(shape, dtype=F32):
    return jax.ShapeDtypeStruct(shape, dtype)


VMEM_SPEC = pl.BlockSpec(memory_space=pltpu.VMEM)
HBM_SPEC = pl.BlockSpec(memory_space=pltpu.HBM)
SMEM_SPEC = pl.BlockSpec(memory_space=pltpu.SMEM)
PARAMS = pltpu.CompilerParams(vmem_limit_bytes=VMEM_BYTES)


def layer_sizes(weights):
    return weights[0].shape[0], weights[1].shape[0], weights[0].shape[1] - LANES


def forward_layer(mode, which, ids, weights, choices):
    tok = ids.shape[2]
    feat, inner, width = layer_sizes(weights)
    return pl.pallas_call(
        functools.partial(fwd_kernel, tuple(index for _, index in choices), mode),
        in_specs=[SMEM_SPEC] + [VMEM_SPEC] * (9 + len(choices)),
        out_specs=[VMEM_SPEC] * 9,
        out_shape=(
            shape_of((tok, feat), BF16),
            shape_of((tok, feat), BF16),
            shape_of((tok, width)),
            shape_of((tok, LANES)),
            shape_of((tok, inner)),
            shape_of((tok, inner), BF16),
            shape_of((tok, width - inner)),
            shape_of((tok, inner)),
            shape_of((tok, LANES)),
        ),
        compiler_params=PARAMS,
        name="layer_forward",
    )(which, ids, *weights, *[source for source, _ in choices])


def backward_layer(mode, which, ids, weights, choices):
    tok = ids.shape[2]
    feat, inner, width = layer_sizes(weights)
    return pl.pallas_call(
        functools.partial(bwd_kernel, tuple(tuple(index for _, index in choice) for choice in choices), mode),
        in_specs=[SMEM_SPEC] + [VMEM_SPEC] * (9 + KEPT * len(choices)),
        out_specs=[VMEM_SPEC] * 8,
        out_shape=(
            shape_of((tok, feat)),
            shape_of((tok, feat), BF16),
            shape_of((tok, width), BF16),
            shape_of((tok, LANES), BF16),
            shape_of((8, width - inner)),
            shape_of((8, inner)),
            shape_of((8, feat)),
            shape_of((8, LANES)),
        ),
        scratch_shapes=[pltpu.VMEM((tok, inner), F32)],
        compiler_params=PARAMS,
        name="layer_backward",
    )(which, ids, *weights, *[source for choice in choices for source, _ in choice])


def lay(blocks, size, chunks):
    lane = lax.broadcasted_iota(jnp.int32, (8, LANES), 1)
    out = [jnp.zeros((8, LANES), F32) for _ in range(chunks)]
    for i, block in enumerate(blocks):
        chunk, shift = (i * size) // LANES, (i * size) % LANES
        turned = pltpu.roll(block, shift, 1) if shift else block
        out[chunk] = jnp.where((lane >= shift) & (lane < shift + size), turned, out[chunk])
        if shift + size > LANES:
            out[chunk + 1] = jnp.where(lane < shift + size - LANES, turned, out[chunk + 1])
    return out


def cut(chunks, size, i):
    lane = lax.broadcasted_iota(jnp.int32, (8, LANES), 1)
    chunk, shift = (i * size) // LANES, (i * size) % LANES
    turn = (LANES - shift) % LANES
    block = pltpu.roll(chunks[chunk], turn, 1) if turn else chunks[chunk]
    if shift + size > LANES:
        block = jnp.where(lane < LANES - shift, block, pltpu.roll(chunks[chunk + 1], turn, 1))
    return jnp.where(lane < size, block, 0.0)


def pack_kernel(wm_ref, wo_ref, wdt_ref, cw_ref, cb_ref, gg_ref, ng_ref, out_ref, line, square):
    rows, width = wm_ref.shape
    feat = wo_ref.shape[1]
    blocks = wo_ref.shape[0] // rows
    out_ref[:, :width] = wm_ref[...]
    for b in range(blocks):
        out_ref[:, width + b * feat : width + (b + 1) * feat] = wo_ref[b * rows : (b + 1) * rows, :]
    last = width + blocks * feat
    out_ref[:, last + LANES :] = jnp.zeros((rows, LANES), BF16)
    square[...] = jnp.zeros(square.shape, F32)
    square[: wdt_ref.shape[0], :rows] = wdt_ref[...].astype(F32)
    out_ref[:, last : last + LANES] = square[...].T[:rows].astype(BF16)
    line[...] = jnp.zeros(line.shape, F32)
    line[0:TAPS, : cw_ref.shape[1]] = cw_ref[...].astype(F32)
    for k, ref in enumerate((cb_ref, gg_ref, ng_ref)):
        line[TAPS + k : TAPS + k + 1, : ref.shape[1]] = ref[...].astype(F32)
    out_ref[0:16, last + LANES :] = line[...].astype(BF16)


def pack_shard(wm, wo, wdt, cw, cb, gg, ng):
    rows, width = wm.shape
    full = width + wo.shape[0] // rows * wo.shape[1] + 2 * LANES
    return pl.pallas_call(
        pack_kernel,
        out_shape=shape_of((rows, full), BF16),
        scratch_shapes=[pltpu.VMEM((16, LANES), F32), pltpu.VMEM((LANES, LANES), F32)],
        compiler_params=pltpu.CompilerParams(vmem_limit_bytes=2 * VMEM_BYTES),
        name="pack_shard",
    )(wm, wo, wdt, cw, cb, gg, ng)


Z_CHIPS = 4


def spot(z, y, c):
    return (z * 2 + y) * 2 + c


def routed(value, move):
    pairs = []
    for z in range(Z_CHIPS):
        for y in range(2):
            for c in range(2):
                target = move(z, y, c)
                if target is not None:
                    pairs.append((spot(z, y, c), spot(*target)))
    return lax.ppermute(value, "dp", pairs)


def to_core(z, y, c):
    return z, y, 1 - c


def to_y(z, y, c):
    return z, 1 - y, c


def to_near(z, y, c):
    return z ^ 1, y, c


def to_middle(z, y, c):
    return (3 - z, y, c) if z in (1, 2) else None


def to_ends(z, y, c):
    return (z ^ 1, y, c) if z in (1, 2) else None


def from_ends(z, y, c):
    return (z ^ 1, y, c) if z in (0, 3) else None


def slot_places(z):
    return (z, z + 1 - 2 * lax.rem(z, 2), jnp.where(z < 2, 2, 1), jnp.where(z < 2, 3, 0))


def behind(value, other):
    return lax.optimization_barrier((value, other))[0]


def gather_slots(own):
    def pair(block, across):
        return jnp.concatenate([across, block], axis=0)

    near, second, own_y = lax.optimization_barrier((routed(own, to_near), routed(own, to_middle), routed(own, to_y)))
    own_pair = pair(own, own_y)
    last, ends, near_y = lax.optimization_barrier((routed(near, to_middle), routed(second, to_ends), routed(near, to_y)))
    second = second + ends
    near_pair = pair(near, near_y)
    own_core = routed(behind(own_pair, ends), to_core)
    ends, second_y = lax.optimization_barrier((routed(last, to_ends), routed(second, to_y)))
    last = last + ends
    second_pair = pair(second, second_y)
    near_core = routed(behind(near_pair, ends), to_core)
    second_core = routed(second_pair, to_core)
    last_pair = pair(last, routed(last, to_y))
    return [own_pair, near_pair, second_pair, last_pair, own_core, near_core, second_core, routed(last_pair, to_core)]


def scatter_slots(first_pair, rest, vectors):
    rows = first_pair[0].shape[0] // 2

    def met(kept, value):
        total = kept.astype(F32) + value.astype(F32)
        return total[:rows].astype(BF16), total[rows:]

    def low(value):
        return value.astype(BF16)

    def summed(step):
        return vectors + lax.ppermute(vectors, "dp", [(i, i ^ step) for i in range(4 * Z_CHIPS)])

    far, last = met(first_pair[0], routed(first_pair[1], to_core))
    kept, sent = rest(far)
    vectors = behind(vectors, far)
    vectors = summed(1)
    came = routed(far, to_y)
    over = [routed(block, to_core) for block in sent]
    far, second = met(kept[2], over[2])
    came, vectors = lax.optimization_barrier((came, vectors))
    came, last = routed(behind(far, came), to_y), last + came.astype(F32)
    line = routed(low(last), from_ends)
    vectors = summed(2)
    far, near = met(kept[1], over[1])
    came, line, vectors = lax.optimization_barrier((came, line, vectors))
    last, second = last + line.astype(F32), second + came.astype(F32)
    came, line, ends = routed(behind(far, came), to_y), routed(low(last), to_middle), routed(low(second), from_ends)
    vectors = summed(4)
    far, own = met(kept[0], over[0])
    came, line, ends, vectors = lax.optimization_barrier((came, line, ends, vectors))
    near, second = near + came.astype(F32) + line.astype(F32), second + ends.astype(F32)
    started = came
    came = routed(behind(far, came), to_y)
    near, second = routed(low(near), to_near), routed(low(second), to_middle)
    vectors = summed(8)
    return (own + came.astype(F32), second, near), vectors, started


def owners_of(where_ref):
    z, y, c = where_ref[1], where_ref[2], where_ref[3]
    return [(spot(at, 1 - y, core), spot(at, y, core)) for core in (c, 1 - c) for at in slot_places(z)]


def settle_kernel(chans, where_ref, *refs):
    pairs, (wm_ref, wo_ref, cw_ref, cb_ref, gg_ref, gin_ref, line_ref, sem) = refs[:8], refs[8:]
    rows = pairs[0].shape[0] // 2
    feat = wo_ref.shape[1]
    width = wm_ref.shape[1] - LANES
    inner = wo_ref.shape[0]
    last = width + inner
    copies = []
    for pair, owners in zip(pairs, owners_of(where_ref)):
        for half, owner in enumerate(owners):
            mine = pl.ds(half * rows, rows)
            to = pl.ds(pl.multiple_of(owner * rows, 16), rows)
            copies.append((pair.at[pl.ds(half * rows, 16), pl.ds(last + LANES, LANES)], line_ref.at[owner]))
            copies.append((pair.at[mine, pl.ds(0, width)], wm_ref.at[to, pl.ds(0, width)]))
            copies.append((pair.at[mine, pl.ds(last, LANES)], wm_ref.at[to, pl.ds(width, LANES)]))
            for b in range(inner // wm_ref.shape[0]):
                into = pl.ds(pl.multiple_of((owner * (inner // wm_ref.shape[0]) + b) * rows, 16), rows)
                copies.append((pair.at[mine, pl.ds(width + b * feat, feat)], wo_ref.at[into]))
    for source, target in copies:
        pltpu.make_async_copy(source, target, sem).start()
    for whole in (wm_ref, wo_ref, line_ref):
        pltpu.make_async_copy(whole, whole, sem).wait()
    lines = [line_ref[i].astype(F32)[0:8] for i in range(line_ref.shape[0])]
    for c, chunk in enumerate(lay(lines, chans, cw_ref.shape[1] // LANES)):
        cw_ref[:, cols(c)] = chunk[0:TAPS]
        cb_ref[:, cols(c)] = chunk[TAPS : TAPS + 1]
    for c, chunk in enumerate(lay(lines, inner // len(lines), gg_ref.shape[1] // LANES)):
        gg_ref[:, cols(c)] = chunk[TAPS + 1 : TAPS + 2]
    for c, chunk in enumerate(lay(lines, rows, gin_ref.shape[1] // LANES)):
        gin_ref[:, cols(c)] = chunk[TAPS + 2 : TAPS + 3]


def settle(where, pairs, width, chans, feat):
    rows, full = pairs[0].shape[0] // 2, pairs[0].shape[1]
    owners, inner = feat // rows, full - width - 2 * LANES
    return pl.pallas_call(
        functools.partial(settle_kernel, chans),
        in_specs=[SMEM_SPEC] + [HBM_SPEC] * 8,
        out_specs=[VMEM_SPEC] * 6,
        out_shape=(
            shape_of((feat, width + LANES), BF16),
            shape_of((inner, feat), BF16),
            shape_of((TAPS, owners * chans)),
            shape_of((1, owners * chans)),
            shape_of((1, inner)),
            shape_of((1, feat)),
        ),
        scratch_shapes=[pltpu.VMEM((owners, 16, LANES), BF16), pltpu.SemaphoreType.DMA],
        compiler_params=PARAMS,
        name="settle_weights",
    )(where, *pairs)


def slot_blocks(where_ref):
    owners = owners_of(where_ref)
    return [owner for slot in range(4) for pair in (owners[slot], owners[4 + slot]) for owner in pair]


def write_slot(slot, turned, mixed, gp_ref, gb_ref, gdt_ref, line_ref, kept_ref, sent_ref, where_ref):
    rows, width, feat = kept_ref.shape[0] // 2, gp_ref.shape[1], gb_ref.shape[1]
    blocks = mixed.shape[0] // turned.shape[0]
    last = width + blocks * feat
    mine = turned[4 * slot * rows : 4 * (slot + 1) * rows, :]

    def put(at, term):
        kept_ref[:, at] = term[: 2 * rows].astype(BF16)
        sent_ref[:, at] = term[2 * rows :].astype(BF16)

    for c in range(width // 256):
        put(cols(c, 256), dot_nn(mine, gp_ref[:, cols(c, 256)]))
    put(slice(last, last + LANES), dot_nn(mine, gdt_ref[...]))
    owners = slot_blocks(where_ref)[4 * slot : 4 * slot + 4]
    for part, owner in enumerate(owners):
        ref, to = (kept_ref, sent_ref)[part // 2], part % 2 * rows
        for b in range(blocks):
            start = ((4 * slot + part) * blocks + b) * rows
            at = slice(width + b * feat, width + (b + 1) * feat)
            ref[to : to + rows, at] = dot_nn(mixed[start : start + rows, :], gb_ref[...]).astype(BF16)
        line = line_ref[owner]
        ref[to : to + 16, last + LANES :] = jnp.concatenate([line, jnp.zeros_like(line)], axis=0).astype(BF16)
        ref[to + 16 : to + rows, last + LANES :] = jnp.zeros((rows - 16, LANES), BF16)


def first_weight_kernel(rows, chans, where_ref, *refs):
    sources, smalls, outs, scratch = refs[:20], refs[20:32], refs[32:41], refs[41:]
    kept_ref, sent_ref, vec_ref, turned_ref, mixed_ref, gp_ref, gb_ref, gdt_ref, line_ref = outs
    n_ref, mix_ref, flat_ref, wide_ref, sems = scratch
    tok, feat, inner = sources[0].shape[0], n_ref.shape[1], mix_ref.shape[1]
    blocks = inner // feat
    into = [ref.at[part * tok : (part + 1) * tok] for part in range(2) for ref in (n_ref, mix_ref, gp_ref, gb_ref, gdt_ref)]
    take(where_ref, [[(source, None) for source in sources[10 * i : 10 * i + 10]] for i in range(2)], into, sems)
    early = jnp.where(where_ref[0] == 0, 0.0, 1.0)
    sums = [one[...] + early * zero[...] + (1.0 - early) * two[...] for zero, one, two in zip(smalls[0::3], smalls[1::3], smalls[2::3])]
    vec_ref[...] = sums[3]
    pieces = [[total[:, cols(c)] for c in range(total.shape[1] // LANES)] for total in sums]
    row = lax.broadcasted_iota(jnp.int32, (8, LANES), 0)
    for i in range(feat // rows):
        block = cut(pieces[0], chans, i)
        block = jnp.where(row == TAPS + 1, jnp.broadcast_to(cut(pieces[1], blocks * rows, i)[0:1], block.shape), block)
        line_ref[i] = jnp.where(row == TAPS + 2, jnp.broadcast_to(cut(pieces[2], rows, i)[0:1], block.shape), block)
    owners = slot_blocks(where_ref)
    taken(into, sems, 0, 5)
    flat_ref[...] = n_ref[...].T
    for i, owner in enumerate(owners):
        turned_ref[i * rows : (i + 1) * rows, :] = flat_ref[pl.ds(pl.multiple_of(owner * rows, 16), rows), :]
    taken(into, sems, 1, 6)
    wide_ref[...] = mix_ref[...].T
    many = blocks * rows
    for i, owner in enumerate(owners):
        mixed_ref[i * many : (i + 1) * many, :] = wide_ref[pl.ds(pl.multiple_of(owner * many, 16), many), :]
    taken(into, sems, 2, 7, 3, 8, 4, 9)
    write_slot(3, turned_ref, mixed_ref, gp_ref, gb_ref, gdt_ref, line_ref, kept_ref, sent_ref, where_ref)


def rest_weight_kernel(where_ref, turned_ref, mixed_ref, gp_ref, gb_ref, gdt_ref, line_ref, *outs):
    for slot in (2, 1, 0):
        write_slot(slot, turned_ref, mixed_ref, gp_ref, gb_ref, gdt_ref, line_ref, outs[slot], outs[3 + slot], where_ref)


def weight_terms(where, one, other, smalls, rows, chans):
    tok, feat = one[0].shape
    inner, width = one[1].shape[1], one[2].shape[1]
    pair = shape_of((2 * rows, width + inner + 2 * LANES), BF16)
    shared = (
        shape_of((feat, 2 * tok), BF16),
        shape_of((inner, 2 * tok), BF16),
        shape_of((2 * tok, width), BF16),
        shape_of((2 * tok, feat), BF16),
        shape_of((2 * tok, LANES), BF16),
        shape_of((feat // rows, 8, LANES)),
    )
    kept, sent, vectors, *common = pl.pallas_call(
        functools.partial(first_weight_kernel, rows, chans),
        in_specs=[SMEM_SPEC] + [HBM_SPEC] * 20 + [VMEM_SPEC] * 12,
        out_specs=[VMEM_SPEC] * 9,
        out_shape=(pair, pair, shape_of((8, LANES))) + shared,
        scratch_shapes=[
            pltpu.VMEM((2 * tok, feat), BF16),
            pltpu.VMEM((2 * tok, inner), BF16),
            pltpu.VMEM((feat, 2 * tok), BF16),
            pltpu.VMEM((inner, 2 * tok), BF16),
            pltpu.SemaphoreType.DMA((10,)),
        ],
        compiler_params=PARAMS,
        name="weight_gradients_first",
    )(where, *one, *other, *smalls)

    def rest(after):
        outs = pl.pallas_call(
            rest_weight_kernel,
            in_specs=[SMEM_SPEC] + [VMEM_SPEC] * 6,
            out_specs=[VMEM_SPEC] * 6,
            out_shape=(pair,) * 6,
            compiler_params=PARAMS,
            name="weight_gradients_rest",
        )(where, behind(common[0], after), *common[1:])
        return outs[:3], outs[3:]

    return (kept, sent), vectors, rest


def unpack_kernel(own_ref, second_ref, near_ref, wm_ref, wo_ref, wdt_ref, cw_ref, cb_ref, gg_ref, ng_ref, square):
    rows, width = wm_ref.shape
    feat = wo_ref.shape[1]
    blocks = wo_ref.shape[0] // rows
    last = width + blocks * feat

    def total(at, count):
        some = slice(0, count)
        return own_ref[some, at] + (second_ref[some, at].astype(F32) + near_ref[some, at].astype(F32))

    for c in range(width // 256):
        wm_ref[:, cols(c, 256)] = total(cols(c, 256), rows)
    for b in range(blocks):
        wo_ref[b * rows : (b + 1) * rows, :] = total(slice(width + b * feat, width + (b + 1) * feat), rows)
    square[...] = jnp.zeros(square.shape, F32)
    square[:rows, :] = total(slice(last, last + LANES), rows)
    wdt_ref[...] = square[...].T[: wdt_ref.shape[0], :rows]
    line = total(slice(last + LANES, last + 2 * LANES), 16)
    cw_ref[...] = line[0:TAPS, : cw_ref.shape[1]]
    for k, ref in enumerate((cb_ref, gg_ref, ng_ref)):
        ref[...] = line[TAPS + k : TAPS + k + 1, : ref.shape[1]]


def unpack_sums(terms, wm, wo, wdt, cw, cb, gg, ng):
    return pl.pallas_call(
        unpack_kernel,
        out_shape=tuple(shape_of(part.shape) for part in (wm, wo, wdt, cw, cb, gg, ng)),
        scratch_shapes=[pltpu.VMEM((LANES, LANES), F32)],
        compiler_params=PARAMS,
        name="unpack_sums",
    )(*terms)


def small_rows(vectors, rows):
    flat = jnp.concatenate([vector.reshape(-1) for vector in vectors])
    lines = -(-flat.shape[0] // LANES)
    wide = -(-lines // rows)
    flat = jnp.pad(flat, (0, lines * LANES - flat.shape[0])).reshape(lines, LANES)
    flat = jnp.pad(flat, ((0, rows * wide - lines), (0, 0)))
    return flat.reshape(wide, rows, LANES).transpose(1, 0, 2).reshape(rows, wide * LANES)


def small_flat(block, owners):
    rows, wide = block.shape[0] // owners, block.shape[1] // LANES
    return block.reshape(owners, rows, wide, LANES).transpose(0, 2, 1, 3).reshape(owners, wide * rows * LANES)


def total_over(value, axis):
    count = lax.axis_size(axis)
    step = 1
    while step < count:
        value = value + lax.ppermute(value, axis, [(i, i ^ step) for i in range(count)])
        step = step * 2
    return value


def shards(inputs, segments, cotangent, norm_gain, w_main, w_dt, conv_weight, conv_bias, dt_bias, a_log, skip_d, gate_gain, w_out):
    first = lax.axis_index("section") == 0
    dp = lax.axis_size("dp")
    feat = inputs.shape[2]
    rows, width = w_main.shape[1:]
    heads = w_dt.shape[2]
    chans, own_inner = conv_weight.shape[2], gate_gain.shape[1]
    inner = own_inner * dp
    blocks = own_inner // rows

    owned = (w_main[0], w_out[0], jnp.swapaxes(w_dt[0], 0, 1), conv_weight[0], conv_bias, gate_gain, norm_gain)
    aligned = rows % 16 == 0 and dp == 4 * Z_CHIPS
    side = lax.axis_index("section")
    place = lax.axis_index("dp")
    where = jnp.stack([side, place // 4, place // 2 % 2, place % 2]).astype(jnp.int32)
    if aligned:
        wm, wo, cw, cb, gg, gin = settle(where, gather_slots(pack_shard(*owned)), width, chans, feat)
    else:
        small = small_rows((conv_weight[0], conv_bias[0], gate_gain[0], norm_gain[0]), rows)
        out_block = w_out[0].reshape(blocks, rows, feat).transpose(1, 0, 2).reshape(rows, inner)
        packed = jnp.concatenate([w_main[0], out_block, jnp.pad(w_dt[0], ((0, 0), (0, LANES - heads))), small], axis=1)
        whole = lax.all_gather(packed, "dp", axis=0, tiled=True)
    marks = [TAPS * chans, (TAPS + 1) * chans, (TAPS + 1) * chans + own_inner, (TAPS + 1) * chans + own_inner + rows]
    if not aligned:
        wm = jnp.concatenate([whole[:, :width], whole[:, width + inner : width + inner + LANES]], axis=1)
        wo = whole[:, width : width + inner].reshape(dp, rows, blocks, feat).transpose(0, 2, 1, 3).reshape(inner, feat)
        flat = small_flat(whole[:, width + inner + LANES :], dp).astype(F32)
        cw = flat[:, : marks[0]].reshape(dp, TAPS, chans).transpose(1, 0, 2).reshape(TAPS, dp * chans)
        cb = flat[:, marks[0] : marks[1]].reshape(1, dp * chans)
        gg = flat[:, marks[1] : marks[2]].reshape(1, inner)
        gin = flat[:, marks[2] : marks[3]].reshape(1, feat)
    hp = jnp.pad(jnp.concatenate([dt_bias, a_log], axis=0), ((0, 6), (0, LANES - heads)))
    sk = jnp.repeat(skip_d, inner // heads, axis=1)
    weights = (wm, wo, gin, cw, cb, gg, hp, sk)

    def choose(one, other):
        return jnp.where(first, one, other)

    up = down = [(0, 1), (1, 0)]
    ids = segments.astype(F32)[:, None, :]
    f0 = forward_layer(0, where, ids, weights, [(inputs, 0)])
    r0 = lax.ppermute(f0[0], "section", up)
    f1 = forward_layer(3, where, ids, weights, [(inputs, 1), (r0, None)])
    r1 = lax.ppermute(f1[0], "section", up)
    f2 = forward_layer(1, where, ids, weights, [(inputs, 1), (r1, None)])

    def stored(tick):
        return [(tick[i], None) for i in (2, 3, 4, 6, 7, 8)]

    kept = stored(f1)
    now = [[(cotangent, 0), (inputs, 1)] + kept, [(cotangent, 0), (r0, None)] + kept]
    b0 = backward_layer(0, where, ids, weights, now)
    d0 = lax.ppermute(b0[1], "section", down)
    now = [
        [(d0, None), (inputs, 0)] + stored(f0),
        [(cotangent, 1), (r1, None)] + stored(f2),
    ]
    b1 = backward_layer(2, where, ids, weights, now)
    d1 = lax.ppermute(b1[1], "section", down)
    b2 = backward_layer(1, where, ids, weights, [[(d1, None), (inputs, 1)] + kept])
    dch, din, dgin, dhp = tuple(choose(two, zero) + one for zero, one, two in zip(b0[4:], b1[4:], b2[4:]))
    on_first = (f0[1], f0[5], b1[2], d0, b1[3]), (f1[1], f1[5], b2[2], d1, b2[3])
    on_last = (f2[1], f2[5], b1[2], cotangent[1], b1[3]), (f1[1], f1[5], b0[2], cotangent[0], b0[3])
    if aligned:
        smalls = [part[i] for i in (4, 5, 6, 7) for part in (b0, b1, b2)]
        first_pair, vectors, rest = weight_terms(where, on_first[0] + on_first[1], on_last[0] + on_last[1], smalls, rows, chans)
    else:
        n, mix, gp, gb, gdt = tuple(
            jnp.concatenate([choose(on_first[0][i], on_last[0][i]), choose(on_first[1][i], on_last[1][i])], axis=0) for i in range(5)
        )
        own = [
            small_rows(
                (
                    dch[:TAPS, i * chans : (i + 1) * chans],
                    dch[TAPS, i * chans : (i + 1) * chans],
                    din[0, i * own_inner : (i + 1) * own_inner],
                    dgin[0, i * rows : (i + 1) * rows],
                ),
                rows,
            )
            for i in range(dp)
        ]
        wide = dot_tn(mix, gb).reshape(dp, blocks, rows, feat).transpose(0, 2, 1, 3).reshape(feat, inner)
        parts = [dot_tn(n, gp), wide, dot_tn(n, gdt), jnp.concatenate(own, axis=0)]
        packed_grad = jnp.concatenate([part.astype(BF16) for part in parts], axis=1)
    if aligned:
        terms, vectors, started = scatter_slots(first_pair, rest, vectors)
        heads_sum = vectors[:, :heads]
    else:
        summed = lax.psum_scatter(packed_grad, "dp", scatter_dimension=0, tiled=True)
        heads_sum = total_over(dhp[:3, :heads], "dp")
        started = summed
    if aligned:
        g_main, g_out, g_dt, g_cw, g_cb, g_gg, g_ng = unpack_sums(terms, *owned)
        g_dt = jnp.swapaxes(g_dt, 0, 1)
    else:
        summed = summed.astype(F32)
        got = small_flat(summed[:, width + inner + LANES :], 1)[0]
        g_main = summed[:, :width]
        g_out = summed[:, width : width + inner].reshape(rows, blocks, feat).transpose(1, 0, 2).reshape(own_inner, feat)
        g_dt = summed[:, width + inner : width + inner + heads]
        g_cw = got[: marks[0]].reshape(TAPS, chans)
        g_cb, g_gg, g_ng = (got[None, marks[i] : marks[i + 1]] for i in range(3))
    outs = [part[0] for part in (f0, f1, f2, b0, b1, b2)]
    outs = lax.optimization_barrier((*outs, started))
    hidden = jnp.stack([choose(outs[0], outs[1]), choose(outs[1], outs[2])])[None]
    grad_inputs = jnp.stack([choose(outs[4], outs[3]), choose(outs[5], outs[4])])[None]
    return (
        hidden,
        grad_inputs,
        g_ng,
        g_main[None],
        g_dt[None],
        g_cw[None],
        g_cb,
        heads_sum[0:1],
        heads_sum[1:2],
        heads_sum[2:3],
        g_gg,
        g_out[None],
    )


def solution(mesh):
    placed = (
        P(None, "dp", None),
        P(None, "dp"),
        P(None, "dp", None),
        P("section", "dp"),
        P("section", "dp", None),
        P("section", "dp", None),
        P("section", None, "dp"),
        P("section", "dp"),
        P("section", None),
        P("section", None),
        P("section", None),
        P("section", "dp"),
        P("section", "dp", None),
    )
    return jax.shard_map(
        shards,
        mesh=mesh,
        in_specs=placed,
        out_specs=(
            P("section", None, "dp", None),
            P("section", None, "dp", None),
            P("section", "dp"),
            P("section", "dp", None),
            P("section", "dp", None),
            P("section", None, "dp"),
            P("section", "dp"),
            P("section", None),
            P("section", None),
            P("section", None),
            P("section", "dp"),
            P("section", "dp", None),
        ),
        check_vma=False,
    )
```

```python
import functools

import jax
import jax.numpy as jnp
from jax import lax
from jax.experimental import pallas as pl
from jax.experimental.pallas import tpu as pltpu
from jax.sharding import PartitionSpec as P

norm_eps = 1e-05
F32 = jnp.float32
BF16 = jnp.bfloat16
LANES = 128
TAPS = 4
VMEM_BYTES = 28 * 1024 * 1024


def dot_nn(a, b):
    return lax.dot_general(a, b, (((1,), (0,)), ((), ())), preferred_element_type=F32)


def dot_nt(a, b):
    return lax.dot_general(a, b, (((1,), (1,)), ((), ())), preferred_element_type=F32)


def dot_tn(a, b):
    return lax.dot_general(a, b, (((0,), (0,)), ((), ())), preferred_element_type=F32)


def split(a):
    high = a.astype(BF16)
    return high, (a - high.astype(F32)).astype(BF16)


def exact(dot, a, b):
    ah, al = split(a)
    bh, bl = split(b)
    return dot(ah, bh) + (dot(ah, bl) + dot(al, bh))


def near(dot, a, b):
    return exact(dot, a, b)


def triangle(lower):
    rows = lax.broadcasted_iota(jnp.int32, (LANES, LANES), 0)
    cols = lax.broadcasted_iota(jnp.int32, (LANES, LANES), 1)
    return jnp.where(rows >= cols if lower else rows <= cols, 1.0, 0.0).astype(BF16)


def running(tri, a):
    high = a.astype(BF16)
    rest = a - high.astype(F32)
    mid = rest.astype(BF16)
    low = (rest - mid.astype(F32)).astype(BF16)
    return dot_nn(tri, high) + (dot_nn(tri, mid) + dot_nn(tri, low))


def sigmoid(a):
    return 0.5 * jnp.tanh(0.5 * a) + 0.5


def softplus(a):
    return jnp.maximum(a, 0.0) + jnp.log1p(jnp.exp(-jnp.abs(a)))


def cols(j, width=LANES):
    return slice(j * width, (j + 1) * width)


def token_masks(ids):
    length = ids.shape[1]
    across = jnp.broadcast_to(ids, (length, length))
    wide = across.T
    rows = lax.broadcasted_iota(jnp.int32, (length, length), 0)
    lane = lax.broadcasted_iota(jnp.int32, (length, length), 1)
    linked = jnp.where((rows >= lane) & (wide == across), 1.0, 0.0)
    sees = [None]
    for k in range(1, TAPS):
        sees.append(jnp.where((rows >= k) & (pltpu.roll(wide, k, 0) == wide), 1.0, 0.0))
    return linked, sees


def take(which_ref, choices, into, sems):
    def start(choice):
        for i, ((ref, index), target) in enumerate(zip(choice, into)):
            pltpu.make_async_copy(ref if index is None else ref.at[index], target, sems.at[i]).start()

    if len(choices) == 1:
        start(choices[0])
        return
    for number, choice in enumerate(choices):
        pl.when(which_ref[0] == number)(functools.partial(start, choice))


def taken(into, sems, *numbers):
    for i in numbers:
        pltpu.make_async_copy(into[i], into[i], sems.at[i]).wait()


def conv_taps(v, sees):
    return [v] + [sees[k] * pltpu.roll(v, k, 0) for k in range(1, TAPS)]


def conv_sum(taps, cw_ref, cb_ref, at):
    total = cb_ref[:, at] + cw_ref[TAPS - 1 : TAPS, at] * taps[0]
    for k in range(1, TAPS):
        total = total + cw_ref[TAPS - 1 - k : TAPS - k, at] * taps[k]
    return total


def pair_of(values, j):
    lane = lax.broadcasted_iota(jnp.int32, (values.shape[0], LANES), 1)
    first = jnp.broadcast_to(values[:, 2 * j : 2 * j + 1], lane.shape)
    second = jnp.broadcast_to(values[:, 2 * j + 1 : 2 * j + 2], lane.shape)
    return jnp.where(lane < LANES // 2, first, second)


def halves(values):
    lane = lax.broadcasted_iota(jnp.int32, values.shape, 1)
    low = jnp.where(lane < LANES // 2, values, 0.0)
    return jnp.concatenate([low, values - low], axis=0)


def decay(cum, cum_t, linked, h):
    spread = cum[:, h : h + 1] - cum_t[h : h + 1, :]
    return linked * jnp.exp(jnp.minimum(spread, 0.0))


def micro_of(which_ref, mode):
    return (0, 1, which_ref[0], 1 - which_ref[0])[mode]


def held(which_ref, options, indices):
    refs = [ref if index is None else ref.at[index] for ref, index in zip(options, indices)]

    def read(at=slice(None)):
        values = [ref[:, at] for ref in refs]
        return values[0] if len(values) == 1 else jnp.where(which_ref[0] == 0, values[0], values[1])

    return read


KEPT = 8


def fwd_kernel(plan, mode, which_ref, ids_ref, wm_ref, wo_ref, gin_ref, cw_ref, cb_ref, gg_ref, hp_ref, sk_ref, *refs):
    sources, refs = refs[: len(plan)], refs[len(plan) :]
    v_ref, n_ref, p_ref, dtr_ref, y_ref, mix_ref, total_ref, g_ref, r2_ref = refs
    inner, width = gg_ref.shape[1], p_ref.shape[1]
    pairs = inner // LANES
    linked, sees = token_masks(ids_ref[micro_of(which_ref, mode)])
    u = held(which_ref, sources, plan)().astype(F32)
    r = lax.rsqrt(jnp.mean(u * u, axis=-1, keepdims=True) + norm_eps)
    n = (u * r * gin_ref[...]).astype(BF16)
    n_ref[...] = n
    for c in range(width // 256):
        p_ref[:, cols(c, 256)] = dot_nn(n, wm_ref[:, cols(c, 256)])
    dtr = dot_nn(n, wm_ref[:, width:])
    dtr_ref[...] = dtr

    def conv(j):
        total = conv_sum(conv_taps(p_ref[:, inner + j * LANES : inner + (j + 1) * LANES], sees), cw_ref, cb_ref, cols(j))
        total_ref[:, cols(j)] = total
        return total * sigmoid(total)

    b_state = conv(pairs)
    c_state = conv(pairs + 1)
    cross = exact(dot_nt, c_state, b_state)
    dt = softplus(dtr + hp_ref[0:1, :])
    cum = running(triangle(True), -dt * jnp.exp(hp_ref[1:2, :]))
    cum_t = cum.T
    squares = jnp.zeros((u.shape[0], LANES), F32)
    for j in range(pairs):
        at = cols(j)
        x = conv(j)
        m = jnp.concatenate([cross * decay(cum, cum_t, linked, 2 * j), cross * decay(cum, cum_t, linked, 2 * j + 1)], axis=1)
        y = near(dot_nn, m, halves(x * pair_of(dt, j))) + sk_ref[:, at] * x
        y_ref[:, at] = y
        z = p_ref[:, at]
        g = y * (z * sigmoid(z))
        g_ref[:, at] = g
        squares = squares + g * g
    r2 = lax.rsqrt(jnp.sum(squares, axis=-1, keepdims=True) / inner + norm_eps)
    for j in range(pairs):
        at = cols(j)
        mix_ref[:, at] = (g_ref[:, at] * r2 * gg_ref[:, at]).astype(BF16)
    r2_ref[...] = jnp.broadcast_to(r2, r2_ref.shape)
    mixed = mix_ref[...]
    for c in range(u.shape[1] // 256):
        at = cols(c, 256)
        v_ref[:, at] = (u[:, at] + dot_nn(mixed, wo_ref[:, at])).astype(BF16)


def bwd_kernel(plan, mode, which_ref, ids_ref, wm_ref, wo_ref, gin_ref, cw_ref, cb_ref, gg_ref, hp_ref, sk_ref, *refs):
    count = KEPT * len(plan)
    sources, refs = refs[:count], refs[count:]
    gi_ref, gl_ref, gp_ref, gdt_ref, dch_ref, din_ref, dgin_ref, dhp_ref, gm_scr = refs
    gv, u_low, p, dtr, y_kept, totals, g_kept, r2_kept = [
        held(which_ref, [sources[KEPT * k + i] for k in range(len(plan))], [indices[i] for indices in plan]) for i in range(KEPT)
    ]
    dch_ref[...] = jnp.zeros(dch_ref.shape, F32)
    din_ref[...] = jnp.zeros(din_ref.shape, F32)
    inner = gg_ref.shape[1]
    pairs = inner // LANES
    length = gm_scr.shape[0]
    linked, sees = token_masks(ids_ref[micro_of(which_ref, mode)])
    gb = gv()
    inners = jnp.zeros((length, 256), F32)
    for c in range(inner // 256):
        at = cols(c, 256)
        gm = dot_nt(gb, wo_ref[at, :])
        gm_scr[:, at] = gm
        inners = inners + gm * gg_ref[:, at] * g_kept(at)
    r2 = r2_kept()[:, 0:1]
    pull = r2 * r2 * r2 * (jnp.sum(inners, axis=-1, keepdims=True) / inner)

    def conv(j):
        total = totals(cols(j))
        return total, sigmoid(total)

    def conv_back(j, total, sig, grad):
        at = cols(j)
        v = p(slice(inner + j * LANES, inner + (j + 1) * LANES))
        ds = grad * (sig * (1.0 + total * (1.0 - sig)))
        dch_ref[TAPS : TAPS + 1, at] = jnp.sum(ds, axis=0, keepdims=True)
        dch_ref[TAPS - 1 : TAPS, at] = jnp.sum(ds * v, axis=0, keepdims=True)
        dv = cw_ref[TAPS - 1 : TAPS, at] * ds
        for k in range(1, TAPS):
            row = slice(TAPS - 1 - k, TAPS - k)
            moved = pltpu.roll(sees[k] * ds, length - k, 0)
            dch_ref[row, at] = jnp.sum(moved * v, axis=0, keepdims=True)
            dv = dv + cw_ref[row, at] * moved
        gp_ref[:, inner + j * LANES : inner + (j + 1) * LANES] = dv.astype(BF16)

    sb, gb_sig = conv(pairs)
    b_state = sb * gb_sig
    sc, gc_sig = conv(pairs + 1)
    c_state = sc * gc_sig
    cross = exact(dot_nt, c_state, b_state)
    dt_arg = dtr() + hp_ref[0:1, :]
    dt = softplus(dt_arg)
    rate = jnp.exp(hp_ref[1:2, :])
    cum = running(triangle(True), -dt * rate)
    cum_t = cum.T
    dcross = jnp.zeros((length, length), F32)
    dcum = jnp.zeros((length, LANES), F32)
    ddt = jnp.zeros((length, LANES), F32)
    dskip = jnp.zeros((8, LANES), F32)
    lane = lax.broadcasted_iota(jnp.int32, (2 * LANES, LANES), 1)
    row = lax.broadcasted_iota(jnp.int32, (2 * LANES, LANES), 0)
    half = jnp.where((row % LANES) < LANES // 2, 0, 1)
    for j in range(pairs):
        at = cols(j)
        pick = jnp.where(lane == 2 * j + half, 1.0, 0.0).astype(BF16)
        gm = gm_scr[:, at]
        g = g_kept(at)
        din_ref[0:1, at] = jnp.sum(gm * (g * r2), axis=0, keepdims=True)
        dg = gm * gg_ref[:, at] * r2 - g * pull
        z = p(at)
        sig = sigmoid(z)
        y = y_kept(at)
        dy = dg * (z * sig)
        gp_ref[:, at] = (dg * y * (sig * (1.0 + z * (1.0 - sig)))).astype(BF16)
        total, tsig = conv(j)
        x = total * tsig
        dtp = pair_of(dt, j)
        xw = x * dtp
        dy_st = halves(dy)
        l1 = decay(cum, cum_t, linked, 2 * j)
        l2 = decay(cum, cum_t, linked, 2 * j + 1)
        dm = dot_nt(dy_st.astype(BF16), xw.astype(BF16))
        dcross = dcross + dm[:length] * l1 + dm[length:] * l2
        m = jnp.concatenate([cross * l1, cross * l2], axis=0)
        dxw = near(dot_tn, m, dy_st)
        skip = sk_ref[:, at]
        lanes = jnp.broadcast_to(jnp.sum(dy * x, axis=0, keepdims=True), (8, LANES))
        dskip = dskip + dot_nn(jnp.concatenate(split(lanes), axis=1), pick)
        q = dy * (y - skip * x) - dxw * xw
        dcum = dcum + dot_nn(jnp.concatenate(split(q), axis=1), pick)
        ddt = ddt + dot_nn(jnp.concatenate(split(dxw * x), axis=1), pick)
        conv_back(j, total, tsig, skip * dy + dxw * dtp)
    conv_back(pairs, sb, gb_sig, exact(dot_tn, dcross, c_state))
    conv_back(pairs + 1, sc, gc_sig, exact(dot_nn, dcross, b_state))
    dlog = running(triangle(False), dcum)
    draw = (ddt - rate * dlog) * sigmoid(dt_arg)
    gdt = draw.astype(BF16)
    gdt_ref[...] = gdt
    dhp_ref[0:1, :] = jnp.sum(draw, axis=0, keepdims=True)
    dhp_ref[1:2, :] = jnp.sum(dlog * (-dt * rate), axis=0, keepdims=True)
    dhp_ref[2:3, :] = dskip[0:1]
    dhp_ref[3:8, :] = jnp.zeros((5, LANES), F32)
    u = u_low().astype(F32)
    gin = gin_ref[...]
    r = lax.rsqrt(jnp.mean(u * u, axis=-1, keepdims=True) + norm_eps)
    gp = gp_ref[...]
    width = gp.shape[1]
    gn = jnp.concatenate(
        [dot_nt(gp, wm_ref[cols(c, 256), :width]) + dot_nt(gdt, wm_ref[cols(c, 256), width:]) for c in range(u.shape[1] // 256)], axis=1
    )
    dgin_ref[...] = jnp.broadcast_to(jnp.sum(gn * (u * r), axis=0, keepdims=True), dgin_ref.shape)
    gng = gn * gin
    back = r * r * r * jnp.mean(gng * u, axis=-1, keepdims=True)
    grad = gb.astype(F32) + (gng * r - u * back)
    gi_ref[...] = grad
    gl_ref[...] = grad.astype(BF16)


def shape_of(shape, dtype=F32):
    return jax.ShapeDtypeStruct(shape, dtype)


VMEM_SPEC = pl.BlockSpec(memory_space=pltpu.VMEM)
HBM_SPEC = pl.BlockSpec(memory_space=pltpu.HBM)
SMEM_SPEC = pl.BlockSpec(memory_space=pltpu.SMEM)
PARAMS = pltpu.CompilerParams(vmem_limit_bytes=VMEM_BYTES)


def layer_sizes(weights):
    return weights[0].shape[0], weights[1].shape[0], weights[0].shape[1] - LANES


def forward_layer(mode, which, ids, weights, choices):
    tok = ids.shape[2]
    feat, inner, width = layer_sizes(weights)
    return pl.pallas_call(
        functools.partial(fwd_kernel, tuple(index for _, index in choices), mode),
        in_specs=[SMEM_SPEC] + [VMEM_SPEC] * (9 + len(choices)),
        out_specs=[VMEM_SPEC] * 9,
        out_shape=(
            shape_of((tok, feat), BF16),
            shape_of((tok, feat), BF16),
            shape_of((tok, width)),
            shape_of((tok, LANES)),
            shape_of((tok, inner)),
            shape_of((tok, inner), BF16),
            shape_of((tok, width - inner)),
            shape_of((tok, inner)),
            shape_of((tok, LANES)),
        ),
        compiler_params=PARAMS,
        name="layer_forward",
    )(which, ids, *weights, *[source for source, _ in choices])


def backward_layer(mode, which, ids, weights, choices):
    tok = ids.shape[2]
    feat, inner, width = layer_sizes(weights)
    return pl.pallas_call(
        functools.partial(bwd_kernel, tuple(tuple(index for _, index in choice) for choice in choices), mode),
        in_specs=[SMEM_SPEC] + [VMEM_SPEC] * (9 + KEPT * len(choices)),
        out_specs=[VMEM_SPEC] * 8,
        out_shape=(
            shape_of((tok, feat)),
            shape_of((tok, feat), BF16),
            shape_of((tok, width), BF16),
            shape_of((tok, LANES), BF16),
            shape_of((8, width - inner)),
            shape_of((8, inner)),
            shape_of((8, feat)),
            shape_of((8, LANES)),
        ),
        scratch_shapes=[pltpu.VMEM((tok, inner), F32)],
        compiler_params=PARAMS,
        name="layer_backward",
    )(which, ids, *weights, *[source for choice in choices for source, _ in choice])


def lay(blocks, size, chunks):
    lane = lax.broadcasted_iota(jnp.int32, (8, LANES), 1)
    out = [jnp.zeros((8, LANES), F32) for _ in range(chunks)]
    for i, block in enumerate(blocks):
        chunk, shift = (i * size) // LANES, (i * size) % LANES
        turned = pltpu.roll(block, shift, 1) if shift else block
        out[chunk] = jnp.where((lane >= shift) & (lane < shift + size), turned, out[chunk])
        if shift + size > LANES:
            out[chunk + 1] = jnp.where(lane < shift + size - LANES, turned, out[chunk + 1])
    return out


def cut(chunks, size, i):
    lane = lax.broadcasted_iota(jnp.int32, (8, LANES), 1)
    chunk, shift = (i * size) // LANES, (i * size) % LANES
    turn = (LANES - shift) % LANES
    block = pltpu.roll(chunks[chunk], turn, 1) if turn else chunks[chunk]
    if shift + size > LANES:
        block = jnp.where(lane < LANES - shift, block, pltpu.roll(chunks[chunk + 1], turn, 1))
    return jnp.where(lane < size, block, 0.0)


def pack_kernel(wm_ref, wo_ref, wdt_ref, cw_ref, cb_ref, gg_ref, ng_ref, out_ref, line, square):
    rows, width = wm_ref.shape
    feat = wo_ref.shape[1]
    blocks = wo_ref.shape[0] // rows
    out_ref[:, :width] = wm_ref[...]
    for b in range(blocks):
        out_ref[:, width + b * feat : width + (b + 1) * feat] = wo_ref[b * rows : (b + 1) * rows, :]
    last = width + blocks * feat
    out_ref[:, last + LANES :] = jnp.zeros((rows, LANES), BF16)
    square[...] = jnp.zeros(square.shape, F32)
    square[: wdt_ref.shape[0], :rows] = wdt_ref[...].astype(F32)
    out_ref[:, last : last + LANES] = square[...].T[:rows].astype(BF16)
    line[...] = jnp.zeros(line.shape, F32)
    line[0:TAPS, : cw_ref.shape[1]] = cw_ref[...].astype(F32)
    for k, ref in enumerate((cb_ref, gg_ref, ng_ref)):
        line[TAPS + k : TAPS + k + 1, : ref.shape[1]] = ref[...].astype(F32)
    out_ref[0:16, last + LANES :] = line[...].astype(BF16)


def pack_shard(wm, wo, wdt, cw, cb, gg, ng):
    rows, width = wm.shape
    full = width + wo.shape[0] // rows * wo.shape[1] + 2 * LANES
    return pl.pallas_call(
        pack_kernel,
        out_shape=shape_of((rows, full), BF16),
        scratch_shapes=[pltpu.VMEM((16, LANES), F32), pltpu.VMEM((LANES, LANES), F32)],
        compiler_params=pltpu.CompilerParams(vmem_limit_bytes=2 * VMEM_BYTES),
        name="pack_shard",
    )(wm, wo, wdt, cw, cb, gg, ng)


Z_CHIPS = 4


def spot(z, y, c):
    return (z * 2 + y) * 2 + c


def routed(value, move):
    pairs = []
    for z in range(Z_CHIPS):
        for y in range(2):
            for c in range(2):
                target = move(z, y, c)
                if target is not None:
                    pairs.append((spot(z, y, c), spot(*target)))
    return lax.ppermute(value, "dp", pairs)


def to_core(z, y, c):
    return z, y, 1 - c


def to_y(z, y, c):
    return z, 1 - y, c


def to_near(z, y, c):
    return z ^ 1, y, c


def to_middle(z, y, c):
    return (3 - z, y, c) if z in (1, 2) else None


def to_ends(z, y, c):
    return (z ^ 1, y, c) if z in (1, 2) else None


def from_ends(z, y, c):
    return (z ^ 1, y, c) if z in (0, 3) else None


def slot_places(z):
    return (z, z + 1 - 2 * lax.rem(z, 2), jnp.where(z < 2, 2, 1), jnp.where(z < 2, 3, 0))


def behind(value, other):
    return lax.optimization_barrier((value, other))[0]


def gather_slots(own):
    def pair(block, across):
        return jnp.concatenate([across, block], axis=0)

    near, second, own_y = lax.optimization_barrier((routed(own, to_near), routed(own, to_middle), routed(own, to_y)))
    own_pair = pair(own, own_y)
    last, ends, near_y = lax.optimization_barrier((routed(near, to_middle), routed(second, to_ends), routed(near, to_y)))
    second = second + ends
    near_pair = pair(near, near_y)
    own_core = routed(behind(own_pair, ends), to_core)
    ends, second_y = lax.optimization_barrier((routed(last, to_ends), routed(second, to_y)))
    last = last + ends
    second_pair = pair(second, second_y)
    near_core = routed(behind(near_pair, ends), to_core)
    second_core = routed(second_pair, to_core)
    last_pair = pair(last, routed(last, to_y))
    return [own_pair, near_pair, second_pair, last_pair, own_core, near_core, second_core, routed(last_pair, to_core)]


def scatter_slots(first_blocks, rest, vectors):
    rows = first_blocks[0].shape[0]

    def met(kept, value):
        total = kept.astype(F32) + value.astype(F32)
        return total[:rows].astype(BF16), total[rows:]

    def low(value):
        return value.astype(BF16)

    def summed(step):
        return vectors + lax.ppermute(vectors, "dp", [(i, i ^ step) for i in range(4 * Z_CHIPS)])

    kept_far, kept_near, sent_far, sent_near = first_blocks
    far = low(kept_far.astype(F32) + routed(sent_far, to_core).astype(F32))
    last = kept_near.astype(F32) + routed(behind(sent_near, far), to_core).astype(F32)
    kept, sent = rest(far)
    came = routed(far, to_y)
    vectors = behind(vectors, far)
    vectors = summed(1)
    over = [routed(block, to_core) for block in sent]
    far, second = met(kept[2], over[2])
    came, vectors = lax.optimization_barrier((came, vectors))
    came, last = routed(behind(far, came), to_y), last + came.astype(F32)
    line = routed(low(last), from_ends)
    vectors = summed(2)
    far, near = met(kept[1], over[1])
    came, line, vectors = lax.optimization_barrier((came, line, vectors))
    last, second = last + line.astype(F32), second + came.astype(F32)
    came, line, ends = routed(behind(far, came), to_y), routed(low(last), to_middle), routed(low(second), from_ends)
    vectors = summed(4)
    far, own = met(kept[0], over[0])
    came, line, ends, vectors = lax.optimization_barrier((came, line, ends, vectors))
    near, second = near + came.astype(F32) + line.astype(F32), second + ends.astype(F32)
    started = came
    came = routed(behind(far, came), to_y)
    near, second = routed(low(near), to_near), routed(low(second), to_middle)
    vectors = summed(8)
    return (own + came.astype(F32), second, near), vectors, started


def owners_of(where_ref):
    z, y, c = where_ref[1], where_ref[2], where_ref[3]
    return [(spot(at, 1 - y, core), spot(at, y, core)) for core in (c, 1 - c) for at in slot_places(z)]


def settle_kernel(chans, where_ref, *refs):
    pairs, (wm_ref, wo_ref, cw_ref, cb_ref, gg_ref, gin_ref, line_ref, sem) = refs[:8], refs[8:]
    rows = pairs[0].shape[0] // 2
    feat = wo_ref.shape[1]
    width = wm_ref.shape[1] - LANES
    inner = wo_ref.shape[0]
    last = width + inner
    copies = []
    for pair, owners in zip(pairs, owners_of(where_ref)):
        for half, owner in enumerate(owners):
            mine = pl.ds(half * rows, rows)
            to = pl.ds(pl.multiple_of(owner * rows, 16), rows)
            copies.append((pair.at[pl.ds(half * rows, 16), pl.ds(last + LANES, LANES)], line_ref.at[owner]))
            copies.append((pair.at[mine, pl.ds(0, width)], wm_ref.at[to, pl.ds(0, width)]))
            copies.append((pair.at[mine, pl.ds(last, LANES)], wm_ref.at[to, pl.ds(width, LANES)]))
            for b in range(inner // wm_ref.shape[0]):
                into = pl.ds(pl.multiple_of((owner * (inner // wm_ref.shape[0]) + b) * rows, 16), rows)
                copies.append((pair.at[mine, pl.ds(width + b * feat, feat)], wo_ref.at[into]))
    for source, target in copies:
        pltpu.make_async_copy(source, target, sem).start()
    for whole in (wm_ref, wo_ref, line_ref):
        pltpu.make_async_copy(whole, whole, sem).wait()
    lines = [line_ref[i].astype(F32)[0:8] for i in range(line_ref.shape[0])]
    for c, chunk in enumerate(lay(lines, chans, cw_ref.shape[1] // LANES)):
        cw_ref[:, cols(c)] = chunk[0:TAPS]
        cb_ref[:, cols(c)] = chunk[TAPS : TAPS + 1]
    for c, chunk in enumerate(lay(lines, inner // len(lines), gg_ref.shape[1] // LANES)):
        gg_ref[:, cols(c)] = chunk[TAPS + 1 : TAPS + 2]
    for c, chunk in enumerate(lay(lines, rows, gin_ref.shape[1] // LANES)):
        gin_ref[:, cols(c)] = chunk[TAPS + 2 : TAPS + 3]


def settle(where, pairs, width, chans, feat):
    rows, full = pairs[0].shape[0] // 2, pairs[0].shape[1]
    owners, inner = feat // rows, full - width - 2 * LANES
    return pl.pallas_call(
        functools.partial(settle_kernel, chans),
        in_specs=[SMEM_SPEC] + [HBM_SPEC] * 8,
        out_specs=[VMEM_SPEC] * 6,
        out_shape=(
            shape_of((feat, width + LANES), BF16),
            shape_of((inner, feat), BF16),
            shape_of((TAPS, owners * chans)),
            shape_of((1, owners * chans)),
            shape_of((1, inner)),
            shape_of((1, feat)),
        ),
        scratch_shapes=[pltpu.VMEM((owners, 16, LANES), BF16), pltpu.SemaphoreType.DMA],
        compiler_params=PARAMS,
        name="settle_weights",
    )(where, *pairs)


def slot_blocks(where_ref):
    owners = owners_of(where_ref)
    return [owner for slot in range(4) for pair in (owners[slot], owners[4 + slot]) for owner in pair]


def write_slot(slot, turned, mixed, gp_ref, gb_ref, gdt_ref, line_ref, out_refs, where_ref):
    rows, width, feat = turned.shape[0] // 16, gp_ref.shape[1], gb_ref.shape[1]
    blocks = mixed.shape[0] // turned.shape[0]
    last = width + blocks * feat
    mine = turned[4 * slot * rows : 4 * (slot + 1) * rows, :]

    def put(at, term):
        for part, (ref, to) in enumerate(out_refs):
            ref[to : to + rows, at] = term[part * rows : (part + 1) * rows].astype(BF16)

    for c in range(width // 256):
        put(cols(c, 256), dot_nn(mine, gp_ref[:, cols(c, 256)]))
    put(slice(last, last + LANES), dot_nn(mine, gdt_ref[...]))
    owners = slot_blocks(where_ref)[4 * slot : 4 * slot + 4]
    for part, owner in enumerate(owners):
        ref, to = out_refs[part]
        for b in range(blocks):
            start = ((4 * slot + part) * blocks + b) * rows
            at = slice(width + b * feat, width + (b + 1) * feat)
            ref[to : to + rows, at] = dot_nn(mixed[start : start + rows, :], gb_ref[...]).astype(BF16)
        line = line_ref[owner]
        ref[to : to + 16, last + LANES :] = jnp.concatenate([line, jnp.zeros_like(line)], axis=0).astype(BF16)
        ref[to + 16 : to + rows, last + LANES :] = jnp.zeros((rows - 16, LANES), BF16)


def turn_kernel(rows, where_ref, n_first, mix_first, n_last, mix_last, n_both, mix_both, turned_ref, mixed_ref, flat_ref, wide_ref):
    tok, feat = n_both.shape
    many = mix_both.shape[1] // feat * rows

    def early(one, other):
        return jnp.where(where_ref[0] == 0, one[...], other[...])

    flat_ref[:, :tok] = early(n_first, n_last).T
    flat_ref[:, tok:] = n_both[...].T
    wide_ref[:, :tok] = early(mix_first, mix_last).T
    wide_ref[:, tok:] = mix_both[...].T
    for i, owner in enumerate(slot_blocks(where_ref)):
        turned_ref[i * rows : (i + 1) * rows, :] = flat_ref[pl.ds(pl.multiple_of(owner * rows, 16), rows), :]
        mixed_ref[i * many : (i + 1) * many, :] = wide_ref[pl.ds(pl.multiple_of(owner * many, 16), many), :]


def turn(where, first, last, both, rows):
    tok, feat = both[0].shape
    inner = both[1].shape[1]
    return pl.pallas_call(
        functools.partial(turn_kernel, rows),
        in_specs=[SMEM_SPEC] + [VMEM_SPEC] * 6,
        out_specs=[VMEM_SPEC] * 2,
        out_shape=(shape_of((feat, 2 * tok), BF16), shape_of((inner, 2 * tok), BF16)),
        scratch_shapes=[pltpu.VMEM((feat, 2 * tok), BF16), pltpu.VMEM((inner, 2 * tok), BF16)],
        compiler_params=PARAMS,
        name="turn_rows",
    )(where, *first, *last, *both)


def first_weight_kernel(rows, chans, where_ref, turned_ref, mixed_ref, *refs):
    sources, smalls, outs, sems = refs[:12], refs[12:24], refs[24:33], refs[33]
    vec_ref, gp_ref, gb_ref, gdt_ref, line_ref = outs[4:]
    feat, inner = turned_ref.shape[0], mixed_ref.shape[0]
    tok = turned_ref.shape[1] // 2
    blocks = inner // feat
    into = [ref.at[part * tok : (part + 1) * tok] for part in range(2) for ref in (gp_ref, gb_ref, gdt_ref)]
    take(where_ref, [[(source, None) for source in sources[6 * i : 6 * i + 6]] for i in range(2)], into, sems)
    early = jnp.where(where_ref[0] == 0, 0.0, 1.0)
    sums = [one[...] + early * zero[...] + (1.0 - early) * two[...] for zero, one, two in zip(smalls[0::3], smalls[1::3], smalls[2::3])]
    vec_ref[...] = sums[3]
    pieces = [[total[:, cols(c)] for c in range(total.shape[1] // LANES)] for total in sums]
    row = lax.broadcasted_iota(jnp.int32, (8, LANES), 0)
    for i in range(feat // rows):
        block = cut(pieces[0], chans, i)
        block = jnp.where(row == TAPS + 1, jnp.broadcast_to(cut(pieces[1], blocks * rows, i)[0:1], block.shape), block)
        line_ref[i] = jnp.where(row == TAPS + 2, jnp.broadcast_to(cut(pieces[2], rows, i)[0:1], block.shape), block)
    taken(into, sems, 0, 1, 2, 3, 4, 5)
    write_slot(3, turned_ref, mixed_ref, gp_ref, gb_ref, gdt_ref, line_ref, [(ref, 0) for ref in outs[:4]], where_ref)


def rest_weight_kernel(where_ref, turned_ref, mixed_ref, gp_ref, gb_ref, gdt_ref, line_ref, *outs):
    for slot in (2, 1, 0):
        targets = [(ref, to) for ref in (outs[slot], outs[3 + slot]) for to in (0, outs[slot].shape[0] // 2)]
        write_slot(slot, turned_ref, mixed_ref, gp_ref, gb_ref, gdt_ref, line_ref, targets, where_ref)


def weight_terms(where, turned, one, other, smalls, rows, chans):
    feat, inner = turned[0].shape[0], turned[1].shape[0]
    tok, width = one[0].shape
    full = width + inner + 2 * LANES
    block, pair = shape_of((rows, full), BF16), shape_of((2 * rows, full), BF16)
    shared = (
        shape_of((2 * tok, width), BF16),
        shape_of((2 * tok, feat), BF16),
        shape_of((2 * tok, LANES), BF16),
        shape_of((feat // rows, 8, LANES)),
    )
    *blocks, vectors, gp, gb, gdt, lines = pl.pallas_call(
        functools.partial(first_weight_kernel, rows, chans),
        in_specs=[SMEM_SPEC] + [VMEM_SPEC] * 2 + [HBM_SPEC] * 12 + [VMEM_SPEC] * 12,
        out_specs=[VMEM_SPEC] * 9,
        out_shape=(block,) * 4 + (shape_of((8, LANES)),) + shared,
        scratch_shapes=[pltpu.SemaphoreType.DMA((6,))],
        compiler_params=PARAMS,
        name="weight_gradients_first",
    )(where, *turned, *one, *other, *smalls)

    def rest(after):
        outs = pl.pallas_call(
            rest_weight_kernel,
            in_specs=[SMEM_SPEC] + [VMEM_SPEC] * 6,
            out_specs=[VMEM_SPEC] * 6,
            out_shape=(pair,) * 6,
            compiler_params=PARAMS,
            name="weight_gradients_rest",
        )(where, *turned, behind(gp, after), gb, gdt, lines)
        return outs[:3], outs[3:]

    return blocks, vectors, rest


def unpack_kernel(own_ref, second_ref, near_ref, wm_ref, wo_ref, wdt_ref, cw_ref, cb_ref, gg_ref, ng_ref, square):
    rows, width = wm_ref.shape
    feat = wo_ref.shape[1]
    blocks = wo_ref.shape[0] // rows
    last = width + blocks * feat

    def total(at, count):
        some = slice(0, count)
        return own_ref[some, at] + (second_ref[some, at].astype(F32) + near_ref[some, at].astype(F32))

    for c in range(width // 256):
        wm_ref[:, cols(c, 256)] = total(cols(c, 256), rows)
    for b in range(blocks):
        wo_ref[b * rows : (b + 1) * rows, :] = total(slice(width + b * feat, width + (b + 1) * feat), rows)
    square[...] = jnp.zeros(square.shape, F32)
    square[:rows, :] = total(slice(last, last + LANES), rows)
    wdt_ref[...] = square[...].T[: wdt_ref.shape[0], :rows]
    line = total(slice(last + LANES, last + 2 * LANES), 16)
    cw_ref[...] = line[0:TAPS, : cw_ref.shape[1]]
    for k, ref in enumerate((cb_ref, gg_ref, ng_ref)):
        ref[...] = line[TAPS + k : TAPS + k + 1, : ref.shape[1]]


def unpack_sums(terms, wm, wo, wdt, cw, cb, gg, ng):
    return pl.pallas_call(
        unpack_kernel,
        out_shape=tuple(shape_of(part.shape) for part in (wm, wo, wdt, cw, cb, gg, ng)),
        scratch_shapes=[pltpu.VMEM((LANES, LANES), F32)],
        compiler_params=PARAMS,
        name="unpack_sums",
    )(*terms)


def small_rows(vectors, rows):
    flat = jnp.concatenate([vector.reshape(-1) for vector in vectors])
    lines = -(-flat.shape[0] // LANES)
    wide = -(-lines // rows)
    flat = jnp.pad(flat, (0, lines * LANES - flat.shape[0])).reshape(lines, LANES)
    flat = jnp.pad(flat, ((0, rows * wide - lines), (0, 0)))
    return flat.reshape(wide, rows, LANES).transpose(1, 0, 2).reshape(rows, wide * LANES)


def small_flat(block, owners):
    rows, wide = block.shape[0] // owners, block.shape[1] // LANES
    return block.reshape(owners, rows, wide, LANES).transpose(0, 2, 1, 3).reshape(owners, wide * rows * LANES)


def total_over(value, axis):
    count = lax.axis_size(axis)
    step = 1
    while step < count:
        value = value + lax.ppermute(value, axis, [(i, i ^ step) for i in range(count)])
        step = step * 2
    return value


def shards(inputs, segments, cotangent, norm_gain, w_main, w_dt, conv_weight, conv_bias, dt_bias, a_log, skip_d, gate_gain, w_out):
    first = lax.axis_index("section") == 0
    dp = lax.axis_size("dp")
    feat = inputs.shape[2]
    rows, width = w_main.shape[1:]
    heads = w_dt.shape[2]
    chans, own_inner = conv_weight.shape[2], gate_gain.shape[1]
    inner = own_inner * dp
    blocks = own_inner // rows

    owned = (w_main[0], w_out[0], jnp.swapaxes(w_dt[0], 0, 1), conv_weight[0], conv_bias, gate_gain, norm_gain)
    aligned = rows % 16 == 0 and dp == 4 * Z_CHIPS
    side = lax.axis_index("section")
    place = lax.axis_index("dp")
    where = jnp.stack([side, place // 4, place // 2 % 2, place % 2]).astype(jnp.int32)
    if aligned:
        wm, wo, cw, cb, gg, gin = settle(where, gather_slots(pack_shard(*owned)), width, chans, feat)
    else:
        small = small_rows((conv_weight[0], conv_bias[0], gate_gain[0], norm_gain[0]), rows)
        out_block = w_out[0].reshape(blocks, rows, feat).transpose(1, 0, 2).reshape(rows, inner)
        packed = jnp.concatenate([w_main[0], out_block, jnp.pad(w_dt[0], ((0, 0), (0, LANES - heads))), small], axis=1)
        whole = lax.all_gather(packed, "dp", axis=0, tiled=True)
    marks = [TAPS * chans, (TAPS + 1) * chans, (TAPS + 1) * chans + own_inner, (TAPS + 1) * chans + own_inner + rows]
    if not aligned:
        wm = jnp.concatenate([whole[:, :width], whole[:, width + inner : width + inner + LANES]], axis=1)
        wo = whole[:, width : width + inner].reshape(dp, rows, blocks, feat).transpose(0, 2, 1, 3).reshape(inner, feat)
        flat = small_flat(whole[:, width + inner + LANES :], dp).astype(F32)
        cw = flat[:, : marks[0]].reshape(dp, TAPS, chans).transpose(1, 0, 2).reshape(TAPS, dp * chans)
        cb = flat[:, marks[0] : marks[1]].reshape(1, dp * chans)
        gg = flat[:, marks[1] : marks[2]].reshape(1, inner)
        gin = flat[:, marks[2] : marks[3]].reshape(1, feat)
    hp = jnp.pad(jnp.concatenate([dt_bias, a_log], axis=0), ((0, 6), (0, LANES - heads)))
    sk = jnp.repeat(skip_d, inner // heads, axis=1)
    weights = (wm, wo, gin, cw, cb, gg, hp, sk)

    def choose(one, other):
        return jnp.where(first, one, other)

    up = down = [(0, 1), (1, 0)]
    ids = segments.astype(F32)[:, None, :]
    f0 = forward_layer(0, where, ids, weights, [(inputs, 0)])
    r0 = lax.ppermute(f0[0], "section", up)
    f1 = forward_layer(3, where, ids, weights, [(inputs, 1), (r0, None)])
    r1 = lax.ppermute(f1[0], "section", up)
    f2 = forward_layer(1, where, ids, weights, [(inputs, 1), (r1, None)])

    def stored(tick):
        return [(tick[i], None) for i in (2, 3, 4, 6, 7, 8)]

    kept = stored(f1)
    now = [[(cotangent, 0), (inputs, 1)] + kept, [(cotangent, 0), (r0, None)] + kept]
    b0 = backward_layer(0, where, ids, weights, now)
    d0 = lax.ppermute(b0[1], "section", down)
    now = [
        [(d0, None), (inputs, 0)] + stored(f0),
        [(cotangent, 1), (r1, None)] + stored(f2),
    ]
    b1 = backward_layer(2, where, ids, weights, now)
    d1 = lax.ppermute(b1[1], "section", down)
    if aligned:
        rows_of = (f0[1], f0[5]), (f2[1], f2[5]), (f1[1], behind(f1[5], b1[1]))
        turned = turn(where, *rows_of, rows)
    b2 = backward_layer(1, where, ids, weights, [[(d1, None), (inputs, 1)] + kept])
    dch, din, dgin, dhp = tuple(choose(two, zero) + one for zero, one, two in zip(b0[4:], b1[4:], b2[4:]))
    on_first = (f0[1], f0[5], b1[2], d0, b1[3]), (f1[1], f1[5], b2[2], d1, b2[3])
    on_last = (f2[1], f2[5], b1[2], cotangent[1], b1[3]), (f1[1], f1[5], b0[2], cotangent[0], b0[3])
    if aligned:
        smalls = [part[i] for i in (4, 5, 6, 7) for part in (b0, b1, b2)]
        one, other = (pair[0][2:] + pair[1][2:] for pair in (on_first, on_last))
        first_blocks, vectors, rest = weight_terms(where, turned, one, other, smalls, rows, chans)
    else:
        n, mix, gp, gb, gdt = tuple(
            jnp.concatenate([choose(on_first[0][i], on_last[0][i]), choose(on_first[1][i], on_last[1][i])], axis=0) for i in range(5)
        )
        own = [
            small_rows(
                (
                    dch[:TAPS, i * chans : (i + 1) * chans],
                    dch[TAPS, i * chans : (i + 1) * chans],
                    din[0, i * own_inner : (i + 1) * own_inner],
                    dgin[0, i * rows : (i + 1) * rows],
                ),
                rows,
            )
            for i in range(dp)
        ]
        wide = dot_tn(mix, gb).reshape(dp, blocks, rows, feat).transpose(0, 2, 1, 3).reshape(feat, inner)
        parts = [dot_tn(n, gp), wide, dot_tn(n, gdt), jnp.concatenate(own, axis=0)]
        packed_grad = jnp.concatenate([part.astype(BF16) for part in parts], axis=1)
    if aligned:
        terms, vectors, started = scatter_slots(first_blocks, rest, vectors)
        heads_sum = vectors[:, :heads]
    else:
        summed = lax.psum_scatter(packed_grad, "dp", scatter_dimension=0, tiled=True)
        heads_sum = total_over(dhp[:3, :heads], "dp")
        started = summed
    if aligned:
        g_main, g_out, g_dt, g_cw, g_cb, g_gg, g_ng = unpack_sums(terms, *owned)
        g_dt = jnp.swapaxes(g_dt, 0, 1)
    else:
        summed = summed.astype(F32)
        got = small_flat(summed[:, width + inner + LANES :], 1)[0]
        g_main = summed[:, :width]
        g_out = summed[:, width : width + inner].reshape(rows, blocks, feat).transpose(1, 0, 2).reshape(own_inner, feat)
        g_dt = summed[:, width + inner : width + inner + heads]
        g_cw = got[: marks[0]].reshape(TAPS, chans)
        g_cb, g_gg, g_ng = (got[None, marks[i] : marks[i + 1]] for i in range(3))
    outs = [part[0] for part in (f0, f1, f2, b0, b1, b2)]
    outs = lax.optimization_barrier((*outs, started))
    hidden = jnp.stack([choose(outs[0], outs[1]), choose(outs[1], outs[2])])[None]
    grad_inputs = jnp.stack([choose(outs[4], outs[3]), choose(outs[5], outs[4])])[None]
    return (
        hidden,
        grad_inputs,
        g_ng,
        g_main[None],
        g_dt[None],
        g_cw[None],
        g_cb,
        heads_sum[0:1],
        heads_sum[1:2],
        heads_sum[2:3],
        g_gg,
        g_out[None],
    )


def solution(mesh):
    placed = (
        P(None, "dp", None),
        P(None, "dp"),
        P(None, "dp", None),
        P("section", "dp"),
        P("section", "dp", None),
        P("section", "dp", None),
        P("section", None, "dp"),
        P("section", "dp"),
        P("section", None),
        P("section", None),
        P("section", None),
        P("section", "dp"),
        P("section", "dp", None),
    )
    return jax.shard_map(
        shards,
        mesh=mesh,
        in_specs=placed,
        out_specs=(
            P("section", None, "dp", None),
            P("section", None, "dp", None),
            P("section", "dp"),
            P("section", "dp", None),
            P("section", "dp", None),
            P("section", None, "dp"),
            P("section", "dp"),
            P("section", None),
            P("section", None),
            P("section", None),
            P("section", "dp"),
            P("section", "dp", None),
        ),
        check_vma=False,
    )
```

```python
import functools

import jax
import jax.numpy as jnp
from jax import lax
from jax.experimental import pallas as pl
from jax.experimental.pallas import tpu as pltpu
from jax.sharding import PartitionSpec as P

norm_eps = 1e-05
F32 = jnp.float32
BF16 = jnp.bfloat16
LANES = 128
TAPS = 4
VMEM_BYTES = 28 * 1024 * 1024


def dot_nn(a, b):
    return lax.dot_general(a, b, (((1,), (0,)), ((), ())), preferred_element_type=F32)


def dot_nt(a, b):
    return lax.dot_general(a, b, (((1,), (1,)), ((), ())), preferred_element_type=F32)


def dot_tn(a, b):
    return lax.dot_general(a, b, (((0,), (0,)), ((), ())), preferred_element_type=F32)


def split(a):
    high = a.astype(BF16)
    return high, (a - high.astype(F32)).astype(BF16)


def exact(dot, a, b):
    ah, al = split(a)
    bh, bl = split(b)
    return dot(ah, bh) + (dot(ah, bl) + dot(al, bh))


def near(dot, a, b):
    return exact(dot, a, b)


def triangle(lower):
    rows = lax.broadcasted_iota(jnp.int32, (LANES, LANES), 0)
    cols = lax.broadcasted_iota(jnp.int32, (LANES, LANES), 1)
    return jnp.where(rows >= cols if lower else rows <= cols, 1.0, 0.0).astype(BF16)


def running(tri, a):
    high = a.astype(BF16)
    rest = a - high.astype(F32)
    mid = rest.astype(BF16)
    low = (rest - mid.astype(F32)).astype(BF16)
    return dot_nn(tri, high) + (dot_nn(tri, mid) + dot_nn(tri, low))


def sigmoid(a):
    return 0.5 * jnp.tanh(0.5 * a) + 0.5


def softplus(a):
    return jnp.maximum(a, 0.0) + jnp.log1p(jnp.exp(-jnp.abs(a)))


def cols(j, width=LANES):
    return slice(j * width, (j + 1) * width)


def token_masks(ids):
    length = ids.shape[1]
    across = jnp.broadcast_to(ids, (length, length))
    wide = across.T
    rows = lax.broadcasted_iota(jnp.int32, (length, length), 0)
    lane = lax.broadcasted_iota(jnp.int32, (length, length), 1)
    linked = jnp.where((rows >= lane) & (wide == across), 1.0, 0.0)
    sees = [None]
    for k in range(1, TAPS):
        sees.append(jnp.where((rows >= k) & (pltpu.roll(wide, k, 0) == wide), 1.0, 0.0))
    return linked, sees


def take(which_ref, choices, into, sems):
    def start(choice):
        for i, ((ref, index), target) in enumerate(zip(choice, into)):
            pltpu.make_async_copy(ref if index is None else ref.at[index], target, sems.at[i]).start()

    if len(choices) == 1:
        start(choices[0])
        return
    for number, choice in enumerate(choices):
        pl.when(which_ref[0] == number)(functools.partial(start, choice))


def taken(into, sems, *numbers):
    for i in numbers:
        pltpu.make_async_copy(into[i], into[i], sems.at[i]).wait()


def conv_taps(v, sees):
    return [v] + [sees[k] * pltpu.roll(v, k, 0) for k in range(1, TAPS)]


def conv_sum(taps, cw_ref, cb_ref, at):
    total = cb_ref[:, at] + cw_ref[TAPS - 1 : TAPS, at] * taps[0]
    for k in range(1, TAPS):
        total = total + cw_ref[TAPS - 1 - k : TAPS - k, at] * taps[k]
    return total


def pair_of(values, j):
    lane = lax.broadcasted_iota(jnp.int32, (values.shape[0], LANES), 1)
    first = jnp.broadcast_to(values[:, 2 * j : 2 * j + 1], lane.shape)
    second = jnp.broadcast_to(values[:, 2 * j + 1 : 2 * j + 2], lane.shape)
    return jnp.where(lane < LANES // 2, first, second)


def halves(values):
    lane = lax.broadcasted_iota(jnp.int32, values.shape, 1)
    low = jnp.where(lane < LANES // 2, values, 0.0)
    return jnp.concatenate([low, values - low], axis=0)


def decay(cum, cum_t, linked, h):
    spread = cum[:, h : h + 1] - cum_t[h : h + 1, :]
    return linked * jnp.exp(jnp.minimum(spread, 0.0))


def micro_of(which_ref, mode):
    return (0, 1, which_ref[0], 1 - which_ref[0])[mode]


def held(which_ref, options, indices):
    refs = [ref if index is None else ref.at[index] for ref, index in zip(options, indices)]

    def read(at=slice(None)):
        values = [ref[:, at] for ref in refs]
        return values[0] if len(values) == 1 else jnp.where(which_ref[0] == 0, values[0], values[1])

    return read


KEPT = 8


def fwd_kernel(plan, mode, which_ref, ids_ref, wm_ref, wo_ref, gin_ref, cw_ref, cb_ref, gg_ref, hp_ref, sk_ref, *refs):
    sources, refs = refs[: len(plan)], refs[len(plan) :]
    v_ref, n_ref, p_ref, dtr_ref, y_ref, mix_ref, total_ref, g_ref, r2_ref = refs
    inner, width = gg_ref.shape[1], p_ref.shape[1]
    pairs = inner // LANES
    linked, sees = token_masks(ids_ref[micro_of(which_ref, mode)])
    u = held(which_ref, sources, plan)().astype(F32)
    r = lax.rsqrt(jnp.mean(u * u, axis=-1, keepdims=True) + norm_eps)
    n = (u * r * gin_ref[...]).astype(BF16)
    n_ref[...] = n
    for c in range(width // 256):
        p_ref[:, cols(c, 256)] = dot_nn(n, wm_ref[:, cols(c, 256)])
    dtr = dot_nn(n, wm_ref[:, width:])
    dtr_ref[...] = dtr

    def conv(j):
        total = conv_sum(conv_taps(p_ref[:, inner + j * LANES : inner + (j + 1) * LANES], sees), cw_ref, cb_ref, cols(j))
        total_ref[:, cols(j)] = total
        return total * sigmoid(total)

    b_state = conv(pairs)
    c_state = conv(pairs + 1)
    cross = exact(dot_nt, c_state, b_state)
    dt = softplus(dtr + hp_ref[0:1, :])
    cum = running(triangle(True), -dt * jnp.exp(hp_ref[1:2, :]))
    cum_t = cum.T
    squares = jnp.zeros((u.shape[0], LANES), F32)
    for j in range(pairs):
        at = cols(j)
        x = conv(j)
        m = jnp.concatenate([cross * decay(cum, cum_t, linked, 2 * j), cross * decay(cum, cum_t, linked, 2 * j + 1)], axis=1)
        y = near(dot_nn, m, halves(x * pair_of(dt, j))) + sk_ref[:, at] * x
        y_ref[:, at] = y
        z = p_ref[:, at]
        g = y * (z * sigmoid(z))
        g_ref[:, at] = g
        squares = squares + g * g
    r2 = lax.rsqrt(jnp.sum(squares, axis=-1, keepdims=True) / inner + norm_eps)
    for j in range(pairs):
        at = cols(j)
        mix_ref[:, at] = (g_ref[:, at] * r2 * gg_ref[:, at]).astype(BF16)
    r2_ref[...] = jnp.broadcast_to(r2, r2_ref.shape)
    mixed = mix_ref[...]
    for c in range(u.shape[1] // 256):
        at = cols(c, 256)
        v_ref[:, at] = (u[:, at] + dot_nn(mixed, wo_ref[:, at])).astype(BF16)


def bwd_kernel(plan, mode, which_ref, ids_ref, wm_ref, wo_ref, gin_ref, cw_ref, cb_ref, gg_ref, hp_ref, sk_ref, *refs):
    count = KEPT * len(plan)
    sources, refs = refs[:count], refs[count:]
    gi_ref, gl_ref, gp_ref, gdt_ref, dch_ref, din_ref, dgin_ref, dhp_ref, gm_scr = refs
    gv, u_low, p, dtr, y_kept, totals, g_kept, r2_kept = [
        held(which_ref, [sources[KEPT * k + i] for k in range(len(plan))], [indices[i] for indices in plan]) for i in range(KEPT)
    ]
    dch_ref[...] = jnp.zeros(dch_ref.shape, F32)
    din_ref[...] = jnp.zeros(din_ref.shape, F32)
    inner = gg_ref.shape[1]
    pairs = inner // LANES
    length = gm_scr.shape[0]
    linked, sees = token_masks(ids_ref[micro_of(which_ref, mode)])
    gb = gv()
    inners = jnp.zeros((length, 256), F32)
    for c in range(inner // 256):
        at = cols(c, 256)
        gm = dot_nt(gb, wo_ref[at, :])
        gm_scr[:, at] = gm
        inners = inners + gm * gg_ref[:, at] * g_kept(at)
    r2 = r2_kept()[:, 0:1]
    pull = r2 * r2 * r2 * (jnp.sum(inners, axis=-1, keepdims=True) / inner)

    def conv(j):
        total = totals(cols(j))
        return total, sigmoid(total)

    def conv_back(j, total, sig, grad):
        at = cols(j)
        v = p(slice(inner + j * LANES, inner + (j + 1) * LANES))
        ds = grad * (sig * (1.0 + total * (1.0 - sig)))
        dch_ref[TAPS : TAPS + 1, at] = jnp.sum(ds, axis=0, keepdims=True)
        dch_ref[TAPS - 1 : TAPS, at] = jnp.sum(ds * v, axis=0, keepdims=True)
        dv = cw_ref[TAPS - 1 : TAPS, at] * ds
        for k in range(1, TAPS):
            row = slice(TAPS - 1 - k, TAPS - k)
            moved = pltpu.roll(sees[k] * ds, length - k, 0)
            dch_ref[row, at] = jnp.sum(moved * v, axis=0, keepdims=True)
            dv = dv + cw_ref[row, at] * moved
        gp_ref[:, inner + j * LANES : inner + (j + 1) * LANES] = dv.astype(BF16)

    sb, gb_sig = conv(pairs)
    b_state = sb * gb_sig
    sc, gc_sig = conv(pairs + 1)
    c_state = sc * gc_sig
    cross = exact(dot_nt, c_state, b_state)
    dt_arg = dtr() + hp_ref[0:1, :]
    dt = softplus(dt_arg)
    rate = jnp.exp(hp_ref[1:2, :])
    cum = running(triangle(True), -dt * rate)
    cum_t = cum.T
    dcross = jnp.zeros((length, length), F32)
    dcum = jnp.zeros((length, LANES), F32)
    ddt = jnp.zeros((length, LANES), F32)
    dskip = jnp.zeros((8, LANES), F32)
    lane = lax.broadcasted_iota(jnp.int32, (2 * LANES, LANES), 1)
    row = lax.broadcasted_iota(jnp.int32, (2 * LANES, LANES), 0)
    half = jnp.where((row % LANES) < LANES // 2, 0, 1)
    for j in range(pairs):
        at = cols(j)
        pick = jnp.where(lane == 2 * j + half, 1.0, 0.0).astype(BF16)
        gm = gm_scr[:, at]
        g = g_kept(at)
        din_ref[0:1, at] = jnp.sum(gm * (g * r2), axis=0, keepdims=True)
        dg = gm * gg_ref[:, at] * r2 - g * pull
        z = p(at)
        sig = sigmoid(z)
        y = y_kept(at)
        dy = dg * (z * sig)
        gp_ref[:, at] = (dg * y * (sig * (1.0 + z * (1.0 - sig)))).astype(BF16)
        total, tsig = conv(j)
        x = total * tsig
        dtp = pair_of(dt, j)
        xw = x * dtp
        dy_st = halves(dy)
        l1 = decay(cum, cum_t, linked, 2 * j)
        l2 = decay(cum, cum_t, linked, 2 * j + 1)
        dm = dot_nt(dy_st.astype(BF16), xw.astype(BF16))
        dcross = dcross + dm[:length] * l1 + dm[length:] * l2
        m = jnp.concatenate([cross * l1, cross * l2], axis=0)
        dxw = near(dot_tn, m, dy_st)
        skip = sk_ref[:, at]
        lanes = jnp.broadcast_to(jnp.sum(dy * x, axis=0, keepdims=True), (8, LANES))
        dskip = dskip + dot_nn(jnp.concatenate(split(lanes), axis=1), pick)
        q = dy * (y - skip * x) - dxw * xw
        dcum = dcum + dot_nn(jnp.concatenate(split(q), axis=1), pick)
        ddt = ddt + dot_nn(jnp.concatenate(split(dxw * x), axis=1), pick)
        conv_back(j, total, tsig, skip * dy + dxw * dtp)
    conv_back(pairs, sb, gb_sig, exact(dot_tn, dcross, c_state))
    conv_back(pairs + 1, sc, gc_sig, exact(dot_nn, dcross, b_state))
    dlog = running(triangle(False), dcum)
    draw = (ddt - rate * dlog) * sigmoid(dt_arg)
    gdt = draw.astype(BF16)
    gdt_ref[...] = gdt
    dhp_ref[0:1, :] = jnp.sum(draw, axis=0, keepdims=True)
    dhp_ref[1:2, :] = jnp.sum(dlog * (-dt * rate), axis=0, keepdims=True)
    dhp_ref[2:3, :] = dskip[0:1]
    dhp_ref[3:8, :] = jnp.zeros((5, LANES), F32)
    u = u_low().astype(F32)
    gin = gin_ref[...]
    r = lax.rsqrt(jnp.mean(u * u, axis=-1, keepdims=True) + norm_eps)
    gp = gp_ref[...]
    width = gp.shape[1]
    gn = jnp.concatenate(
        [dot_nt(gp, wm_ref[cols(c, 256), :width]) + dot_nt(gdt, wm_ref[cols(c, 256), width:]) for c in range(u.shape[1] // 256)], axis=1
    )
    dgin_ref[...] = jnp.broadcast_to(jnp.sum(gn * (u * r), axis=0, keepdims=True), dgin_ref.shape)
    gng = gn * gin
    back = r * r * r * jnp.mean(gng * u, axis=-1, keepdims=True)
    grad = gb.astype(F32) + (gng * r - u * back)
    gi_ref[...] = grad
    gl_ref[...] = grad.astype(BF16)


def shape_of(shape, dtype=F32):
    return jax.ShapeDtypeStruct(shape, dtype)


VMEM_SPEC = pl.BlockSpec(memory_space=pltpu.VMEM)
HBM_SPEC = pl.BlockSpec(memory_space=pltpu.HBM)
SMEM_SPEC = pl.BlockSpec(memory_space=pltpu.SMEM)
PARAMS = pltpu.CompilerParams(vmem_limit_bytes=VMEM_BYTES)


def layer_sizes(weights):
    return weights[0].shape[0], weights[1].shape[0], weights[0].shape[1] - LANES


def forward_layer(mode, which, ids, weights, choices):
    tok = ids.shape[2]
    feat, inner, width = layer_sizes(weights)
    return pl.pallas_call(
        functools.partial(fwd_kernel, tuple(index for _, index in choices), mode),
        in_specs=[SMEM_SPEC] + [VMEM_SPEC] * (9 + len(choices)),
        out_specs=[VMEM_SPEC] * 9,
        out_shape=(
            shape_of((tok, feat), BF16),
            shape_of((tok, feat), BF16),
            shape_of((tok, width)),
            shape_of((tok, LANES)),
            shape_of((tok, inner)),
            shape_of((tok, inner), BF16),
            shape_of((tok, width - inner)),
            shape_of((tok, inner)),
            shape_of((tok, LANES)),
        ),
        compiler_params=PARAMS,
        name="layer_forward",
    )(which, ids, *weights, *[source for source, _ in choices])


def backward_layer(mode, which, ids, weights, choices):
    tok = ids.shape[2]
    feat, inner, width = layer_sizes(weights)
    return pl.pallas_call(
        functools.partial(bwd_kernel, tuple(tuple(index for _, index in choice) for choice in choices), mode),
        in_specs=[SMEM_SPEC] + [VMEM_SPEC] * (9 + KEPT * len(choices)),
        out_specs=[VMEM_SPEC] * 8,
        out_shape=(
            shape_of((tok, feat)),
            shape_of((tok, feat), BF16),
            shape_of((tok, width), BF16),
            shape_of((tok, LANES), BF16),
            shape_of((8, width - inner)),
            shape_of((8, inner)),
            shape_of((8, feat)),
            shape_of((8, LANES)),
        ),
        scratch_shapes=[pltpu.VMEM((tok, inner), F32)],
        compiler_params=PARAMS,
        name="layer_backward",
    )(which, ids, *weights, *[source for choice in choices for source, _ in choice])


def lay(blocks, size, chunks):
    lane = lax.broadcasted_iota(jnp.int32, (8, LANES), 1)
    out = [jnp.zeros((8, LANES), F32) for _ in range(chunks)]
    for i, block in enumerate(blocks):
        chunk, shift = (i * size) // LANES, (i * size) % LANES
        turned = pltpu.roll(block, shift, 1) if shift else block
        out[chunk] = jnp.where((lane >= shift) & (lane < shift + size), turned, out[chunk])
        if shift + size > LANES:
            out[chunk + 1] = jnp.where(lane < shift + size - LANES, turned, out[chunk + 1])
    return out


def cut(chunks, size, i):
    lane = lax.broadcasted_iota(jnp.int32, (8, LANES), 1)
    chunk, shift = (i * size) // LANES, (i * size) % LANES
    turn = (LANES - shift) % LANES
    block = pltpu.roll(chunks[chunk], turn, 1) if turn else chunks[chunk]
    if shift + size > LANES:
        block = jnp.where(lane < LANES - shift, block, pltpu.roll(chunks[chunk + 1], turn, 1))
    return jnp.where(lane < size, block, 0.0)


def pack_kernel(wm_ref, wo_ref, wdt_ref, cw_ref, cb_ref, gg_ref, ng_ref, out_ref, line, square):
    rows, width = wm_ref.shape
    feat = wo_ref.shape[1]
    blocks = wo_ref.shape[0] // rows
    out_ref[:, :width] = wm_ref[...]
    for b in range(blocks):
        out_ref[:, width + b * feat : width + (b + 1) * feat] = wo_ref[b * rows : (b + 1) * rows, :]
    last = width + blocks * feat
    out_ref[:, last + LANES :] = jnp.zeros((rows, LANES), BF16)
    square[...] = jnp.zeros(square.shape, F32)
    square[: wdt_ref.shape[0], :rows] = wdt_ref[...].astype(F32)
    out_ref[:, last : last + LANES] = square[...].T[:rows].astype(BF16)
    line[...] = jnp.zeros(line.shape, F32)
    line[0:TAPS, : cw_ref.shape[1]] = cw_ref[...].astype(F32)
    for k, ref in enumerate((cb_ref, gg_ref, ng_ref)):
        line[TAPS + k : TAPS + k + 1, : ref.shape[1]] = ref[...].astype(F32)
    out_ref[0:16, last + LANES :] = line[...].astype(BF16)


def pack_shard(wm, wo, wdt, cw, cb, gg, ng):
    rows, width = wm.shape
    full = width + wo.shape[0] // rows * wo.shape[1] + 2 * LANES
    return pl.pallas_call(
        pack_kernel,
        out_shape=shape_of((rows, full), BF16),
        scratch_shapes=[pltpu.VMEM((16, LANES), F32), pltpu.VMEM((LANES, LANES), F32)],
        compiler_params=pltpu.CompilerParams(vmem_limit_bytes=2 * VMEM_BYTES),
        name="pack_shard",
    )(wm, wo, wdt, cw, cb, gg, ng)


Z_CHIPS = 4


def spot(z, y, c):
    return (z * 2 + y) * 2 + c


def routed(value, move):
    pairs = []
    for z in range(Z_CHIPS):
        for y in range(2):
            for c in range(2):
                target = move(z, y, c)
                if target is not None:
                    pairs.append((spot(z, y, c), spot(*target)))
    return lax.ppermute(value, "dp", pairs)


def to_core(z, y, c):
    return z, y, 1 - c


def to_y(z, y, c):
    return z, 1 - y, c


def to_near(z, y, c):
    return z ^ 1, y, c


def to_middle(z, y, c):
    return (3 - z, y, c) if z in (1, 2) else None


def slot_places(z):
    return (z, z + 1 - 2 * lax.rem(z, 2), jnp.where(z < 2, 2, 1), jnp.where(z < 2, 3, 0))


def behind(value, other):
    return lax.optimization_barrier((value, other))[0]


def gather_slots(own):
    def pair(block, across):
        return jnp.concatenate([across, block], axis=0)

    near, second, own_y = lax.optimization_barrier((routed(own, to_near), routed(own, to_middle), routed(own, to_y)))
    own_pair = pair(own, own_y)
    last, ends, near_y = lax.optimization_barrier((routed(near, to_middle), routed(second, to_near), routed(near, to_y)))
    second = second + ends
    near_pair = pair(near, near_y)
    own_core = routed(behind(own_pair, ends), to_core)
    ends, second_y = lax.optimization_barrier((routed(last, to_near), routed(second, to_y)))
    last = last + ends
    second_pair = pair(second, second_y)
    near_core = routed(behind(near_pair, ends), to_core)
    second_core = routed(second_pair, to_core)
    last_pair = pair(last, routed(last, to_y))
    return [own_pair, near_pair, second_pair, last_pair, own_core, near_core, second_core, routed(last_pair, to_core)]


def scatter_slots(first_blocks, rest, vectors):
    rows = first_blocks[0].shape[0]

    def met(kept, value):
        total = kept.astype(F32) + value.astype(F32)
        return total[:rows].astype(BF16), total[rows:]

    def low(value):
        return value.astype(BF16)

    def summed(step):
        return vectors + lax.ppermute(vectors, "dp", [(i, i ^ step) for i in range(4 * Z_CHIPS)])

    kept_far, kept_near, sent_far, sent_near = first_blocks
    far = low(kept_far.astype(F32) + routed(sent_far, to_core).astype(F32))
    last = kept_near.astype(F32) + routed(behind(sent_near, far), to_core).astype(F32)
    kept, sent = rest(far)
    came = routed(far, to_y)
    vectors = behind(vectors, far)
    vectors = summed(1)
    over = [routed(block, to_core) for block in sent]
    far, second = met(kept[2], over[2])
    came, vectors = lax.optimization_barrier((came, vectors))
    came, last = routed(behind(far, came), to_y), last + came.astype(F32)
    line = routed(low(last), to_near)
    vectors = summed(2)
    far, near = met(kept[1], over[1])
    came, line, vectors = lax.optimization_barrier((came, line, vectors))
    last, second = last + line.astype(F32), second + came.astype(F32)
    came, line, ends = routed(behind(far, came), to_y), routed(low(last), to_middle), routed(low(second), to_near)
    vectors = summed(4)
    far, own = met(kept[0], over[0])
    came, line, ends, vectors = lax.optimization_barrier((came, line, ends, vectors))
    near, second = near + came.astype(F32) + line.astype(F32), second + ends.astype(F32)
    started = came
    came = routed(behind(far, came), to_y)
    near, second = routed(low(near), to_near), routed(low(second), to_middle)
    vectors = summed(8)
    return (own + came.astype(F32), second, near), vectors, started


def owners_of(where_ref):
    z, y, c = where_ref[1], where_ref[2], where_ref[3]
    return [(spot(at, 1 - y, core), spot(at, y, core)) for core in (c, 1 - c) for at in slot_places(z)]


def settle_kernel(chans, where_ref, *refs):
    pairs, (wm_ref, wo_ref, cw_ref, cb_ref, gg_ref, gin_ref, line_ref, sem) = refs[:8], refs[8:]
    rows = pairs[0].shape[0] // 2
    feat = wo_ref.shape[1]
    width = wm_ref.shape[1] - LANES
    inner = wo_ref.shape[0]
    last = width + inner
    copies = []
    for pair, owners in zip(pairs, owners_of(where_ref)):
        for half, owner in enumerate(owners):
            mine = pl.ds(half * rows, rows)
            to = pl.ds(pl.multiple_of(owner * rows, 16), rows)
            copies.append((pair.at[pl.ds(half * rows, 16), pl.ds(last + LANES, LANES)], line_ref.at[owner]))
            copies.append((pair.at[mine, pl.ds(0, width)], wm_ref.at[to, pl.ds(0, width)]))
            copies.append((pair.at[mine, pl.ds(last, LANES)], wm_ref.at[to, pl.ds(width, LANES)]))
            for b in range(inner // wm_ref.shape[0]):
                into = pl.ds(pl.multiple_of((owner * (inner // wm_ref.shape[0]) + b) * rows, 16), rows)
                copies.append((pair.at[mine, pl.ds(width + b * feat, feat)], wo_ref.at[into]))
    for source, target in copies:
        pltpu.make_async_copy(source, target, sem).start()
    for whole in (wm_ref, wo_ref, line_ref):
        pltpu.make_async_copy(whole, whole, sem).wait()
    lines = [line_ref[i].astype(F32)[0:8] for i in range(line_ref.shape[0])]
    for c, chunk in enumerate(lay(lines, chans, cw_ref.shape[1] // LANES)):
        cw_ref[:, cols(c)] = chunk[0:TAPS]
        cb_ref[:, cols(c)] = chunk[TAPS : TAPS + 1]
    for c, chunk in enumerate(lay(lines, inner // len(lines), gg_ref.shape[1] // LANES)):
        gg_ref[:, cols(c)] = chunk[TAPS + 1 : TAPS + 2]
    for c, chunk in enumerate(lay(lines, rows, gin_ref.shape[1] // LANES)):
        gin_ref[:, cols(c)] = chunk[TAPS + 2 : TAPS + 3]


def settle(where, pairs, width, chans, feat):
    rows, full = pairs[0].shape[0] // 2, pairs[0].shape[1]
    owners, inner = feat // rows, full - width - 2 * LANES
    return pl.pallas_call(
        functools.partial(settle_kernel, chans),
        in_specs=[SMEM_SPEC] + [HBM_SPEC] * 8,
        out_specs=[VMEM_SPEC] * 6,
        out_shape=(
            shape_of((feat, width + LANES), BF16),
            shape_of((inner, feat), BF16),
            shape_of((TAPS, owners * chans)),
            shape_of((1, owners * chans)),
            shape_of((1, inner)),
            shape_of((1, feat)),
        ),
        scratch_shapes=[pltpu.VMEM((owners, 16, LANES), BF16), pltpu.SemaphoreType.DMA],
        compiler_params=PARAMS,
        name="settle_weights",
    )(where, *pairs)


def slot_blocks(where_ref):
    owners = owners_of(where_ref)
    return [owner for slot in range(4) for pair in (owners[slot], owners[4 + slot]) for owner in pair]


def write_slot(slot, turned, mixed, gp_ref, gb_ref, gdt_ref, line_ref, out_refs, where_ref):
    rows, width, feat = turned.shape[0] // 16, gp_ref.shape[1], gb_ref.shape[1]
    blocks = mixed.shape[0] // turned.shape[0]
    last = width + blocks * feat
    mine = turned[4 * slot * rows : 4 * (slot + 1) * rows, :]

    def put(at, term):
        for part, (ref, to) in enumerate(out_refs):
            ref[to : to + rows, at] = term[part * rows : (part + 1) * rows].astype(BF16)

    for c in range(width // 256):
        put(cols(c, 256), dot_nn(mine, gp_ref[:, cols(c, 256)]))
    put(slice(last, last + LANES), dot_nn(mine, gdt_ref[...]))
    owners = slot_blocks(where_ref)[4 * slot : 4 * slot + 4]
    for part, owner in enumerate(owners):
        ref, to = out_refs[part]
        for b in range(blocks):
            start = ((4 * slot + part) * blocks + b) * rows
            at = slice(width + b * feat, width + (b + 1) * feat)
            ref[to : to + rows, at] = dot_nn(mixed[start : start + rows, :], gb_ref[...]).astype(BF16)
        line = line_ref[owner]
        ref[to : to + 16, last + LANES :] = jnp.concatenate([line, jnp.zeros_like(line)], axis=0).astype(BF16)
        ref[to + 16 : to + rows, last + LANES :] = jnp.zeros((rows - 16, LANES), BF16)


def turn_kernel(rows, where_ref, n_first, mix_first, n_last, mix_last, n_both, mix_both, turned_ref, mixed_ref, flat_ref, wide_ref):
    tok, feat = n_both.shape
    many = mix_both.shape[1] // feat * rows

    def early(one, other):
        return jnp.where(where_ref[0] == 0, one[...], other[...])

    flat_ref[:, :tok] = early(n_first, n_last).T
    flat_ref[:, tok:] = n_both[...].T
    wide_ref[:, :tok] = early(mix_first, mix_last).T
    wide_ref[:, tok:] = mix_both[...].T
    for i, owner in enumerate(slot_blocks(where_ref)):
        turned_ref[i * rows : (i + 1) * rows, :] = flat_ref[pl.ds(pl.multiple_of(owner * rows, 16), rows), :]
        mixed_ref[i * many : (i + 1) * many, :] = wide_ref[pl.ds(pl.multiple_of(owner * many, 16), many), :]


def turn(where, first, last, both, rows):
    tok, feat = both[0].shape
    inner = both[1].shape[1]
    return pl.pallas_call(
        functools.partial(turn_kernel, rows),
        in_specs=[SMEM_SPEC] + [VMEM_SPEC] * 6,
        out_specs=[VMEM_SPEC] * 2,
        out_shape=(shape_of((feat, 2 * tok), BF16), shape_of((inner, 2 * tok), BF16)),
        scratch_shapes=[pltpu.VMEM((feat, 2 * tok), BF16), pltpu.VMEM((inner, 2 * tok), BF16)],
        compiler_params=PARAMS,
        name="turn_rows",
    )(where, *first, *last, *both)


def first_weight_kernel(rows, chans, where_ref, turned_ref, mixed_ref, *refs):
    sources, smalls, outs, sems = refs[:12], refs[12:24], refs[24:33], refs[33]
    vec_ref, gp_ref, gb_ref, gdt_ref, line_ref = outs[4:]
    feat, inner = turned_ref.shape[0], mixed_ref.shape[0]
    tok = turned_ref.shape[1] // 2
    blocks = inner // feat
    into = [ref.at[part * tok : (part + 1) * tok] for part in range(2) for ref in (gp_ref, gb_ref, gdt_ref)]
    take(where_ref, [[(source, None) for source in sources[6 * i : 6 * i + 6]] for i in range(2)], into, sems)
    early = jnp.where(where_ref[0] == 0, 0.0, 1.0)
    sums = [one[...] + early * zero[...] + (1.0 - early) * two[...] for zero, one, two in zip(smalls[0::3], smalls[1::3], smalls[2::3])]
    vec_ref[...] = sums[3]
    pieces = [[total[:, cols(c)] for c in range(total.shape[1] // LANES)] for total in sums]
    row = lax.broadcasted_iota(jnp.int32, (8, LANES), 0)
    for i in range(feat // rows):
        block = cut(pieces[0], chans, i)
        block = jnp.where(row == TAPS + 1, jnp.broadcast_to(cut(pieces[1], blocks * rows, i)[0:1], block.shape), block)
        line_ref[i] = jnp.where(row == TAPS + 2, jnp.broadcast_to(cut(pieces[2], rows, i)[0:1], block.shape), block)
    taken(into, sems, 0, 1, 2, 3, 4, 5)
    write_slot(3, turned_ref, mixed_ref, gp_ref, gb_ref, gdt_ref, line_ref, [(ref, 0) for ref in outs[:4]], where_ref)


def rest_weight_kernel(where_ref, turned_ref, mixed_ref, gp_ref, gb_ref, gdt_ref, line_ref, *outs):
    for slot in (2, 1, 0):
        targets = [(ref, to) for ref in (outs[slot], outs[3 + slot]) for to in (0, outs[slot].shape[0] // 2)]
        write_slot(slot, turned_ref, mixed_ref, gp_ref, gb_ref, gdt_ref, line_ref, targets, where_ref)


def weight_terms(where, turned, one, other, smalls, rows, chans):
    feat, inner = turned[0].shape[0], turned[1].shape[0]
    tok, width = one[0].shape
    full = width + inner + 2 * LANES
    block, pair = shape_of((rows, full), BF16), shape_of((2 * rows, full), BF16)
    shared = (
        shape_of((2 * tok, width), BF16),
        shape_of((2 * tok, feat), BF16),
        shape_of((2 * tok, LANES), BF16),
        shape_of((feat // rows, 8, LANES)),
    )
    *blocks, vectors, gp, gb, gdt, lines = pl.pallas_call(
        functools.partial(first_weight_kernel, rows, chans),
        in_specs=[SMEM_SPEC] + [VMEM_SPEC] * 2 + [HBM_SPEC] * 12 + [VMEM_SPEC] * 12,
        out_specs=[VMEM_SPEC] * 9,
        out_shape=(block,) * 4 + (shape_of((8, LANES)),) + shared,
        scratch_shapes=[pltpu.SemaphoreType.DMA((6,))],
        compiler_params=PARAMS,
        name="weight_gradients_first",
    )(where, *turned, *one, *other, *smalls)

    def rest(after):
        outs = pl.pallas_call(
            rest_weight_kernel,
            in_specs=[SMEM_SPEC] + [VMEM_SPEC] * 6,
            out_specs=[VMEM_SPEC] * 6,
            out_shape=(pair,) * 6,
            compiler_params=PARAMS,
            name="weight_gradients_rest",
        )(where, *turned, behind(gp, after), gb, gdt, lines)
        return outs[:3], outs[3:]

    return blocks, vectors, rest


def unpack_kernel(own_ref, second_ref, near_ref, wm_ref, wo_ref, wdt_ref, cw_ref, cb_ref, gg_ref, ng_ref, square):
    rows, width = wm_ref.shape
    feat = wo_ref.shape[1]
    blocks = wo_ref.shape[0] // rows
    last = width + blocks * feat

    def total(at, count):
        some = slice(0, count)
        return own_ref[some, at] + (second_ref[some, at].astype(F32) + near_ref[some, at].astype(F32))

    for c in range(width // 256):
        wm_ref[:, cols(c, 256)] = total(cols(c, 256), rows)
    for b in range(blocks):
        wo_ref[b * rows : (b + 1) * rows, :] = total(slice(width + b * feat, width + (b + 1) * feat), rows)
    square[...] = jnp.zeros(square.shape, F32)
    square[:rows, :] = total(slice(last, last + LANES), rows)
    wdt_ref[...] = square[...].T[: wdt_ref.shape[0], :rows]
    line = total(slice(last + LANES, last + 2 * LANES), 16)
    cw_ref[...] = line[0:TAPS, : cw_ref.shape[1]]
    for k, ref in enumerate((cb_ref, gg_ref, ng_ref)):
        ref[...] = line[TAPS + k : TAPS + k + 1, : ref.shape[1]]


def unpack_sums(terms, wm, wo, wdt, cw, cb, gg, ng):
    return pl.pallas_call(
        unpack_kernel,
        out_shape=tuple(shape_of(part.shape) for part in (wm, wo, wdt, cw, cb, gg, ng)),
        scratch_shapes=[pltpu.VMEM((LANES, LANES), F32)],
        compiler_params=PARAMS,
        name="unpack_sums",
    )(*terms)


def small_rows(vectors, rows):
    flat = jnp.concatenate([vector.reshape(-1) for vector in vectors])
    lines = -(-flat.shape[0] // LANES)
    wide = -(-lines // rows)
    flat = jnp.pad(flat, (0, lines * LANES - flat.shape[0])).reshape(lines, LANES)
    flat = jnp.pad(flat, ((0, rows * wide - lines), (0, 0)))
    return flat.reshape(wide, rows, LANES).transpose(1, 0, 2).reshape(rows, wide * LANES)


def small_flat(block, owners):
    rows, wide = block.shape[0] // owners, block.shape[1] // LANES
    return block.reshape(owners, rows, wide, LANES).transpose(0, 2, 1, 3).reshape(owners, wide * rows * LANES)


def total_over(value, axis):
    count = lax.axis_size(axis)
    step = 1
    while step < count:
        value = value + lax.ppermute(value, axis, [(i, i ^ step) for i in range(count)])
        step = step * 2
    return value


def shards(inputs, segments, cotangent, norm_gain, w_main, w_dt, conv_weight, conv_bias, dt_bias, a_log, skip_d, gate_gain, w_out):
    first = lax.axis_index("section") == 0
    dp = lax.axis_size("dp")
    feat = inputs.shape[2]
    rows, width = w_main.shape[1:]
    heads = w_dt.shape[2]
    chans, own_inner = conv_weight.shape[2], gate_gain.shape[1]
    inner = own_inner * dp
    blocks = own_inner // rows

    owned = (w_main[0], w_out[0], jnp.swapaxes(w_dt[0], 0, 1), conv_weight[0], conv_bias, gate_gain, norm_gain)
    aligned = rows % 16 == 0 and dp == 4 * Z_CHIPS
    side = lax.axis_index("section")
    place = lax.axis_index("dp")
    where = jnp.stack([side, place // 4, place // 2 % 2, place % 2]).astype(jnp.int32)
    if aligned:
        wm, wo, cw, cb, gg, gin = settle(where, gather_slots(pack_shard(*owned)), width, chans, feat)
    else:
        small = small_rows((conv_weight[0], conv_bias[0], gate_gain[0], norm_gain[0]), rows)
        out_block = w_out[0].reshape(blocks, rows, feat).transpose(1, 0, 2).reshape(rows, inner)
        packed = jnp.concatenate([w_main[0], out_block, jnp.pad(w_dt[0], ((0, 0), (0, LANES - heads))), small], axis=1)
        whole = lax.all_gather(packed, "dp", axis=0, tiled=True)
    marks = [TAPS * chans, (TAPS + 1) * chans, (TAPS + 1) * chans + own_inner, (TAPS + 1) * chans + own_inner + rows]
    if not aligned:
        wm = jnp.concatenate([whole[:, :width], whole[:, width + inner : width + inner + LANES]], axis=1)
        wo = whole[:, width : width + inner].reshape(dp, rows, blocks, feat).transpose(0, 2, 1, 3).reshape(inner, feat)
        flat = small_flat(whole[:, width + inner + LANES :], dp).astype(F32)
        cw = flat[:, : marks[0]].reshape(dp, TAPS, chans).transpose(1, 0, 2).reshape(TAPS, dp * chans)
        cb = flat[:, marks[0] : marks[1]].reshape(1, dp * chans)
        gg = flat[:, marks[1] : marks[2]].reshape(1, inner)
        gin = flat[:, marks[2] : marks[3]].reshape(1, feat)
    hp = jnp.pad(jnp.concatenate([dt_bias, a_log], axis=0), ((0, 6), (0, LANES - heads)))
    sk = jnp.repeat(skip_d, inner // heads, axis=1)
    weights = (wm, wo, gin, cw, cb, gg, hp, sk)

    def choose(one, other):
        return jnp.where(first, one, other)

    up = down = [(0, 1), (1, 0)]
    ids = segments.astype(F32)[:, None, :]
    f0 = forward_layer(0, where, ids, weights, [(inputs, 0)])
    r0 = lax.ppermute(f0[0], "section", up)
    f1 = forward_layer(3, where, ids, weights, [(inputs, 1), (r0, None)])
    r1 = lax.ppermute(f1[0], "section", up)
    f2 = forward_layer(1, where, ids, weights, [(inputs, 1), (r1, None)])

    def stored(tick):
        return [(tick[i], None) for i in (2, 3, 4, 6, 7, 8)]

    kept = stored(f1)
    now = [[(cotangent, 0), (inputs, 1)] + kept, [(cotangent, 0), (r0, None)] + kept]
    b0 = backward_layer(0, where, ids, weights, now)
    d0 = lax.ppermute(b0[1], "section", down)
    now = [
        [(d0, None), (inputs, 0)] + stored(f0),
        [(cotangent, 1), (r1, None)] + stored(f2),
    ]
    b1 = backward_layer(2, where, ids, weights, now)
    d1 = lax.ppermute(b1[1], "section", down)
    if aligned:
        rows_of = (f0[1], f0[5]), (f2[1], f2[5]), (f1[1], behind(f1[5], b1[1]))
        turned = turn(where, *rows_of, rows)
    b2 = backward_layer(1, where, ids, weights, [[(d1, None), (inputs, 1)] + kept])
    dch, din, dgin, dhp = tuple(choose(two, zero) + one for zero, one, two in zip(b0[4:], b1[4:], b2[4:]))
    on_first = (f0[1], f0[5], b1[2], d0, b1[3]), (f1[1], f1[5], b2[2], d1, b2[3])
    on_last = (f2[1], f2[5], b1[2], cotangent[1], b1[3]), (f1[1], f1[5], b0[2], cotangent[0], b0[3])
    if aligned:
        smalls = [part[i] for i in (4, 5, 6, 7) for part in (b0, b1, b2)]
        one, other = (pair[0][2:] + pair[1][2:] for pair in (on_first, on_last))
        first_blocks, vectors, rest = weight_terms(where, turned, one, other, smalls, rows, chans)
    else:
        n, mix, gp, gb, gdt = tuple(
            jnp.concatenate([choose(on_first[0][i], on_last[0][i]), choose(on_first[1][i], on_last[1][i])], axis=0) for i in range(5)
        )
        own = [
            small_rows(
                (
                    dch[:TAPS, i * chans : (i + 1) * chans],
                    dch[TAPS, i * chans : (i + 1) * chans],
                    din[0, i * own_inner : (i + 1) * own_inner],
                    dgin[0, i * rows : (i + 1) * rows],
                ),
                rows,
            )
            for i in range(dp)
        ]
        wide = dot_tn(mix, gb).reshape(dp, blocks, rows, feat).transpose(0, 2, 1, 3).reshape(feat, inner)
        parts = [dot_tn(n, gp), wide, dot_tn(n, gdt), jnp.concatenate(own, axis=0)]
        packed_grad = jnp.concatenate([part.astype(BF16) for part in parts], axis=1)
    if aligned:
        terms, vectors, started = scatter_slots(first_blocks, rest, vectors)
        heads_sum = vectors[:, :heads]
    else:
        summed = lax.psum_scatter(packed_grad, "dp", scatter_dimension=0, tiled=True)
        heads_sum = total_over(dhp[:3, :heads], "dp")
        started = summed
    if aligned:
        g_main, g_out, g_dt, g_cw, g_cb, g_gg, g_ng = unpack_sums(terms, *owned)
        g_dt = jnp.swapaxes(g_dt, 0, 1)
    else:
        summed = summed.astype(F32)
        got = small_flat(summed[:, width + inner + LANES :], 1)[0]
        g_main = summed[:, :width]
        g_out = summed[:, width : width + inner].reshape(rows, blocks, feat).transpose(1, 0, 2).reshape(own_inner, feat)
        g_dt = summed[:, width + inner : width + inner + heads]
        g_cw = got[: marks[0]].reshape(TAPS, chans)
        g_cb, g_gg, g_ng = (got[None, marks[i] : marks[i + 1]] for i in range(3))
    outs = [part[0] for part in (f0, f1, f2, b0, b1, b2)]
    outs = lax.optimization_barrier((*outs, started))
    hidden = jnp.stack([choose(outs[0], outs[1]), choose(outs[1], outs[2])])[None]
    grad_inputs = jnp.stack([choose(outs[4], outs[3]), choose(outs[5], outs[4])])[None]
    return (
        hidden,
        grad_inputs,
        g_ng,
        g_main[None],
        g_dt[None],
        g_cw[None],
        g_cb,
        heads_sum[0:1],
        heads_sum[1:2],
        heads_sum[2:3],
        g_gg,
        g_out[None],
    )


def solution(mesh):
    placed = (
        P(None, "dp", None),
        P(None, "dp"),
        P(None, "dp", None),
        P("section", "dp"),
        P("section", "dp", None),
        P("section", "dp", None),
        P("section", None, "dp"),
        P("section", "dp"),
        P("section", None),
        P("section", None),
        P("section", None),
        P("section", "dp"),
        P("section", "dp", None),
    )
    return jax.shard_map(
        shards,
        mesh=mesh,
        in_specs=placed,
        out_specs=(
            P("section", None, "dp", None),
            P("section", None, "dp", None),
            P("section", "dp"),
            P("section", "dp", None),
            P("section", "dp", None),
            P("section", None, "dp"),
            P("section", "dp"),
            P("section", None),
            P("section", None),
            P("section", None),
            P("section", "dp"),
            P("section", "dp", None),
        ),
        check_vma=False,
    )
```

```python
import functools

import jax
import jax.numpy as jnp
from jax import lax
from jax.experimental import pallas as pl
from jax.experimental.pallas import tpu as pltpu
from jax.sharding import PartitionSpec as P

norm_eps = 1e-05
F32 = jnp.float32
BF16 = jnp.bfloat16
LANES = 128
TAPS = 4
VMEM_BYTES = 28 * 1024 * 1024


def dot_nn(a, b):
    return lax.dot_general(a, b, (((1,), (0,)), ((), ())), preferred_element_type=F32)


def dot_nt(a, b):
    return lax.dot_general(a, b, (((1,), (1,)), ((), ())), preferred_element_type=F32)


def dot_tn(a, b):
    return lax.dot_general(a, b, (((0,), (0,)), ((), ())), preferred_element_type=F32)


def split(a):
    high = a.astype(BF16)
    return high, (a - high.astype(F32)).astype(BF16)


def exact(dot, a, b):
    ah, al = split(a)
    bh, bl = split(b)
    return dot(ah, bh) + (dot(ah, bl) + dot(al, bh))


def near(dot, a, b):
    return exact(dot, a, b)


def triangle(lower):
    rows = lax.broadcasted_iota(jnp.int32, (LANES, LANES), 0)
    cols = lax.broadcasted_iota(jnp.int32, (LANES, LANES), 1)
    return jnp.where(rows >= cols if lower else rows <= cols, 1.0, 0.0).astype(BF16)


def running(tri, a):
    high = a.astype(BF16)
    rest = a - high.astype(F32)
    mid = rest.astype(BF16)
    low = (rest - mid.astype(F32)).astype(BF16)
    return dot_nn(tri, high) + (dot_nn(tri, mid) + dot_nn(tri, low))


def sigmoid(a):
    return 0.5 * jnp.tanh(0.5 * a) + 0.5


def softplus(a):
    return jnp.maximum(a, 0.0) + jnp.log1p(jnp.exp(-jnp.abs(a)))


def cols(j, width=LANES):
    return slice(j * width, (j + 1) * width)


def token_masks(ids):
    length = ids.shape[1]
    across = jnp.broadcast_to(ids, (length, length))
    wide = across.T
    rows = lax.broadcasted_iota(jnp.int32, (length, length), 0)
    lane = lax.broadcasted_iota(jnp.int32, (length, length), 1)
    linked = jnp.where((rows >= lane) & (wide == across), 1.0, 0.0)
    sees = [None]
    for k in range(1, TAPS):
        sees.append(jnp.where((rows >= k) & (pltpu.roll(wide, k, 0) == wide), 1.0, 0.0))
    return linked, sees


def take(which_ref, choices, into, sems):
    def start(choice):
        for i, ((ref, index), target) in enumerate(zip(choice, into)):
            pltpu.make_async_copy(ref if index is None else ref.at[index], target, sems.at[i]).start()

    if len(choices) == 1:
        start(choices[0])
        return
    for number, choice in enumerate(choices):
        pl.when(which_ref[0] == number)(functools.partial(start, choice))


def taken(into, sems, *numbers):
    for i in numbers:
        pltpu.make_async_copy(into[i], into[i], sems.at[i]).wait()


def conv_taps(v, sees):
    return [v] + [sees[k] * pltpu.roll(v, k, 0) for k in range(1, TAPS)]


def conv_sum(taps, cw_ref, cb_ref, at):
    total = cb_ref[:, at] + cw_ref[TAPS - 1 : TAPS, at] * taps[0]
    for k in range(1, TAPS):
        total = total + cw_ref[TAPS - 1 - k : TAPS - k, at] * taps[k]
    return total


def pair_of(values, j):
    lane = lax.broadcasted_iota(jnp.int32, (values.shape[0], LANES), 1)
    first = jnp.broadcast_to(values[:, 2 * j : 2 * j + 1], lane.shape)
    second = jnp.broadcast_to(values[:, 2 * j + 1 : 2 * j + 2], lane.shape)
    return jnp.where(lane < LANES // 2, first, second)


def halves(values):
    lane = lax.broadcasted_iota(jnp.int32, values.shape, 1)
    low = jnp.where(lane < LANES // 2, values, 0.0)
    return jnp.concatenate([low, values - low], axis=0)


def decay(cum, cum_t, linked, h):
    spread = cum[:, h : h + 1] - cum_t[h : h + 1, :]
    return linked * jnp.exp(jnp.minimum(spread, 0.0))


def micro_of(which_ref, mode):
    return (0, 1, which_ref[0], 1 - which_ref[0])[mode]


def held(which_ref, options, indices):
    refs = [ref if index is None else ref.at[index] for ref, index in zip(options, indices)]

    def read(at=slice(None)):
        values = [ref[:, at] for ref in refs]
        return values[0] if len(values) == 1 else jnp.where(which_ref[0] == 0, values[0], values[1])

    return read


KEPT = 8


def fwd_kernel(plan, mode, which_ref, ids_ref, wm_ref, wo_ref, gin_ref, cw_ref, cb_ref, gg_ref, hp_ref, sk_ref, *refs):
    sources, refs = refs[: len(plan)], refs[len(plan) :]
    v_ref, n_ref, p_ref, dtr_ref, y_ref, mix_ref, total_ref, g_ref, r2_ref = refs
    inner, width = gg_ref.shape[1], p_ref.shape[1]
    pairs = inner // LANES
    linked, sees = token_masks(ids_ref[micro_of(which_ref, mode)])
    u = held(which_ref, sources, plan)().astype(F32)
    r = lax.rsqrt(jnp.mean(u * u, axis=-1, keepdims=True) + norm_eps)
    n = (u * r * gin_ref[...]).astype(BF16)
    n_ref[...] = n
    for c in range(width // 256):
        p_ref[:, cols(c, 256)] = dot_nn(n, wm_ref[:, cols(c, 256)])
    dtr = dot_nn(n, wm_ref[:, width:])
    dtr_ref[...] = dtr

    def conv(j):
        total = conv_sum(conv_taps(p_ref[:, inner + j * LANES : inner + (j + 1) * LANES], sees), cw_ref, cb_ref, cols(j))
        total_ref[:, cols(j)] = total
        return total * sigmoid(total)

    b_state = conv(pairs)
    c_state = conv(pairs + 1)
    cross = exact(dot_nt, c_state, b_state)
    dt = softplus(dtr + hp_ref[0:1, :])
    cum = running(triangle(True), -dt * jnp.exp(hp_ref[1:2, :]))
    cum_t = cum.T
    squares = jnp.zeros((u.shape[0], LANES), F32)
    for j in range(pairs):
        at = cols(j)
        x = conv(j)
        m = jnp.concatenate([cross * decay(cum, cum_t, linked, 2 * j), cross * decay(cum, cum_t, linked, 2 * j + 1)], axis=1)
        y = near(dot_nn, m, halves(x * pair_of(dt, j))) + sk_ref[:, at] * x
        y_ref[:, at] = y
        z = p_ref[:, at]
        g = y * (z * sigmoid(z))
        g_ref[:, at] = g
        squares = squares + g * g
    r2 = lax.rsqrt(jnp.sum(squares, axis=-1, keepdims=True) / inner + norm_eps)
    for j in range(pairs):
        at = cols(j)
        mix_ref[:, at] = (g_ref[:, at] * r2 * gg_ref[:, at]).astype(BF16)
    r2_ref[...] = jnp.broadcast_to(r2, r2_ref.shape)
    mixed = mix_ref[...]
    for c in range(u.shape[1] // 256):
        at = cols(c, 256)
        v_ref[:, at] = (u[:, at] + dot_nn(mixed, wo_ref[:, at])).astype(BF16)


def bwd_kernel(plan, mode, which_ref, ids_ref, wm_ref, wo_ref, gin_ref, cw_ref, cb_ref, gg_ref, hp_ref, sk_ref, *refs):
    count = KEPT * len(plan)
    sources, refs = refs[:count], refs[count:]
    gi_ref, gl_ref, gp_ref, gdt_ref, dch_ref, din_ref, dgin_ref, dhp_ref, gm_scr = refs
    gv, u_low, p, dtr, y_kept, totals, g_kept, r2_kept = [
        held(which_ref, [sources[KEPT * k + i] for k in range(len(plan))], [indices[i] for indices in plan]) for i in range(KEPT)
    ]
    dch_ref[...] = jnp.zeros(dch_ref.shape, F32)
    din_ref[...] = jnp.zeros(din_ref.shape, F32)
    inner = gg_ref.shape[1]
    pairs = inner // LANES
    length = gm_scr.shape[0]
    linked, sees = token_masks(ids_ref[micro_of(which_ref, mode)])
    gb = gv()
    inners = jnp.zeros((length, 256), F32)
    for c in range(inner // 256):
        at = cols(c, 256)
        gm = dot_nt(gb, wo_ref[at, :])
        gm_scr[:, at] = gm
        inners = inners + gm * gg_ref[:, at] * g_kept(at)
    r2 = r2_kept()[:, 0:1]
    pull = r2 * r2 * r2 * (jnp.sum(inners, axis=-1, keepdims=True) / inner)

    def conv(j):
        total = totals(cols(j))
        return total, sigmoid(total)

    def conv_back(j, total, sig, grad):
        at = cols(j)
        v = p(slice(inner + j * LANES, inner + (j + 1) * LANES))
        ds = grad * (sig * (1.0 + total * (1.0 - sig)))
        dch_ref[TAPS : TAPS + 1, at] = jnp.sum(ds, axis=0, keepdims=True)
        dch_ref[TAPS - 1 : TAPS, at] = jnp.sum(ds * v, axis=0, keepdims=True)
        dv = cw_ref[TAPS - 1 : TAPS, at] * ds
        for k in range(1, TAPS):
            row = slice(TAPS - 1 - k, TAPS - k)
            moved = pltpu.roll(sees[k] * ds, length - k, 0)
            dch_ref[row, at] = jnp.sum(moved * v, axis=0, keepdims=True)
            dv = dv + cw_ref[row, at] * moved
        gp_ref[:, inner + j * LANES : inner + (j + 1) * LANES] = dv.astype(BF16)

    sb, gb_sig = conv(pairs)
    b_state = sb * gb_sig
    sc, gc_sig = conv(pairs + 1)
    c_state = sc * gc_sig
    cross = exact(dot_nt, c_state, b_state)
    dt_arg = dtr() + hp_ref[0:1, :]
    dt = softplus(dt_arg)
    rate = jnp.exp(hp_ref[1:2, :])
    cum = running(triangle(True), -dt * rate)
    cum_t = cum.T
    dcross = jnp.zeros((length, length), F32)
    dcum = jnp.zeros((length, LANES), F32)
    ddt = jnp.zeros((length, LANES), F32)
    dskip = jnp.zeros((8, LANES), F32)
    lane = lax.broadcasted_iota(jnp.int32, (2 * LANES, LANES), 1)
    row = lax.broadcasted_iota(jnp.int32, (2 * LANES, LANES), 0)
    half = jnp.where((row % LANES) < LANES // 2, 0, 1)
    for j in range(pairs):
        at = cols(j)
        pick = jnp.where(lane == 2 * j + half, 1.0, 0.0).astype(BF16)
        gm = gm_scr[:, at]
        g = g_kept(at)
        din_ref[0:1, at] = jnp.sum(gm * (g * r2), axis=0, keepdims=True)
        dg = gm * gg_ref[:, at] * r2 - g * pull
        z = p(at)
        sig = sigmoid(z)
        y = y_kept(at)
        dy = dg * (z * sig)
        gp_ref[:, at] = (dg * y * (sig * (1.0 + z * (1.0 - sig)))).astype(BF16)
        total, tsig = conv(j)
        x = total * tsig
        dtp = pair_of(dt, j)
        xw = x * dtp
        dy_st = halves(dy)
        l1 = decay(cum, cum_t, linked, 2 * j)
        l2 = decay(cum, cum_t, linked, 2 * j + 1)
        dm = dot_nt(dy_st.astype(BF16), xw.astype(BF16))
        dcross = dcross + dm[:length] * l1 + dm[length:] * l2
        m = jnp.concatenate([cross * l1, cross * l2], axis=0)
        dxw = near(dot_tn, m, dy_st)
        skip = sk_ref[:, at]
        lanes = jnp.broadcast_to(jnp.sum(dy * x, axis=0, keepdims=True), (8, LANES))
        dskip = dskip + dot_nn(jnp.concatenate(split(lanes), axis=1), pick)
        q = dy * (y - skip * x) - dxw * xw
        dcum = dcum + dot_nn(jnp.concatenate(split(q), axis=1), pick)
        ddt = ddt + dot_nn(jnp.concatenate(split(dxw * x), axis=1), pick)
        conv_back(j, total, tsig, skip * dy + dxw * dtp)
    conv_back(pairs, sb, gb_sig, exact(dot_tn, dcross, c_state))
    conv_back(pairs + 1, sc, gc_sig, exact(dot_nn, dcross, b_state))
    dlog = running(triangle(False), dcum)
    draw = (ddt - rate * dlog) * sigmoid(dt_arg)
    gdt = draw.astype(BF16)
    gdt_ref[...] = gdt
    dhp_ref[0:1, :] = jnp.sum(draw, axis=0, keepdims=True)
    dhp_ref[1:2, :] = jnp.sum(dlog * (-dt * rate), axis=0, keepdims=True)
    dhp_ref[2:3, :] = dskip[0:1]
    dhp_ref[3:8, :] = jnp.zeros((5, LANES), F32)
    u = u_low().astype(F32)
    gin = gin_ref[...]
    r = lax.rsqrt(jnp.mean(u * u, axis=-1, keepdims=True) + norm_eps)
    gp = gp_ref[...]
    width = gp.shape[1]
    gn = jnp.concatenate(
        [dot_nt(gp, wm_ref[cols(c, 256), :width]) + dot_nt(gdt, wm_ref[cols(c, 256), width:]) for c in range(u.shape[1] // 256)], axis=1
    )
    dgin_ref[...] = jnp.broadcast_to(jnp.sum(gn * (u * r), axis=0, keepdims=True), dgin_ref.shape)
    gng = gn * gin
    back = r * r * r * jnp.mean(gng * u, axis=-1, keepdims=True)
    grad = gb.astype(F32) + (gng * r - u * back)
    gi_ref[...] = grad
    gl_ref[...] = grad.astype(BF16)


def shape_of(shape, dtype=F32):
    return jax.ShapeDtypeStruct(shape, dtype)


VMEM_SPEC = pl.BlockSpec(memory_space=pltpu.VMEM)
HBM_SPEC = pl.BlockSpec(memory_space=pltpu.HBM)
SMEM_SPEC = pl.BlockSpec(memory_space=pltpu.SMEM)
PARAMS = pltpu.CompilerParams(vmem_limit_bytes=VMEM_BYTES)


def layer_sizes(weights):
    return weights[0].shape[0], weights[1].shape[0], weights[0].shape[1] - LANES


def forward_layer(mode, which, ids, weights, choices):
    tok = ids.shape[2]
    feat, inner, width = layer_sizes(weights)
    return pl.pallas_call(
        functools.partial(fwd_kernel, tuple(index for _, index in choices), mode),
        in_specs=[SMEM_SPEC] + [VMEM_SPEC] * (9 + len(choices)),
        out_specs=[VMEM_SPEC] * 9,
        out_shape=(
            shape_of((tok, feat), BF16),
            shape_of((tok, feat), BF16),
            shape_of((tok, width)),
            shape_of((tok, LANES)),
            shape_of((tok, inner)),
            shape_of((tok, inner), BF16),
            shape_of((tok, width - inner)),
            shape_of((tok, inner)),
            shape_of((tok, LANES)),
        ),
        compiler_params=PARAMS,
        name="layer_forward",
    )(which, ids, *weights, *[source for source, _ in choices])


def backward_layer(mode, which, ids, weights, choices):
    tok = ids.shape[2]
    feat, inner, width = layer_sizes(weights)
    return pl.pallas_call(
        functools.partial(bwd_kernel, tuple(tuple(index for _, index in choice) for choice in choices), mode),
        in_specs=[SMEM_SPEC] + [VMEM_SPEC] * (9 + KEPT * len(choices)),
        out_specs=[VMEM_SPEC] * 8,
        out_shape=(
            shape_of((tok, feat)),
            shape_of((tok, feat), BF16),
            shape_of((tok, width), BF16),
            shape_of((tok, LANES), BF16),
            shape_of((8, width - inner)),
            shape_of((8, inner)),
            shape_of((8, feat)),
            shape_of((8, LANES)),
        ),
        scratch_shapes=[pltpu.VMEM((tok, inner), F32)],
        compiler_params=PARAMS,
        name="layer_backward",
    )(which, ids, *weights, *[source for choice in choices for source, _ in choice])


def lay(blocks, size, chunks):
    lane = lax.broadcasted_iota(jnp.int32, (8, LANES), 1)
    out = [jnp.zeros((8, LANES), F32) for _ in range(chunks)]
    for i, block in enumerate(blocks):
        chunk, shift = (i * size) // LANES, (i * size) % LANES
        turned = pltpu.roll(block, shift, 1) if shift else block
        out[chunk] = jnp.where((lane >= shift) & (lane < shift + size), turned, out[chunk])
        if shift + size > LANES:
            out[chunk + 1] = jnp.where(lane < shift + size - LANES, turned, out[chunk + 1])
    return out


def cut(chunks, size, i):
    lane = lax.broadcasted_iota(jnp.int32, (8, LANES), 1)
    chunk, shift = (i * size) // LANES, (i * size) % LANES
    turn = (LANES - shift) % LANES
    block = pltpu.roll(chunks[chunk], turn, 1) if turn else chunks[chunk]
    if shift + size > LANES:
        block = jnp.where(lane < LANES - shift, block, pltpu.roll(chunks[chunk + 1], turn, 1))
    return jnp.where(lane < size, block, 0.0)


def pack_kernel(wm_ref, wo_ref, wdt_ref, cw_ref, cb_ref, gg_ref, ng_ref, out_ref, line, square):
    rows, width = wm_ref.shape
    feat = wo_ref.shape[1]
    blocks = wo_ref.shape[0] // rows
    out_ref[:, :width] = wm_ref[...]
    for b in range(blocks):
        out_ref[:, width + b * feat : width + (b + 1) * feat] = wo_ref[b * rows : (b + 1) * rows, :]
    last = width + blocks * feat
    out_ref[:, last + LANES :] = jnp.zeros((rows, LANES), BF16)
    square[...] = jnp.zeros(square.shape, F32)
    square[: wdt_ref.shape[0], :rows] = wdt_ref[...].astype(F32)
    out_ref[:, last : last + LANES] = square[...].T[:rows].astype(BF16)
    line[...] = jnp.zeros(line.shape, F32)
    line[0:TAPS, : cw_ref.shape[1]] = cw_ref[...].astype(F32)
    for k, ref in enumerate((cb_ref, gg_ref, ng_ref)):
        line[TAPS + k : TAPS + k + 1, : ref.shape[1]] = ref[...].astype(F32)
    out_ref[0:16, last + LANES :] = line[...].astype(BF16)


def pack_shard(wm, wo, wdt, cw, cb, gg, ng):
    rows, width = wm.shape
    full = width + wo.shape[0] // rows * wo.shape[1] + 2 * LANES
    return pl.pallas_call(
        pack_kernel,
        out_shape=shape_of((rows, full), BF16),
        scratch_shapes=[pltpu.VMEM((16, LANES), F32), pltpu.VMEM((LANES, LANES), F32)],
        compiler_params=pltpu.CompilerParams(vmem_limit_bytes=2 * VMEM_BYTES),
        name="pack_shard",
    )(wm, wo, wdt, cw, cb, gg, ng)


Z_CHIPS = 4


def spot(z, y, c):
    return (z * 2 + y) * 2 + c


def routed(value, move):
    pairs = []
    for z in range(Z_CHIPS):
        for y in range(2):
            for c in range(2):
                target = move(z, y, c)
                if target is not None:
                    pairs.append((spot(z, y, c), spot(*target)))
    return lax.ppermute(value, "dp", pairs)


def to_core(z, y, c):
    return z, y, 1 - c


def to_y(z, y, c):
    return z, 1 - y, c


def to_near(z, y, c):
    return z ^ 1, y, c


def to_middle(z, y, c):
    return (3 - z, y, c) if z in (1, 2) else None


def slot_places(z):
    return (z, z + 1 - 2 * lax.rem(z, 2), jnp.where(z < 2, 2, 1), jnp.where(z < 2, 3, 0))


def behind(value, other):
    return lax.optimization_barrier((value, other))[0]


def gather_slots(own):
    def pair(block, across):
        return jnp.concatenate([across, block], axis=0)

    near, second, own_y = lax.optimization_barrier((routed(own, to_near), routed(own, to_middle), routed(own, to_y)))
    own_pair = pair(own, own_y)
    last, ends, near_y = lax.optimization_barrier((routed(near, to_middle), routed(second, to_near), routed(near, to_y)))
    second = second + ends
    near_pair = pair(near, near_y)
    own_core = routed(behind(own_pair, ends), to_core)
    ends, second_y = lax.optimization_barrier((routed(last, to_near), routed(second, to_y)))
    last = last + ends
    second_pair = pair(second, second_y)
    near_core = routed(behind(near_pair, ends), to_core)
    second_core = routed(second_pair, to_core)
    last_pair = pair(last, routed(last, to_y))
    return [own_pair, near_pair, second_pair, last_pair, own_core, near_core, second_core, routed(last_pair, to_core)]


def scatter_slots(first_blocks, rest, vectors):
    rows = first_blocks[0].shape[0]

    def met(kept, value):
        total = kept.astype(F32) + value.astype(F32)
        return total[:rows].astype(BF16), total[rows:]

    def low(value):
        return value.astype(BF16)

    def summed(step):
        return vectors + lax.ppermute(vectors, "dp", [(i, i ^ step) for i in range(4 * Z_CHIPS)])

    kept_far, kept_near, sent_far, sent_near = first_blocks
    far = low(kept_far.astype(F32) + routed(sent_far, to_core).astype(F32))
    last = kept_near.astype(F32) + routed(behind(sent_near, far), to_core).astype(F32)
    kept, sent = rest(far)
    came = routed(far, to_y)
    vectors = behind(vectors, far)
    vectors = summed(1)
    over = [routed(block, to_core) for block in sent]
    far, second = met(kept[2], over[2])
    came, vectors = lax.optimization_barrier((came, vectors))
    came, last = routed(behind(far, came), to_y), last + came.astype(F32)
    line = routed(low(last), to_near)
    vectors = summed(2)
    far, near = met(kept[1], over[1])
    came, line, vectors = lax.optimization_barrier((came, line, vectors))
    last, second = last + line.astype(F32), second + came.astype(F32)
    came, line, ends = routed(behind(far, came), to_y), routed(low(last), to_middle), routed(low(second), to_near)
    vectors = summed(4)
    far, own = met(kept[0], over[0])
    came, line, ends, vectors = lax.optimization_barrier((came, line, ends, vectors))
    near, second = near + came.astype(F32) + line.astype(F32), second + ends.astype(F32)
    started = came
    came = routed(behind(far, came), to_y)
    near = low(near)
    vectors = behind(vectors, near)
    near, second = routed(near, to_near), routed(low(second), to_middle)
    vectors = summed(8)
    return (own + came.astype(F32), second, near), vectors, started


def owners_of(where_ref):
    z, y, c = where_ref[1], where_ref[2], where_ref[3]
    return [(spot(at, 1 - y, core), spot(at, y, core)) for core in (c, 1 - c) for at in slot_places(z)]


def settle_kernel(chans, where_ref, *refs):
    pairs, (wm_ref, wo_ref, cw_ref, cb_ref, gg_ref, gin_ref, line_ref, sem) = refs[:8], refs[8:]
    rows = pairs[0].shape[0] // 2
    feat = wo_ref.shape[1]
    width = wm_ref.shape[1] - LANES
    inner = wo_ref.shape[0]
    last = width + inner
    copies = []
    for pair, owners in zip(pairs, owners_of(where_ref)):
        for half, owner in enumerate(owners):
            mine = pl.ds(half * rows, rows)
            to = pl.ds(pl.multiple_of(owner * rows, 16), rows)
            copies.append((pair.at[pl.ds(half * rows, 16), pl.ds(last + LANES, LANES)], line_ref.at[owner]))
            copies.append((pair.at[mine, pl.ds(0, width)], wm_ref.at[to, pl.ds(0, width)]))
            copies.append((pair.at[mine, pl.ds(last, LANES)], wm_ref.at[to, pl.ds(width, LANES)]))
            for b in range(inner // wm_ref.shape[0]):
                into = pl.ds(pl.multiple_of((owner * (inner // wm_ref.shape[0]) + b) * rows, 16), rows)
                copies.append((pair.at[mine, pl.ds(width + b * feat, feat)], wo_ref.at[into]))
    for source, target in copies:
        pltpu.make_async_copy(source, target, sem).start()
    for whole in (wm_ref, wo_ref, line_ref):
        pltpu.make_async_copy(whole, whole, sem).wait()
    lines = [line_ref[i].astype(F32)[0:8] for i in range(line_ref.shape[0])]
    for c, chunk in enumerate(lay(lines, chans, cw_ref.shape[1] // LANES)):
        cw_ref[:, cols(c)] = chunk[0:TAPS]
        cb_ref[:, cols(c)] = chunk[TAPS : TAPS + 1]
    for c, chunk in enumerate(lay(lines, inner // len(lines), gg_ref.shape[1] // LANES)):
        gg_ref[:, cols(c)] = chunk[TAPS + 1 : TAPS + 2]
    for c, chunk in enumerate(lay(lines, rows, gin_ref.shape[1] // LANES)):
        gin_ref[:, cols(c)] = chunk[TAPS + 2 : TAPS + 3]


def settle(where, pairs, width, chans, feat):
    rows, full = pairs[0].shape[0] // 2, pairs[0].shape[1]
    owners, inner = feat // rows, full - width - 2 * LANES
    return pl.pallas_call(
        functools.partial(settle_kernel, chans),
        in_specs=[SMEM_SPEC] + [HBM_SPEC] * 8,
        out_specs=[VMEM_SPEC] * 6,
        out_shape=(
            shape_of((feat, width + LANES), BF16),
            shape_of((inner, feat), BF16),
            shape_of((TAPS, owners * chans)),
            shape_of((1, owners * chans)),
            shape_of((1, inner)),
            shape_of((1, feat)),
        ),
        scratch_shapes=[pltpu.VMEM((owners, 16, LANES), BF16), pltpu.SemaphoreType.DMA],
        compiler_params=PARAMS,
        name="settle_weights",
    )(where, *pairs)


def slot_blocks(where_ref):
    owners = owners_of(where_ref)
    return [owner for slot in range(4) for pair in (owners[slot], owners[4 + slot]) for owner in pair]


def write_slot(slot, turned, mixed, gp_ref, gb_ref, gdt_ref, line_ref, out_refs, where_ref):
    rows, width, feat = turned.shape[0] // 16, gp_ref.shape[1], gb_ref.shape[1]
    blocks = mixed.shape[0] // turned.shape[0]
    last = width + blocks * feat
    mine = turned[4 * slot * rows : 4 * (slot + 1) * rows, :]

    def put(at, term):
        for part, (ref, to) in enumerate(out_refs):
            ref[to : to + rows, at] = term[part * rows : (part + 1) * rows].astype(BF16)

    for c in range(width // 256):
        put(cols(c, 256), dot_nn(mine, gp_ref[:, cols(c, 256)]))
    put(slice(last, last + LANES), dot_nn(mine, gdt_ref[...]))
    owners = slot_blocks(where_ref)[4 * slot : 4 * slot + 4]
    for part, owner in enumerate(owners):
        ref, to = out_refs[part]
        for b in range(blocks):
            start = ((4 * slot + part) * blocks + b) * rows
            at = slice(width + b * feat, width + (b + 1) * feat)
            ref[to : to + rows, at] = dot_nn(mixed[start : start + rows, :], gb_ref[...]).astype(BF16)
        line = line_ref[owner]
        ref[to : to + 16, last + LANES :] = jnp.concatenate([line, jnp.zeros_like(line)], axis=0).astype(BF16)
        ref[to + 16 : to + rows, last + LANES :] = jnp.zeros((rows - 16, LANES), BF16)


def turn_kernel(rows, where_ref, n_first, mix_first, n_last, mix_last, n_both, mix_both, turned_ref, mixed_ref, flat_ref, wide_ref):
    tok, feat = n_both.shape
    many = mix_both.shape[1] // feat * rows

    def early(one, other):
        return jnp.where(where_ref[0] == 0, one[...], other[...])

    flat_ref[:, :tok] = early(n_first, n_last).T
    flat_ref[:, tok:] = n_both[...].T
    wide_ref[:, :tok] = early(mix_first, mix_last).T
    wide_ref[:, tok:] = mix_both[...].T
    for i, owner in enumerate(slot_blocks(where_ref)):
        turned_ref[i * rows : (i + 1) * rows, :] = flat_ref[pl.ds(pl.multiple_of(owner * rows, 16), rows), :]
        mixed_ref[i * many : (i + 1) * many, :] = wide_ref[pl.ds(pl.multiple_of(owner * many, 16), many), :]


def turn(where, first, last, both, rows):
    tok, feat = both[0].shape
    inner = both[1].shape[1]
    return pl.pallas_call(
        functools.partial(turn_kernel, rows),
        in_specs=[SMEM_SPEC] + [VMEM_SPEC] * 6,
        out_specs=[VMEM_SPEC] * 2,
        out_shape=(shape_of((feat, 2 * tok), BF16), shape_of((inner, 2 * tok), BF16)),
        scratch_shapes=[pltpu.VMEM((feat, 2 * tok), BF16), pltpu.VMEM((inner, 2 * tok), BF16)],
        compiler_params=PARAMS,
        name="turn_rows",
    )(where, *first, *last, *both)


def first_weight_kernel(rows, chans, where_ref, turned_ref, mixed_ref, *refs):
    sources, smalls, outs, sems = refs[:12], refs[12:24], refs[24:33], refs[33]
    vec_ref, gp_ref, gb_ref, gdt_ref, line_ref = outs[4:]
    feat, inner = turned_ref.shape[0], mixed_ref.shape[0]
    tok = turned_ref.shape[1] // 2
    blocks = inner // feat
    into = [ref.at[part * tok : (part + 1) * tok] for part in range(2) for ref in (gp_ref, gb_ref, gdt_ref)]
    take(where_ref, [[(source, None) for source in sources[6 * i : 6 * i + 6]] for i in range(2)], into, sems)
    early = jnp.where(where_ref[0] == 0, 0.0, 1.0)
    sums = [one[...] + early * zero[...] + (1.0 - early) * two[...] for zero, one, two in zip(smalls[0::3], smalls[1::3], smalls[2::3])]
    vec_ref[...] = sums[3]
    pieces = [[total[:, cols(c)] for c in range(total.shape[1] // LANES)] for total in sums]
    row = lax.broadcasted_iota(jnp.int32, (8, LANES), 0)
    for i in range(feat // rows):
        block = cut(pieces[0], chans, i)
        block = jnp.where(row == TAPS + 1, jnp.broadcast_to(cut(pieces[1], blocks * rows, i)[0:1], block.shape), block)
        line_ref[i] = jnp.where(row == TAPS + 2, jnp.broadcast_to(cut(pieces[2], rows, i)[0:1], block.shape), block)
    taken(into, sems, 0, 1, 2, 3, 4, 5)
    write_slot(3, turned_ref, mixed_ref, gp_ref, gb_ref, gdt_ref, line_ref, [(ref, 0) for ref in outs[:4]], where_ref)


def rest_weight_kernel(where_ref, turned_ref, mixed_ref, gp_ref, gb_ref, gdt_ref, line_ref, *outs):
    for slot in (2, 1, 0):
        targets = [(ref, to) for ref in (outs[slot], outs[3 + slot]) for to in (0, outs[slot].shape[0] // 2)]
        write_slot(slot, turned_ref, mixed_ref, gp_ref, gb_ref, gdt_ref, line_ref, targets, where_ref)


def weight_terms(where, turned, one, other, smalls, rows, chans):
    feat, inner = turned[0].shape[0], turned[1].shape[0]
    tok, width = one[0].shape
    full = width + inner + 2 * LANES
    block, pair = shape_of((rows, full), BF16), shape_of((2 * rows, full), BF16)
    shared = (
        shape_of((2 * tok, width), BF16),
        shape_of((2 * tok, feat), BF16),
        shape_of((2 * tok, LANES), BF16),
        shape_of((feat // rows, 8, LANES)),
    )
    *blocks, vectors, gp, gb, gdt, lines = pl.pallas_call(
        functools.partial(first_weight_kernel, rows, chans),
        in_specs=[SMEM_SPEC] + [VMEM_SPEC] * 2 + [HBM_SPEC] * 12 + [VMEM_SPEC] * 12,
        out_specs=[VMEM_SPEC] * 9,
        out_shape=(block,) * 4 + (shape_of((8, LANES)),) + shared,
        scratch_shapes=[pltpu.SemaphoreType.DMA((6,))],
        compiler_params=PARAMS,
        name="weight_gradients_first",
    )(where, *turned, *one, *other, *smalls)

    def rest(after):
        outs = pl.pallas_call(
            rest_weight_kernel,
            in_specs=[SMEM_SPEC] + [VMEM_SPEC] * 6,
            out_specs=[VMEM_SPEC] * 6,
            out_shape=(pair,) * 6,
            compiler_params=PARAMS,
            name="weight_gradients_rest",
        )(where, *turned, behind(gp, after), gb, gdt, lines)
        return outs[:3], outs[3:]

    return blocks, vectors, rest


def unpack_kernel(own_ref, second_ref, near_ref, wm_ref, wo_ref, wdt_ref, cw_ref, cb_ref, gg_ref, ng_ref, square):
    rows, width = wm_ref.shape
    feat = wo_ref.shape[1]
    blocks = wo_ref.shape[0] // rows
    last = width + blocks * feat

    def total(at, count):
        some = slice(0, count)
        return own_ref[some, at] + (second_ref[some, at].astype(F32) + near_ref[some, at].astype(F32))

    for c in range(width // 256):
        wm_ref[:, cols(c, 256)] = total(cols(c, 256), rows)
    for b in range(blocks):
        wo_ref[b * rows : (b + 1) * rows, :] = total(slice(width + b * feat, width + (b + 1) * feat), rows)
    square[...] = jnp.zeros(square.shape, F32)
    square[:rows, :] = total(slice(last, last + LANES), rows)
    wdt_ref[...] = square[...].T[: wdt_ref.shape[0], :rows]
    line = total(slice(last + LANES, last + 2 * LANES), 16)
    cw_ref[...] = line[0:TAPS, : cw_ref.shape[1]]
    for k, ref in enumerate((cb_ref, gg_ref, ng_ref)):
        ref[...] = line[TAPS + k : TAPS + k + 1, : ref.shape[1]]


def unpack_sums(terms, wm, wo, wdt, cw, cb, gg, ng):
    return pl.pallas_call(
        unpack_kernel,
        out_shape=tuple(shape_of(part.shape) for part in (wm, wo, wdt, cw, cb, gg, ng)),
        scratch_shapes=[pltpu.VMEM((LANES, LANES), F32)],
        compiler_params=PARAMS,
        name="unpack_sums",
    )(*terms)


def small_rows(vectors, rows):
    flat = jnp.concatenate([vector.reshape(-1) for vector in vectors])
    lines = -(-flat.shape[0] // LANES)
    wide = -(-lines // rows)
    flat = jnp.pad(flat, (0, lines * LANES - flat.shape[0])).reshape(lines, LANES)
    flat = jnp.pad(flat, ((0, rows * wide - lines), (0, 0)))
    return flat.reshape(wide, rows, LANES).transpose(1, 0, 2).reshape(rows, wide * LANES)


def small_flat(block, owners):
    rows, wide = block.shape[0] // owners, block.shape[1] // LANES
    return block.reshape(owners, rows, wide, LANES).transpose(0, 2, 1, 3).reshape(owners, wide * rows * LANES)


def total_over(value, axis):
    count = lax.axis_size(axis)
    step = 1
    while step < count:
        value = value + lax.ppermute(value, axis, [(i, i ^ step) for i in range(count)])
        step = step * 2
    return value


def shards(inputs, segments, cotangent, norm_gain, w_main, w_dt, conv_weight, conv_bias, dt_bias, a_log, skip_d, gate_gain, w_out):
    first = lax.axis_index("section") == 0
    dp = lax.axis_size("dp")
    feat = inputs.shape[2]
    rows, width = w_main.shape[1:]
    heads = w_dt.shape[2]
    chans, own_inner = conv_weight.shape[2], gate_gain.shape[1]
    inner = own_inner * dp
    blocks = own_inner // rows

    owned = (w_main[0], w_out[0], jnp.swapaxes(w_dt[0], 0, 1), conv_weight[0], conv_bias, gate_gain, norm_gain)
    aligned = rows % 16 == 0 and dp == 4 * Z_CHIPS
    side = lax.axis_index("section")
    place = lax.axis_index("dp")
    where = jnp.stack([side, place // 4, place // 2 % 2, place % 2]).astype(jnp.int32)
    if aligned:
        wm, wo, cw, cb, gg, gin = settle(where, gather_slots(pack_shard(*owned)), width, chans, feat)
    else:
        small = small_rows((conv_weight[0], conv_bias[0], gate_gain[0], norm_gain[0]), rows)
        out_block = w_out[0].reshape(blocks, rows, feat).transpose(1, 0, 2).reshape(rows, inner)
        packed = jnp.concatenate([w_main[0], out_block, jnp.pad(w_dt[0], ((0, 0), (0, LANES - heads))), small], axis=1)
        whole = lax.all_gather(packed, "dp", axis=0, tiled=True)
    marks = [TAPS * chans, (TAPS + 1) * chans, (TAPS + 1) * chans + own_inner, (TAPS + 1) * chans + own_inner + rows]
    if not aligned:
        wm = jnp.concatenate([whole[:, :width], whole[:, width + inner : width + inner + LANES]], axis=1)
        wo = whole[:, width : width + inner].reshape(dp, rows, blocks, feat).transpose(0, 2, 1, 3).reshape(inner, feat)
        flat = small_flat(whole[:, width + inner + LANES :], dp).astype(F32)
        cw = flat[:, : marks[0]].reshape(dp, TAPS, chans).transpose(1, 0, 2).reshape(TAPS, dp * chans)
        cb = flat[:, marks[0] : marks[1]].reshape(1, dp * chans)
        gg = flat[:, marks[1] : marks[2]].reshape(1, inner)
        gin = flat[:, marks[2] : marks[3]].reshape(1, feat)
    hp = jnp.pad(jnp.concatenate([dt_bias, a_log], axis=0), ((0, 6), (0, LANES - heads)))
    sk = jnp.repeat(skip_d, inner // heads, axis=1)
    weights = (wm, wo, gin, cw, cb, gg, hp, sk)

    def choose(one, other):
        return jnp.where(first, one, other)

    up = down = [(0, 1), (1, 0)]
    ids = segments.astype(F32)[:, None, :]
    f0 = forward_layer(0, where, ids, weights, [(inputs, 0)])
    r0 = lax.ppermute(f0[0], "section", up)
    f1 = forward_layer(3, where, ids, weights, [(inputs, 1), (r0, None)])
    r1 = lax.ppermute(f1[0], "section", up)
    f2 = forward_layer(1, where, ids, weights, [(inputs, 1), (r1, None)])

    def stored(tick):
        return [(tick[i], None) for i in (2, 3, 4, 6, 7, 8)]

    kept = stored(f1)
    now = [[(cotangent, 0), (inputs, 1)] + kept, [(cotangent, 0), (r0, None)] + kept]
    b0 = backward_layer(0, where, ids, weights, now)
    d0 = lax.ppermute(b0[1], "section", down)
    now = [
        [(d0, None), (inputs, 0)] + stored(f0),
        [(cotangent, 1), (r1, None)] + stored(f2),
    ]
    b1 = backward_layer(2, where, ids, weights, now)
    d1 = lax.ppermute(b1[1], "section", down)
    if aligned:
        rows_of = (f0[1], f0[5]), (f2[1], f2[5]), (f1[1], behind(f1[5], b1[1]))
        turned = turn(where, *rows_of, rows)
    b2 = backward_layer(1, where, ids, weights, [[(d1, None), (inputs, 1)] + kept])
    dch, din, dgin, dhp = tuple(choose(two, zero) + one for zero, one, two in zip(b0[4:], b1[4:], b2[4:]))
    on_first = (f0[1], f0[5], b1[2], d0, b1[3]), (f1[1], f1[5], b2[2], d1, b2[3])
    on_last = (f2[1], f2[5], b1[2], cotangent[1], b1[3]), (f1[1], f1[5], b0[2], cotangent[0], b0[3])
    if aligned:
        smalls = [part[i] for i in (4, 5, 6, 7) for part in (b0, b1, b2)]
        one, other = (pair[0][2:] + pair[1][2:] for pair in (on_first, on_last))
        first_blocks, vectors, rest = weight_terms(where, turned, one, other, smalls, rows, chans)
    else:
        n, mix, gp, gb, gdt = tuple(
            jnp.concatenate([choose(on_first[0][i], on_last[0][i]), choose(on_first[1][i], on_last[1][i])], axis=0) for i in range(5)
        )
        own = [
            small_rows(
                (
                    dch[:TAPS, i * chans : (i + 1) * chans],
                    dch[TAPS, i * chans : (i + 1) * chans],
                    din[0, i * own_inner : (i + 1) * own_inner],
                    dgin[0, i * rows : (i + 1) * rows],
                ),
                rows,
            )
            for i in range(dp)
        ]
        wide = dot_tn(mix, gb).reshape(dp, blocks, rows, feat).transpose(0, 2, 1, 3).reshape(feat, inner)
        parts = [dot_tn(n, gp), wide, dot_tn(n, gdt), jnp.concatenate(own, axis=0)]
        packed_grad = jnp.concatenate([part.astype(BF16) for part in parts], axis=1)
    if aligned:
        terms, vectors, started = scatter_slots(first_blocks, rest, vectors)
        heads_sum = vectors[:, :heads]
    else:
        summed = lax.psum_scatter(packed_grad, "dp", scatter_dimension=0, tiled=True)
        heads_sum = total_over(dhp[:3, :heads], "dp")
        started = summed
    if aligned:
        g_main, g_out, g_dt, g_cw, g_cb, g_gg, g_ng = unpack_sums(terms, *owned)
        g_dt = jnp.swapaxes(g_dt, 0, 1)
    else:
        summed = summed.astype(F32)
        got = small_flat(summed[:, width + inner + LANES :], 1)[0]
        g_main = summed[:, :width]
        g_out = summed[:, width : width + inner].reshape(rows, blocks, feat).transpose(1, 0, 2).reshape(own_inner, feat)
        g_dt = summed[:, width + inner : width + inner + heads]
        g_cw = got[: marks[0]].reshape(TAPS, chans)
        g_cb, g_gg, g_ng = (got[None, marks[i] : marks[i + 1]] for i in range(3))
    outs = [part[0] for part in (f0, f1, f2, b0, b1, b2)]
    outs = lax.optimization_barrier((*outs, started))
    hidden = jnp.stack([choose(outs[0], outs[1]), choose(outs[1], outs[2])])[None]
    grad_inputs = jnp.stack([choose(outs[4], outs[3]), choose(outs[5], outs[4])])[None]
    return (
        hidden,
        grad_inputs,
        g_ng,
        g_main[None],
        g_dt[None],
        g_cw[None],
        g_cb,
        heads_sum[0:1],
        heads_sum[1:2],
        heads_sum[2:3],
        g_gg,
        g_out[None],
    )


def solution(mesh):
    placed = (
        P(None, "dp", None),
        P(None, "dp"),
        P(None, "dp", None),
        P("section", "dp"),
        P("section", "dp", None),
        P("section", "dp", None),
        P("section", None, "dp"),
        P("section", "dp"),
        P("section", None),
        P("section", None),
        P("section", None),
        P("section", "dp"),
        P("section", "dp", None),
    )
    return jax.shard_map(
        shards,
        mesh=mesh,
        in_specs=placed,
        out_specs=(
            P("section", None, "dp", None),
            P("section", None, "dp", None),
            P("section", "dp"),
            P("section", "dp", None),
            P("section", "dp", None),
            P("section", None, "dp"),
            P("section", "dp"),
            P("section", None),
            P("section", None),
            P("section", None),
            P("section", "dp"),
            P("section", "dp", None),
        ),
        check_vma=False,
    )
```
